256 devices in a mesh: dp: 8 (over z_hi, x), ctx: 32 (over z_lo, y, core).
Axes of the slice: x: 4, y: 4, z: 8 (z_hi: 2, z_lo: 4; z = z_hi * 4 + z_lo), core: 2. Of those that a mesh axis runs over, the one named last changes fastest.
Arguments:
- tokens: bfloat16 [8, 4096, 512], P('dp', 'ctx'), may hold values from -6 to 6
- cotangent: bfloat16 [8, 4096, 512], P('dp', 'ctx'), may hold values from -6 to 6
- decay: float32 [8, 512], replicated, may hold values from 0 to 1, as said below
- residue: float32 [8, 512], replicated, may hold values from -1 to 1
- skip: float32 [512], replicated, may hold values from -3 to 3
Outputs:
- grad_tokens: float32 [8, 4096, 512], P('dp', 'ctx')
- grad_residue: float32 [8, 512], P(None, 'ctx')
- grad_decay: float32 [8, 512], P(None, 'ctx')
- grad_skip: float32 [512], P('ctx')
The draws below stay inside these ranges and needn't reach their ends.
Inputs may be any that keep to these rules, and one draw needn't show every extreme that they name: `decay`: positive.
All inputs are finite; a program needn't handle non-finite values.
Results may differ from the reference program's by a relative error of at most 0.0003.
Values may be sent and summed in bfloat16 or wider, within the bound.
A program may use at most 128 MiB of HBM per device.

```python
import math
import jax
import jax.numpy as jnp
from jax import lax

CHANNELS = 512
MODES = 8
SEQ = 4096
NSEQ = 8
TOKENS = 32768


def decay_rates(key, share):
    key_pick, key_slow, key_fast = jax.random.split(key, 3)
    shape = (MODES, CHANNELS)
    picked = jax.random.uniform(key_pick, shape, jnp.float32)
    slow_rates = jnp.exp(jax.random.uniform(key_slow, shape, jnp.float32, minval=math.log(0.2 / SEQ), maxval=math.log(2.3 / SEQ)))
    fast_rates = jnp.exp(jax.random.uniform(key_fast, shape, jnp.float32, minval=math.log(1.0 / 50.0), maxval=math.log(1.0 / 30.0)))
    return jnp.where(picked < share, slow_rates, fast_rates)


def draw_decay(key, part):
    share = 0.5
    return decay_rates(key, share)


def draw_residue(key, part):
    share = 0.5
    rates = decay_rates(key, share)
    key = jax.random.fold_in(key, 7)
    shape = (MODES, CHANNELS)
    noise = jax.random.truncated_normal(key, -4.0, 4.0, shape, jnp.float32)
    return noise * jnp.sqrt(jnp.maximum(2.0 * rates, 1.0 / SEQ)) / math.sqrt(MODES)


def strengthened(entries, key, source, target, blocks, factor):
    owner, partner = [(jnp.arange(entries.shape[dim]) // (entries.shape[dim] // blocks)).reshape([-1 if axis == dim else 1 for axis in range(entries.ndim)]) for dim in (source, target)]
    chosen = jax.random.permutation(key, blocks)[partner]
    strong = (owner == chosen) | (owner == (partner + blocks // 2) % blocks)
    return jnp.where(strong, factor * entries, entries)


def shard_levels(stream_key, dims, cuts, low, largest):
    def one(dim, parts):
        heights = jax.random.uniform(jax.random.fold_in(jax.random.fold_in(stream_key, 6), dim), (parts,), jnp.float32, low / len(cuts), largest / len(cuts))
        return jnp.repeat(jnp.exp(heights), dims[dim] // parts).reshape((-1,) + (1,) * (len(dims) - dim - 1))

    level = one(*cuts[0])
    for cut in cuts[1:]:
        level = level * one(*cut)
    return level


def scatter_about(rng, dims, deviation, reach, pieces=(), kind=jnp.bfloat16):
    loudness = shard_levels(rng, dims, pieces, -0.22, 0.18) if pieces else 1.0
    drawn = jax.random.normal(rng, dims, jnp.float32) * deviation * loudness
    return jnp.minimum(jnp.maximum(drawn, -reach), reach).astype(kind)


def gaussian_with(own_key, shape, deviation, most, shards, heavy, kind=jnp.bfloat16):
    entries = deviation * jax.random.normal(own_key, shape, jnp.float32)
    if shards:
        entries = entries * shard_levels(own_key, shape, shards, -0.22, 0.18)
    return jnp.clip(strengthened(entries, jax.random.fold_in(own_key, 3), *heavy), -most, most).astype(kind)


def setup_inputs(seed: int = 0) -> dict:
    arg_keys = jax.random.split(jax.random.key(seed), 6)
    return {
        "tokens": scatter_about(arg_keys[0], (NSEQ, SEQ, CHANNELS), 1.0, 6.0, ((0, 8), (1, 32))),
        "cotangent": gaussian_with(arg_keys[1], (NSEQ, SEQ, CHANNELS), 1.0, 6.0, ((0, 8), (1, 32)), (1, 2, 32, 2.75)),
        "decay": draw_decay(jax.random.fold_in(arg_keys[5], 71), 0),
        "residue": draw_residue(jax.random.fold_in(arg_keys[5], 71), 0),
        "skip": scatter_about(arg_keys[4], (CHANNELS,), 0.5, 3.0, (), jnp.float32),
    }


def channel_group(inputs, cotangents, decay, residue, skip):
    factors = jnp.exp(-decay)
    mode_count, group_width = decay.shape

    def forward_step(carry_state, token_now):
        return factors * carry_state + token_now[None, :], carry_state

    zeros_state = jnp.zeros((mode_count, group_width), jnp.float32)
    _, previous = lax.scan(forward_step, zeros_state, inputs)

    def backward_step(carry, sliced):
        carry_state, sum_residue, sum_decay = carry
        grad_now, token_now, state_before = sliced
        carry_state = factors * carry_state + grad_now[None, :]
        state_now = factors * state_before + token_now[None, :]
        sum_residue = sum_residue + grad_now[None, :] * state_now
        sum_decay = sum_decay + carry_state * state_before
        output_row = jnp.sum(residue * carry_state, axis=0) + skip * grad_now
        return (carry_state, sum_residue, sum_decay), output_row

    (_, sum_residue, sum_decay), grads = lax.scan(
        backward_step, (zeros_state, zeros_state, zeros_state), (cotangents, inputs, previous), reverse=True)
    sum_skip = jnp.sum(cotangents * inputs, axis=0)
    return grads, sum_residue, sum_decay, sum_skip


def reference(tokens, cotangent, decay, residue, skip):
    group_width = 64 if CHANNELS % 64 == 0 else CHANNELS
    groups = CHANNELS // group_width
    inputs = tokens.astype(jnp.float32).reshape(NSEQ, SEQ, groups, group_width)
    inputs = inputs.transpose(0, 2, 1, 3).reshape(NSEQ * groups, SEQ, group_width)
    grads_in = cotangent.astype(jnp.float32).reshape(NSEQ, SEQ, groups, group_width)
    grads_in = grads_in.transpose(0, 2, 1, 3).reshape(NSEQ * groups, SEQ, group_width)
    decay_groups = decay.reshape(MODES, groups, group_width).transpose(1, 0, 2)
    residue_groups = residue.reshape(MODES, groups, group_width).transpose(1, 0, 2)
    skip_groups = skip.reshape(groups, group_width)

    def run_one(position):
        member = position % groups
        return channel_group(inputs[position], grads_in[position], decay_groups[member],
                             residue_groups[member], skip_groups[member])

    grads, sum_residue, sum_decay, sum_skip = lax.map(run_one, jnp.arange(NSEQ * groups, dtype=jnp.int32))
    grad_tokens = grads.reshape(NSEQ, groups, SEQ, group_width).transpose(0, 2, 1, 3).reshape(NSEQ, SEQ, CHANNELS)
    sum_residue = sum_residue.reshape(NSEQ, groups, MODES, group_width).sum(axis=0).transpose(1, 0, 2).reshape(MODES, CHANNELS)
    sum_decay = sum_decay.reshape(NSEQ, groups, MODES, group_width).sum(axis=0).transpose(1, 0, 2).reshape(MODES, CHANNELS)
    sum_skip = sum_skip.reshape(NSEQ, groups, group_width).sum(axis=0).reshape(CHANNELS)
    grad_residue = sum_residue / TOKENS
    grad_decay = -jnp.exp(-decay) * residue * sum_decay / TOKENS
    grad_skip = sum_skip / TOKENS
    return grad_tokens, grad_residue, grad_decay, grad_skip
```

```python
import functools

import jax
import jax.numpy as jnp
from jax import lax
from jax.experimental import pallas as pl
from jax.experimental.pallas import tpu as pltpu
from jax.sharding import PartitionSpec as P

MESH = pl.DeviceIdType.MESH
MODES = 8
LANES = 128
GROUP = 16
RUNS = 8
RUN = 16
SIDE = 8


def roll(value, groups):
    return pltpu.roll(value, (groups * GROUP) % LANES, 1)


def lane_group():
    return lax.broadcasted_iota(jnp.int32, (8, LANES), 1) // GROUP


def swap_blocks(blocks):
    group = lane_group()
    blocks = list(blocks)
    for step in (4, 2, 1):
        low = (group // step) % 2 == 0
        for a in range(SIDE):
            if (a // step) % 2 == 0:
                first, second = blocks[a], blocks[a + step]
                blocks[a] = jnp.where(low, first, roll(second, step))
                blocks[a + step] = jnp.where(low, roll(first, -step), second)
    return blocks


def summarise(g, xs, cs, rates, factors, sums, lags, starts, tx):
    lanes = pl.ds(pl.multiple_of(g * LANES, LANES), LANES)
    x = [xs[g, pl.ds(i, RUNS, stride=RUN), :] for i in range(RUN)]
    c = [cs[g, pl.ds(i, RUNS, stride=RUN), :] for i in range(RUN)]
    for mode in range(MODES):
        factor = jnp.broadcast_to(factors[pl.ds(mode, 1), lanes], (RUNS, LANES))
        state, tail = x[0], jnp.zeros((RUNS, LANES), jnp.float32)
        for i in range(1, RUN):
            tail = factor * (tail + state)
            state = factor * state + x[i]
        adjoint, head = c[RUN - 1], jnp.zeros((RUNS, LANES), jnp.float32)
        for i in range(RUN - 2, -1, -1):
            head = factor * (head + adjoint)
            adjoint = factor * adjoint + c[i]
        rows = pl.ds(mode * RUNS, RUNS)
        sums[0, rows, :] = state
        sums[1, rows, :] = tail
        sums[2, rows, :] = adjoint
        sums[3, rows, :] = head + adjoint
    for lag in range(RUN):
        total = c[lag] * x[0]
        for i in range(1, RUN - lag):
            total = total + c[i + lag] * x[i]
        lags[pl.ds(lag, 1), :] = jnp.sum(total, axis=0, keepdims=True)
    rate = rates[:, lanes]
    factor = factors[:, lanes]
    power = jnp.exp(rate * -float(RUN))

    def spread(lag):
        return jnp.broadcast_to(lags[pl.ds(lag, 1), :], (MODES, LANES))

    zeros = jnp.zeros((MODES, LANES), jnp.float32)
    inner, cross = spread(RUN - 1), zeros
    for lag in range(RUN - 2, -1, -1):
        cross = factor * cross + inner
        inner = factor * inner + spread(lag)
    run = [[sums[q, pl.ds(a, MODES, stride=RUNS), :] for q in range(4)] for a in range(RUNS)]
    state, tail, outer = zeros, zeros, zeros
    befores = []
    for a in range(RUNS):
        run_state, run_tail, run_adjoint, run_head = run[a]
        befores.append(state)
        outer = outer + state * run_adjoint
        cross = cross + state * run_head
        tail = run_tail + power * (tail + float(RUN) * state)
        state = run_state + power * state
    adjoint, head = zeros, zeros
    for a in range(RUNS - 1, -1, -1):
        run_state, run_tail, run_adjoint, run_head = run[a]
        starts[g, pl.ds(a * MODES, MODES), :] = adjoint
        cross = cross + adjoint * (run_tail + (float(RUN) * power) * befores[a])
        head = run_head + power * (head + float(RUN) * adjoint)
        adjoint = run_adjoint + power * adjoint
    inner = inner + factor * outer
    tiles = swap_blocks([adjoint, state, head, state, inner, cross, spread(0), tail])
    for i in range(SIDE):
        tx[g * SIDE + i] = tiles[i]


def local_grads(g, cs, factors, residue, skip, starts, grads):
    lanes = pl.ds(pl.multiple_of(g * LANES, LANES), LANES)

    def row(ref, mode):
        return jnp.broadcast_to(ref[pl.ds(mode, 1), lanes], (RUNS, LANES))

    factor = [row(factors, mode) for mode in range(MODES)]
    weight = [row(residue, mode) for mode in range(MODES)]
    direct = row(skip, 0)
    adjoint = [starts[g, pl.ds(mode, RUNS, stride=MODES), :] for mode in range(MODES)]
    for i in range(RUN - 1, -1, -1):
        now = cs[g, pl.ds(i, RUNS, stride=RUN), :]
        total = direct * now
        for mode in range(MODES):
            adjoint[mode] = factor[mode] * adjoint[mode] + now
            total = total + weight[mode] * adjoint[mode]
        grads[g, pl.ds(i, RUNS, stride=RUN), :] = total


def own_lanes(value, place):
    value = jnp.where(lane_group() == place, value, 0.0)
    for step in (1, 2, 4):
        value = value + roll(value, step)
    return value


def owner_sums(place, block, length, positions, rates, residue, rx, zbuf):
    lanes = pl.ds(pl.multiple_of(block * LANES, LANES), LANES)
    rate = own_lanes(rates[:, lanes], place)
    weight = own_lanes(residue[:, lanes], place)
    factor = jnp.exp(-rate)
    power = jnp.exp(rate * -float(length))
    shards = rx.shape[0]
    zeros = jnp.zeros((MODES, LANES), jnp.float32)
    state, plain, by_state, by_adjoint, both = zeros, zeros, zeros, zeros, zeros
    befores = []
    for k in range(shards):
        tile = rx[k]
        befores.append(state)
        plain = plain + tile
        by_state = by_state + state * roll(tile, 1)
        state = power * state + tile
    adjoint = zeros
    for k in range(shards - 1, -1, -1):
        tile = rx[k]
        zbuf[pl.ds(k * MODES, MODES), :] = adjoint
        by_adjoint = by_adjoint + adjoint * roll(tile, 1)
        both = both + befores[k] * roll(adjoint, 1)
        adjoint = power * adjoint + tile
    scale = 1.0 / positions
    sum_residue = roll(plain, -4) + factor * roll(by_state, -1)
    sum_decay = roll(plain, -5) + roll(by_state, -3) + by_adjoint + (float(length) * power) * roll(both, -1)
    sum_skip = roll(plain, -6)
    last = [sum_residue * scale, (-scale) * factor * weight * sum_decay, sum_skip * scale]
    for k in range(SIDE):
        zbuf[pl.ds((shards + k) * MODES, MODES), :] = last[k] if k < len(last) else zeros


def pack_rows(zbuf, a):
    group = lane_group()
    packed = zbuf[pl.ds(a * SIDE * MODES, SIDE, stride=MODES), :]
    for mode in range(1, MODES):
        rows = zbuf[pl.ds(a * SIDE * MODES + mode, SIDE, stride=MODES), :]
        packed = jnp.where(group == mode, roll(rows, mode), packed)
    return packed


def unpack_rows(rows):
    apart = (lane_group() - lax.broadcasted_iota(jnp.int32, (8, LANES), 0) + SIDE) % SIDE
    out = rows
    for step in range(1, SIDE):
        moved = roll(pltpu.roll(rows, SIDE - step, 0), step)
        out = jnp.where(apart == step, moved, out)
    return out


def exchange_kernel(
    shards,
    groups,
    positions,
    tokens,
    cotangent,
    rates_in,
    residue_in,
    skip_in,
    grads,
    carry_out,
    totals_out,
    x_raw,
    c_raw,
    rates,
    residue,
    skip,
    xs,
    cs,
    factors,
    sums,
    lags,
    starts,
    tx,
    rx,
    zbuf,
    ztx,
    zrx,
    ptx,
    prx,
    in_sems,
    ctx_sems,
    back_sems,
    dp_sems,
):
    dp, ctx = lax.axis_index("dp"), lax.axis_index("ctx")
    length, channels = x_raw.shape
    blocks = channels // LANES
    loads = [
        pltpu.make_async_copy(source, target, in_sems.at[n])
        for n, (source, target) in enumerate(
            ((tokens, x_raw), (cotangent, c_raw), (rates_in, rates), (residue_in, residue), (skip_in, skip))
        )
    ]
    for load in loads:
        load.start()
    barrier = pltpu.get_barrier_semaphore()

    @pl.loop(1, shards)
    def _(d):
        pl.semaphore_signal(barrier, inc=1, device_id=(dp, lax.rem(ctx + d, shards)), device_id_type=MESH)

    @pl.loop(1, groups)
    def _(d):
        pl.semaphore_signal(barrier, inc=1, device_id=(lax.rem(dp + d, groups), ctx), device_id_type=MESH)

    for load in loads[2:]:
        load.wait()
    factors[...] = jnp.exp(-rates[...])
    for load, raw, wide in ((loads[0], x_raw, xs), (loads[1], c_raw, cs)):
        load.wait()
        for g in range(blocks):
            wide[g] = raw[:, pl.ds(g * LANES, LANES)].astype(jnp.float32)

    @pl.loop(0, blocks)
    def _(g):
        summarise(g, xs, cs, rates, factors, sums, lags, starts, tx)

    carry_out[pl.ds(MODES, MODES), :] = rates[...]
    rx[ctx] = tx[ctx]
    pl.semaphore_wait(barrier, shards + groups - 2)

    @pl.loop(1, shards)
    def _(d):
        peer = lax.rem(ctx + d, shards)
        pltpu.make_async_remote_copy(
            src_ref=tx.at[peer],
            dst_ref=rx.at[ctx],
            send_sem=ctx_sems.at[0],
            recv_sem=ctx_sems.at[1],
            device_id=(dp, peer),
            device_id_type=MESH,
        ).start()

    @pl.loop(0, blocks)
    def _(g):
        local_grads(g, cs, factors, residue, skip, starts, grads)

    most = pl.ds(0, shards - 1)
    pltpu.make_async_copy(rx.at[most], rx.at[most], ctx_sems.at[1]).wait()
    owner_sums(lax.rem(ctx, SIDE), ctx // SIDE, length, positions, rates, residue, rx, zbuf)
    ptx[...] = pack_rows(zbuf, shards // SIDE)
    prx[dp] = ptx[...]

    @pl.loop(1, groups)
    def _(d):
        pltpu.make_async_remote_copy(
            src_ref=ptx,
            dst_ref=prx.at[dp],
            send_sem=dp_sems.at[0],
            recv_sem=dp_sems.at[1],
            device_id=(lax.rem(dp + d, groups), ctx),
            device_id_type=MESH,
        ).start()

    for a in range(shards // SIDE):
        ztx[pl.ds(a * SIDE, SIDE)] = pack_rows(zbuf, a).reshape(SIDE, 1, LANES)
    zrx[ctx] = ztx[ctx]

    @pl.loop(1, shards)
    def _(d):
        peer = lax.rem(ctx + d, shards)
        pltpu.make_async_remote_copy(
            src_ref=ztx.at[peer],
            dst_ref=zrx.at[ctx],
            send_sem=back_sems.at[0],
            recv_sem=back_sems.at[1],
            device_id=(dp, peer),
            device_id_type=MESH,
        ).start()

    pltpu.make_async_copy(tx.at[most], tx.at[most], ctx_sems.at[0]).wait()
    pltpu.make_async_copy(zrx.at[most], zrx.at[most], back_sems.at[1]).wait()
    for g in range(blocks):
        rows = zrx[pl.ds(g * SIDE, SIDE)].reshape(SIDE, LANES)
        lanes = pl.ds(g * LANES, LANES)
        carry_out[pl.ds(0, MODES), lanes] = residue[:, lanes] * unpack_rows(rows)
    pltpu.make_async_copy(ztx.at[most], ztx.at[most], back_sems.at[0]).wait()
    others = pl.ds(0, groups - 1)
    pltpu.make_async_copy(prx.at[others], prx.at[others], dp_sems.at[1]).wait()
    total = prx[0]
    for n in range(1, groups):
        total = total + prx[n]
    totals_out[...] = total
    pltpu.make_async_copy(prx.at[others], prx.at[others], dp_sems.at[0]).wait()


def finish_kernel(grads, carry, totals, out, out_residue, out_decay, out_skip):
    blocks, length, _ = grads.shape
    ahead = (SIDE - lax.broadcasted_iota(jnp.int32, (8, LANES), 0)).astype(jnp.float32)
    for g in range(blocks):
        lanes = pl.ds(g * LANES, LANES)
        rate = [jnp.broadcast_to(carry[pl.ds(MODES + m, 1), lanes], (8, LANES)) for m in range(MODES)]
        power = [jnp.exp(rate[m] * -8.0) for m in range(MODES)]
        term = [
            jnp.exp(-rate[m] * ahead) * jnp.broadcast_to(carry[pl.ds(m, 1), lanes], (8, LANES))
            for m in range(MODES)
        ]
        for b in range(length // 8 - 1, -1, -1):
            rows = pl.ds(b * 8, 8)
            total = grads[g, rows, :]
            for m in range(MODES):
                total = total + term[m]
                if b:
                    term[m] = power[m] * term[m]
            out[rows, lanes] = total
    sublane = lax.broadcasted_iota(jnp.int32, (8, LANES), 0)
    for row, ref in ((0, out_residue), (1, out_decay)):
        spread = jnp.broadcast_to(totals[pl.ds(row, 1), :], (8, LANES))
        value = spread
        for m in range(1, MODES):
            value = jnp.where(sublane == m, roll(spread, -m), value)
        ref[...] = value[:, :GROUP]
    out_skip[...] = totals[2, :GROUP]


def body(shards, groups, tokens, cotangent, decay, residue, skip):
    _, length, channels = tokens.shape
    positions = float(length * shards * groups)
    blocks = channels // LANES
    vmem = pl.BlockSpec(memory_space=pltpu.VMEM)
    hbm = pl.BlockSpec(memory_space=pltpu.HBM)
    f32 = jnp.float32
    grads, carry, totals = pl.pallas_call(
        functools.partial(exchange_kernel, shards, groups, positions),
        out_shape=[
            jax.ShapeDtypeStruct((blocks, length, LANES), f32),
            jax.ShapeDtypeStruct((2 * MODES, channels), f32),
            jax.ShapeDtypeStruct((8, LANES), f32),
        ],
        in_specs=[hbm] * 5,
        out_specs=[vmem] * 3,
        scratch_shapes=[
            pltpu.VMEM((length, channels), jnp.bfloat16),
            pltpu.VMEM((length, channels), jnp.bfloat16),
            pltpu.VMEM((MODES, channels), f32),
            pltpu.VMEM((MODES, channels), f32),
            pltpu.VMEM((1, channels), f32),
            pltpu.VMEM((blocks, length, LANES), f32),
            pltpu.VMEM((blocks, length, LANES), f32),
            pltpu.VMEM((MODES, channels), f32),
            pltpu.VMEM((4, MODES * RUNS, LANES), f32),
            pltpu.VMEM((RUN, LANES), f32),
            pltpu.VMEM((blocks, RUNS * MODES, LANES), f32),
            pltpu.VMEM((shards, 8, LANES), f32),
            pltpu.VMEM((shards, 8, LANES), f32),
            pltpu.VMEM(((shards + SIDE) * MODES, LANES), f32),
            pltpu.VMEM((shards, 1, LANES), f32),
            pltpu.VMEM((shards, 1, LANES), f32),
            pltpu.VMEM((8, LANES), f32),
            pltpu.VMEM((groups, 8, LANES), f32),
            pltpu.SemaphoreType.DMA((5,)),
            pltpu.SemaphoreType.DMA((2,)),
            pltpu.SemaphoreType.DMA((2,)),
            pltpu.SemaphoreType.DMA((2,)),
        ],
        compiler_params=pltpu.CompilerParams(
            collective_id=1, has_side_effects=True, vmem_limit_bytes=32 * 1024 * 1024
        ),
        name="exchange",
    )(tokens[0], cotangent[0], decay, residue, skip.reshape(1, channels))
    out, grad_residue, grad_decay, grad_skip = pl.pallas_call(
        finish_kernel,
        out_shape=[
            jax.ShapeDtypeStruct((length, channels), f32),
            jax.ShapeDtypeStruct((MODES, GROUP), f32),
            jax.ShapeDtypeStruct((MODES, GROUP), f32),
            jax.ShapeDtypeStruct((GROUP,), f32),
        ],
        in_specs=[vmem] * 3,
        out_specs=[vmem] * 4,
        compiler_params=pltpu.CompilerParams(vmem_limit_bytes=32 * 1024 * 1024),
        name="finish",
    )(grads, carry, totals)
    return out[None], grad_residue, grad_decay, grad_skip


def solution(mesh):
    return jax.shard_map(
        functools.partial(body, mesh.shape["ctx"], mesh.shape["dp"]),
        mesh=mesh,
        in_specs=(P("dp", "ctx", None), P("dp", "ctx", None), P(), P(), P()),
        out_specs=(P("dp", "ctx", None), P(None, "ctx"), P(None, "ctx"), P("ctx")),
        check_vma=False,
    )
```

```python
import functools

import jax
import jax.numpy as jnp
from jax import lax
from jax.experimental import pallas as pl
from jax.experimental.pallas import tpu as pltpu
from jax.sharding import PartitionSpec as P

MESH = pl.DeviceIdType.MESH
MODES = 8
LANES = 128
GROUP = 16
RUNS = 8
RUN = 16
SIDE = 8


def roll(value, groups):
    return pltpu.roll(value, (groups * GROUP) % LANES, 1)


def lane_group():
    return lax.broadcasted_iota(jnp.int32, (8, LANES), 1) // GROUP


def swap_blocks(blocks):
    group = lane_group()
    blocks = list(blocks)
    for step in (4, 2, 1):
        low = (group // step) % 2 == 0
        for a in range(SIDE):
            if (a // step) % 2 == 0:
                first, second = blocks[a], blocks[a + step]
                blocks[a] = jnp.where(low, first, roll(second, step))
                blocks[a + step] = jnp.where(low, roll(first, -step), second)
    return blocks


def summarise(g, xs, cs, rates, factors, sums, lags, starts, tx):
    lanes = pl.ds(pl.multiple_of(g * LANES, LANES), LANES)
    x = [xs[g, pl.ds(i, RUNS, stride=RUN), :] for i in range(RUN)]
    c = [cs[g, pl.ds(i, RUNS, stride=RUN), :] for i in range(RUN)]
    for mode in range(MODES):
        factor = jnp.broadcast_to(factors[pl.ds(mode, 1), lanes], (RUNS, LANES))
        state, tail = x[0], jnp.zeros((RUNS, LANES), jnp.float32)
        for i in range(1, RUN):
            tail = factor * (tail + state)
            state = factor * state + x[i]
        adjoint, head = c[RUN - 1], jnp.zeros((RUNS, LANES), jnp.float32)
        for i in range(RUN - 2, -1, -1):
            head = factor * (head + adjoint)
            adjoint = factor * adjoint + c[i]
        rows = pl.ds(mode * RUNS, RUNS)
        sums[0, rows, :] = state
        sums[1, rows, :] = tail
        sums[2, rows, :] = adjoint
        sums[3, rows, :] = head + adjoint
    for lag in range(RUN):
        total = c[lag] * x[0]
        for i in range(1, RUN - lag):
            total = total + c[i + lag] * x[i]
        lags[pl.ds(lag, 1), :] = jnp.sum(total, axis=0, keepdims=True)
    rate = rates[:, lanes]
    factor = factors[:, lanes]
    power = jnp.exp(rate * -float(RUN))

    def spread(lag):
        return jnp.broadcast_to(lags[pl.ds(lag, 1), :], (MODES, LANES))

    zeros = jnp.zeros((MODES, LANES), jnp.float32)
    inner, cross = spread(RUN - 1), zeros
    for lag in range(RUN - 2, -1, -1):
        cross = factor * cross + inner
        inner = factor * inner + spread(lag)
    run = [[sums[q, pl.ds(a, MODES, stride=RUNS), :] for q in range(4)] for a in range(RUNS)]
    state, tail, outer = zeros, zeros, zeros
    befores = []
    for a in range(RUNS):
        run_state, run_tail, run_adjoint, run_head = run[a]
        befores.append(state)
        outer = outer + state * run_adjoint
        cross = cross + state * run_head
        tail = run_tail + power * (tail + float(RUN) * state)
        state = run_state + power * state
    adjoint, head = zeros, zeros
    for a in range(RUNS - 1, -1, -1):
        run_state, run_tail, run_adjoint, run_head = run[a]
        starts[g, pl.ds(a * MODES, MODES), :] = adjoint
        cross = cross + adjoint * (run_tail + (float(RUN) * power) * befores[a])
        head = run_head + power * (head + float(RUN) * adjoint)
        adjoint = run_adjoint + power * adjoint
    inner = inner + factor * outer
    tiles = swap_blocks([adjoint, state, head, state, inner, cross, spread(0), tail])
    for i in range(SIDE):
        tx[g * SIDE + i] = tiles[i]


def local_grads(g, cs, factors, residue, skip, starts, grads):
    lanes = pl.ds(pl.multiple_of(g * LANES, LANES), LANES)

    def row(ref, mode):
        return jnp.broadcast_to(ref[pl.ds(mode, 1), lanes], (RUNS, LANES))

    factor = [row(factors, mode) for mode in range(MODES)]
    weight = [row(residue, mode) for mode in range(MODES)]
    direct = row(skip, 0)
    adjoint = [starts[g, pl.ds(mode, RUNS, stride=MODES), :] for mode in range(MODES)]
    for i in range(RUN - 1, -1, -1):
        now = cs[g, pl.ds(i, RUNS, stride=RUN), :]
        total = direct * now
        for mode in range(MODES):
            adjoint[mode] = factor[mode] * adjoint[mode] + now
            total = total + weight[mode] * adjoint[mode]
        grads[g, pl.ds(i, RUNS, stride=RUN), :] = total


def own_lanes(value, place):
    value = jnp.where(lane_group() == place, value, 0.0)
    for step in (1, 2, 4):
        value = value + roll(value, step)
    return value


def owner_sums(place, block, length, positions, rates, residue, rx, zbuf):
    lanes = pl.ds(pl.multiple_of(block * LANES, LANES), LANES)
    rate = own_lanes(rates[:, lanes], place)
    weight = own_lanes(residue[:, lanes], place)
    factor = jnp.exp(-rate)
    power = jnp.exp(rate * -float(length))
    shards = rx.shape[0]
    zeros = jnp.zeros((MODES, LANES), jnp.float32)
    state, plain, by_state, by_adjoint, both = zeros, zeros, zeros, zeros, zeros
    befores = []
    for k in range(shards):
        tile = rx[k]
        befores.append(state)
        plain = plain + tile
        by_state = by_state + state * roll(tile, 1)
        state = power * state + tile
    adjoint = zeros
    for k in range(shards - 1, -1, -1):
        tile = rx[k]
        zbuf[pl.ds(k * MODES, MODES), :] = adjoint
        by_adjoint = by_adjoint + adjoint * roll(tile, 1)
        both = both + befores[k] * roll(adjoint, 1)
        adjoint = power * adjoint + tile
    scale = 1.0 / positions
    sum_residue = roll(plain, -4) + factor * roll(by_state, -1)
    sum_decay = roll(plain, -5) + roll(by_state, -3) + by_adjoint + (float(length) * power) * roll(both, -1)
    sum_skip = roll(plain, -6)
    last = [sum_residue * scale, (-scale) * factor * weight * sum_decay, sum_skip * scale]
    for k in range(SIDE):
        zbuf[pl.ds((shards + k) * MODES, MODES), :] = last[k] if k < len(last) else zeros


def pack_rows(zbuf, a):
    group = lane_group()
    packed = zbuf[pl.ds(a * SIDE * MODES, SIDE, stride=MODES), :]
    for mode in range(1, MODES):
        rows = zbuf[pl.ds(a * SIDE * MODES + mode, SIDE, stride=MODES), :]
        packed = jnp.where(group == mode, roll(rows, mode), packed)
    return packed


def unpack_rows(rows):
    apart = (lane_group() - lax.broadcasted_iota(jnp.int32, (8, LANES), 0) + SIDE) % SIDE
    out = rows
    for step in range(1, SIDE):
        moved = roll(pltpu.roll(rows, SIDE - step, 0), step)
        out = jnp.where(apart == step, moved, out)
    return out


def exchange_kernel(
    shards,
    groups,
    positions,
    tokens,
    cotangent,
    rates_in,
    residue_in,
    skip_in,
    grads_out,
    carry_out,
    totals_out,
    x_raw,
    c_raw,
    rates,
    residue,
    skip,
    xs,
    cs,
    factors,
    sums,
    lags,
    starts,
    tx,
    rx,
    zbuf,
    ztx,
    zrx,
    ptx,
    prx,
    grads,
    carry,
    totals,
    in_sems,
    out_sems,
    ctx_sems,
    back_sems,
    dp_sems,
):
    dp, ctx = lax.axis_index("dp"), lax.axis_index("ctx")
    length, channels = x_raw.shape
    blocks = channels // LANES
    loads = [
        pltpu.make_async_copy(source, target, in_sems.at[n])
        for n, (source, target) in enumerate(
            ((tokens, x_raw), (cotangent, c_raw), (rates_in, rates), (residue_in, residue), (skip_in, skip))
        )
    ]
    barrier = pltpu.get_barrier_semaphore()

    @pl.loop(1, shards)
    def _(d):
        pl.semaphore_signal(barrier, inc=1, device_id=(dp, lax.rem(ctx + d, shards)), device_id_type=MESH)

    @pl.loop(1, groups)
    def _(d):
        pl.semaphore_signal(barrier, inc=1, device_id=(lax.rem(dp + d, groups), ctx), device_id_type=MESH)

    for load in loads:
        load.start()
    for load in loads[2:]:
        load.wait()
    factors[...] = jnp.exp(-rates[...])
    for load, raw, wide in ((loads[0], x_raw, xs), (loads[1], c_raw, cs)):
        load.wait()
        for g in range(blocks):
            wide[g] = raw[:, pl.ds(g * LANES, LANES)].astype(jnp.float32)

    @pl.loop(0, blocks)
    def _(g):
        summarise(g, xs, cs, rates, factors, sums, lags, starts, tx)

    carry[pl.ds(MODES, MODES), :] = rates[...]
    rx[ctx] = tx[ctx]
    pl.semaphore_wait(barrier, shards + groups - 2)

    @pl.loop(1, shards)
    def _(d):
        peer = lax.rem(ctx + d, shards)
        pltpu.make_async_remote_copy(
            src_ref=tx.at[peer],
            dst_ref=rx.at[ctx],
            send_sem=ctx_sems.at[0],
            recv_sem=ctx_sems.at[1],
            device_id=(dp, peer),
            device_id_type=MESH,
        ).start()

    @pl.loop(0, blocks)
    def _(g):
        local_grads(g, cs, factors, residue, skip, starts, grads)

    stores = [
        pltpu.make_async_copy(source, target, out_sems.at[n])
        for n, (source, target) in enumerate(((grads, grads_out), (carry, carry_out), (totals, totals_out)))
    ]
    stores[0].start()
    most = pl.ds(0, shards - 1)
    pltpu.make_async_copy(rx.at[most], rx.at[most], ctx_sems.at[1]).wait()
    owner_sums(lax.rem(ctx, SIDE), ctx // SIDE, length, positions, rates, residue, rx, zbuf)
    ptx[...] = pack_rows(zbuf, shards // SIDE)
    prx[dp] = ptx[...]

    @pl.loop(1, groups)
    def _(d):
        pltpu.make_async_remote_copy(
            src_ref=ptx,
            dst_ref=prx.at[dp],
            send_sem=dp_sems.at[0],
            recv_sem=dp_sems.at[1],
            device_id=(lax.rem(dp + d, groups), ctx),
            device_id_type=MESH,
        ).start()

    for a in range(shards // SIDE):
        ztx[pl.ds(a * SIDE, SIDE)] = pack_rows(zbuf, a).reshape(SIDE, 1, LANES)
    zrx[ctx] = ztx[ctx]

    @pl.loop(1, shards)
    def _(d):
        peer = lax.rem(ctx + d, shards)
        pltpu.make_async_remote_copy(
            src_ref=ztx.at[peer],
            dst_ref=zrx.at[ctx],
            send_sem=back_sems.at[0],
            recv_sem=back_sems.at[1],
            device_id=(dp, peer),
            device_id_type=MESH,
        ).start()

    pltpu.make_async_copy(tx.at[most], tx.at[most], ctx_sems.at[0]).wait()
    pltpu.make_async_copy(zrx.at[most], zrx.at[most], back_sems.at[1]).wait()
    for g in range(blocks):
        rows = zrx[pl.ds(g * SIDE, SIDE)].reshape(SIDE, LANES)
        lanes = pl.ds(g * LANES, LANES)
        carry[pl.ds(0, MODES), lanes] = residue[:, lanes] * unpack_rows(rows)
    stores[1].start()
    pltpu.make_async_copy(ztx.at[most], ztx.at[most], back_sems.at[0]).wait()
    others = pl.ds(0, groups - 1)
    pltpu.make_async_copy(prx.at[others], prx.at[others], dp_sems.at[1]).wait()
    total = prx[0]
    for n in range(1, groups):
        total = total + prx[n]
    totals[...] = total
    stores[2].start()
    pltpu.make_async_copy(prx.at[others], prx.at[others], dp_sems.at[0]).wait()
    for store in stores:
        store.wait()


def finish_kernel(grads, carry, totals, out, out_residue, out_decay, out_skip):
    blocks, length, _ = grads.shape
    ahead = (SIDE - lax.broadcasted_iota(jnp.int32, (8, LANES), 0)).astype(jnp.float32)
    for g in range(blocks):
        lanes = pl.ds(g * LANES, LANES)
        rate = [jnp.broadcast_to(carry[pl.ds(MODES + m, 1), lanes], (8, LANES)) for m in range(MODES)]
        power = [jnp.exp(rate[m] * -8.0) for m in range(MODES)]
        term = [
            jnp.exp(-rate[m] * ahead) * jnp.broadcast_to(carry[pl.ds(m, 1), lanes], (8, LANES))
            for m in range(MODES)
        ]
        for b in range(length // 8 - 1, -1, -1):
            rows = pl.ds(b * 8, 8)
            total = grads[g, rows, :]
            for m in range(MODES):
                total = total + term[m]
                if b:
                    term[m] = power[m] * term[m]
            out[rows, lanes] = total
    sublane = lax.broadcasted_iota(jnp.int32, (8, LANES), 0)
    for row, ref in ((0, out_residue), (1, out_decay)):
        spread = jnp.broadcast_to(totals[pl.ds(row, 1), :], (8, LANES))
        value = spread
        for m in range(1, MODES):
            value = jnp.where(sublane == m, roll(spread, -m), value)
        ref[...] = value[:, :GROUP]
    out_skip[...] = totals[2, :GROUP]


def body(shards, groups, tokens, cotangent, decay, residue, skip):
    _, length, channels = tokens.shape
    positions = float(length * shards * groups)
    blocks = channels // LANES
    vmem = pl.BlockSpec(memory_space=pltpu.VMEM)
    hbm = pl.BlockSpec(memory_space=pltpu.HBM)
    f32 = jnp.float32
    grads, carry, totals = pl.pallas_call(
        functools.partial(exchange_kernel, shards, groups, positions),
        out_shape=[
            jax.ShapeDtypeStruct((blocks, length, LANES), f32),
            jax.ShapeDtypeStruct((2 * MODES, channels), f32),
            jax.ShapeDtypeStruct((8, LANES), f32),
        ],
        in_specs=[hbm] * 5,
        out_specs=[hbm] * 3,
        scratch_shapes=[
            pltpu.VMEM((length, channels), jnp.bfloat16),
            pltpu.VMEM((length, channels), jnp.bfloat16),
            pltpu.VMEM((MODES, channels), f32),
            pltpu.VMEM((MODES, channels), f32),
            pltpu.VMEM((1, channels), f32),
            pltpu.VMEM((blocks, length, LANES), f32),
            pltpu.VMEM((blocks, length, LANES), f32),
            pltpu.VMEM((MODES, channels), f32),
            pltpu.VMEM((4, MODES * RUNS, LANES), f32),
            pltpu.VMEM((RUN, LANES), f32),
            pltpu.VMEM((blocks, RUNS * MODES, LANES), f32),
            pltpu.VMEM((shards, 8, LANES), f32),
            pltpu.VMEM((shards, 8, LANES), f32),
            pltpu.VMEM(((shards + SIDE) * MODES, LANES), f32),
            pltpu.VMEM((shards, 1, LANES), f32),
            pltpu.VMEM((shards, 1, LANES), f32),
            pltpu.VMEM((8, LANES), f32),
            pltpu.VMEM((groups, 8, LANES), f32),
            pltpu.VMEM((blocks, length, LANES), f32),
            pltpu.VMEM((2 * MODES, channels), f32),
            pltpu.VMEM((8, LANES), f32),
            pltpu.SemaphoreType.DMA((5,)),
            pltpu.SemaphoreType.DMA((3,)),
            pltpu.SemaphoreType.DMA((2,)),
            pltpu.SemaphoreType.DMA((2,)),
            pltpu.SemaphoreType.DMA((2,)),
        ],
        compiler_params=pltpu.CompilerParams(
            collective_id=1, has_side_effects=True, vmem_limit_bytes=60 * 1024 * 1024
        ),
        name="exchange",
    )(tokens[0], cotangent[0], decay, residue, skip.reshape(1, channels))
    out, grad_residue, grad_decay, grad_skip = pl.pallas_call(
        finish_kernel,
        out_shape=[
            jax.ShapeDtypeStruct((length, channels), f32),
            jax.ShapeDtypeStruct((MODES, GROUP), f32),
            jax.ShapeDtypeStruct((MODES, GROUP), f32),
            jax.ShapeDtypeStruct((GROUP,), f32),
        ],
        in_specs=[vmem] * 3,
        out_specs=[vmem] * 4,
        compiler_params=pltpu.CompilerParams(vmem_limit_bytes=60 * 1024 * 1024),
        name="finish",
    )(grads, carry, totals)
    return out[None], grad_residue, grad_decay, grad_skip


def solution(mesh):
    return jax.shard_map(
        functools.partial(body, mesh.shape["ctx"], mesh.shape["dp"]),
        mesh=mesh,
        in_specs=(P("dp", "ctx", None), P("dp", "ctx", None), P(), P(), P()),
        out_specs=(P("dp", "ctx", None), P(None, "ctx"), P(None, "ctx"), P("ctx")),
        check_vma=False,
    )
```

```python
import functools

import jax
import jax.numpy as jnp
from jax import lax
from jax.experimental import pallas as pl
from jax.experimental.pallas import tpu as pltpu
from jax.sharding import PartitionSpec as P

MESH = pl.DeviceIdType.MESH
MODES = 8
LANES = 128
GROUP = 16
RUNS = 8
RUN = 16
SIDE = 8
PLANE = 8


def roll(value, groups):
    return pltpu.roll(value, (groups * GROUP) % LANES, 1)


def lane_group():
    return lax.broadcasted_iota(jnp.int32, (8, LANES), 1) // GROUP


def swap_blocks(blocks):
    group = lane_group()
    blocks = list(blocks)
    for step in (4, 2, 1):
        low = (group // step) % 2 == 0
        for a in range(SIDE):
            if (a // step) % 2 == 0:
                first, second = blocks[a], blocks[a + step]
                blocks[a] = jnp.where(low, first, roll(second, step))
                blocks[a + step] = jnp.where(low, roll(first, -step), second)
    return blocks


def summarise(g, xs, cs, rates, factors, sums, lags, starts, tx):
    lanes = pl.ds(pl.multiple_of(g * LANES, LANES), LANES)
    x = [xs[g, pl.ds(i, RUNS, stride=RUN), :] for i in range(RUN)]
    c = [cs[g, pl.ds(i, RUNS, stride=RUN), :] for i in range(RUN)]
    for mode in range(MODES):
        factor = jnp.broadcast_to(factors[pl.ds(mode, 1), lanes], (RUNS, LANES))
        state, tail = x[0], jnp.zeros((RUNS, LANES), jnp.float32)
        for i in range(1, RUN):
            tail = factor * (tail + state)
            state = factor * state + x[i]
        adjoint, head = c[RUN - 1], jnp.zeros((RUNS, LANES), jnp.float32)
        for i in range(RUN - 2, -1, -1):
            head = factor * (head + adjoint)
            adjoint = factor * adjoint + c[i]
        rows = pl.ds(mode * RUNS, RUNS)
        sums[0, rows, :] = state
        sums[1, rows, :] = tail
        sums[2, rows, :] = adjoint
        sums[3, rows, :] = head + adjoint
    for lag in range(RUN):
        total = c[lag] * x[0]
        for i in range(1, RUN - lag):
            total = total + c[i + lag] * x[i]
        lags[pl.ds(lag, 1), :] = jnp.sum(total, axis=0, keepdims=True)
    rate = rates[:, lanes]
    factor = factors[:, lanes]
    power = jnp.exp(rate * -float(RUN))

    def spread(lag):
        return jnp.broadcast_to(lags[pl.ds(lag, 1), :], (MODES, LANES))

    zeros = jnp.zeros((MODES, LANES), jnp.float32)
    inner, cross = spread(RUN - 1), zeros
    for lag in range(RUN - 2, -1, -1):
        cross = factor * cross + inner
        inner = factor * inner + spread(lag)
    run = [[sums[q, pl.ds(a, MODES, stride=RUNS), :] for q in range(4)] for a in range(RUNS)]
    state, tail, outer = zeros, zeros, zeros
    befores = []
    for a in range(RUNS):
        run_state, run_tail, run_adjoint, run_head = run[a]
        befores.append(state)
        outer = outer + state * run_adjoint
        cross = cross + state * run_head
        tail = run_tail + power * (tail + float(RUN) * state)
        state = run_state + power * state
    adjoint, head = zeros, zeros
    for a in range(RUNS - 1, -1, -1):
        run_state, run_tail, run_adjoint, run_head = run[a]
        starts[g, pl.ds(a * MODES, MODES), :] = adjoint
        cross = cross + adjoint * (run_tail + (float(RUN) * power) * befores[a])
        head = run_head + power * (head + float(RUN) * adjoint)
        adjoint = run_adjoint + power * adjoint
    inner = inner + factor * outer
    tiles = swap_blocks([adjoint, state, head, state, inner, cross, spread(0), tail])
    for i in range(SIDE):
        tx[g * SIDE + i] = tiles[i]


def local_grads(g, cs, factors, residue, skip, starts, grads):
    lanes = pl.ds(pl.multiple_of(g * LANES, LANES), LANES)

    def row(ref, mode):
        return jnp.broadcast_to(ref[pl.ds(mode, 1), lanes], (RUNS, LANES))

    factor = [row(factors, mode) for mode in range(MODES)]
    weight = [row(residue, mode) for mode in range(MODES)]
    direct = row(skip, 0)
    adjoint = [starts[g, pl.ds(mode, RUNS, stride=MODES), :] for mode in range(MODES)]
    for i in range(RUN - 1, -1, -1):
        now = cs[g, pl.ds(i, RUNS, stride=RUN), :]
        total = direct * now
        for mode in range(MODES):
            adjoint[mode] = factor[mode] * adjoint[mode] + now
            total = total + weight[mode] * adjoint[mode]
        grads[g, pl.ds(i, RUNS, stride=RUN), :] = total


def own_lanes(value, place):
    value = jnp.where(lane_group() == place, value, 0.0)
    for step in (1, 2, 4):
        value = value + roll(value, step)
    return value


def owner_sums(place, block, length, positions, rates, residue, rx, zbuf):
    lanes = pl.ds(pl.multiple_of(block * LANES, LANES), LANES)
    rate = own_lanes(rates[:, lanes], place)
    weight = own_lanes(residue[:, lanes], place)
    factor = jnp.exp(-rate)
    power = jnp.exp(rate * -float(length))
    shards = rx.shape[0]
    zeros = jnp.zeros((MODES, LANES), jnp.float32)
    state, plain, by_state, by_adjoint, both = zeros, zeros, zeros, zeros, zeros
    befores = []
    for k in range(shards):
        tile = rx[k]
        befores.append(state)
        plain = plain + tile
        by_state = by_state + state * roll(tile, 1)
        state = power * state + tile
    adjoint = zeros
    for k in range(shards - 1, -1, -1):
        tile = rx[k]
        zbuf[pl.ds(k * MODES, MODES), :] = adjoint
        by_adjoint = by_adjoint + adjoint * roll(tile, 1)
        both = both + befores[k] * roll(adjoint, 1)
        adjoint = power * adjoint + tile
    scale = 1.0 / positions
    sum_residue = roll(plain, -4) + factor * roll(by_state, -1)
    sum_decay = roll(plain, -5) + roll(by_state, -3) + by_adjoint + (float(length) * power) * roll(both, -1)
    sum_skip = roll(plain, -6)
    last = [sum_residue * scale, (-scale) * factor * weight * sum_decay, sum_skip * scale]
    for k in range(SIDE):
        zbuf[pl.ds((shards + k) * MODES, MODES), :] = last[k] if k < len(last) else zeros


def pack_rows(zbuf, a):
    group = lane_group()
    packed = zbuf[pl.ds(a * SIDE * MODES, SIDE, stride=MODES), :]
    for mode in range(1, MODES):
        rows = zbuf[pl.ds(a * SIDE * MODES + mode, SIDE, stride=MODES), :]
        packed = jnp.where(group == mode, roll(rows, mode), packed)
    return packed


def unpack_rows(rows):
    apart = (lane_group() - lax.broadcasted_iota(jnp.int32, (8, LANES), 0) + SIDE) % SIDE
    out = rows
    for step in range(1, SIDE):
        moved = roll(pltpu.roll(rows, SIDE - step, 0), step)
        out = jnp.where(apart == step, moved, out)
    return out


def exchange_kernel(
    shards,
    groups,
    positions,
    tokens,
    cotangent,
    rates_in,
    residue_in,
    skip_in,
    grads_out,
    carry_out,
    totals_out,
    x_raw,
    c_raw,
    rates,
    residue,
    skip,
    xs,
    cs,
    factors,
    sums,
    lags,
    starts,
    tx,
    rx,
    zbuf,
    ztx,
    zrx,
    ptx,
    prx,
    grads,
    carry,
    totals,
    in_sems,
    out_sems,
    ctx_sems,
    back_sems,
    dp_sems,
    ready_sem,
):
    dp, ctx = lax.axis_index("dp"), lax.axis_index("ctx")
    length, channels = x_raw.shape
    blocks = channels // LANES
    loads = [
        pltpu.make_async_copy(source, target, in_sems.at[n])
        for n, (source, target) in enumerate(
            ((tokens, x_raw), (cotangent, c_raw), (rates_in, rates), (residue_in, residue), (skip_in, skip))
        )
    ]
    half = groups // 2
    late = dp // half
    place_x = lax.rem(dp, half)
    mirror = (shards // PLANE - 1 - ctx // PLANE) * PLANE + lax.rem(ctx, PLANE)
    owned = ctx + late * (mirror - ctx)

    def same_half(d):
        return late * half + lax.rem(place_x + d, half)

    def other_half(d):
        return (1 - late) * half + d

    barrier = pltpu.get_barrier_semaphore()

    def greet(group, peer):
        pl.semaphore_signal(barrier, inc=1, device_id=(group, peer), device_id_type=MESH)

    @pl.loop(1, shards)
    def _(d):
        greet(dp, lax.rem(ctx + d, shards))

    @pl.loop(1, half)
    def _(d):
        greet(same_half(d), owned)

    @pl.when(late == 0)
    def _():
        @pl.loop(0, half)
        def _(d):
            greet(other_half(d), mirror)
            greet(other_half(d), ctx)

    for load in loads:
        load.start()
    for load in loads[2:]:
        load.wait()
    factors[...] = jnp.exp(-rates[...])
    for load, raw, wide in ((loads[0], x_raw, xs), (loads[1], c_raw, cs)):
        load.wait()
        for g in range(blocks):
            wide[g] = raw[:, pl.ds(g * LANES, LANES)].astype(jnp.float32)

    @pl.loop(0, blocks)
    def _(g):
        summarise(g, xs, cs, rates, factors, sums, lags, starts, tx)

    carry[pl.ds(MODES, MODES), :] = rates[...]
    rx[ctx] = tx[owned]
    pl.semaphore_wait(barrier, shards - 1 + half - 1 + late * 2 * half)

    @pl.when(late == 1)
    def _():
        @pl.loop(0, half)
        def _(d):
            pl.semaphore_signal(ready_sem, inc=1, device_id=(other_half(d), ctx), device_id_type=MESH)

    @pl.loop(1, shards)
    def _(d):
        peer = lax.rem(ctx + d, shards)
        across = (shards // PLANE - 1 - peer // PLANE) * PLANE + lax.rem(peer, PLANE)
        pltpu.make_async_remote_copy(
            src_ref=tx.at[peer + late * (across - peer)],
            dst_ref=rx.at[ctx],
            send_sem=ctx_sems.at[0],
            recv_sem=ctx_sems.at[1],
            device_id=(dp, peer),
            device_id_type=MESH,
        ).start()

    @pl.loop(0, blocks)
    def _(g):
        local_grads(g, cs, factors, residue, skip, starts, grads)

    stores = [
        pltpu.make_async_copy(source, target, out_sems.at[n])
        for n, (source, target) in enumerate(((grads, grads_out), (carry, carry_out), (totals, totals_out)))
    ]
    stores[0].start()
    most = pl.ds(0, shards - 1)
    pltpu.make_async_copy(rx.at[most], rx.at[most], ctx_sems.at[1]).wait()
    owner_sums(lax.rem(owned, SIDE), owned // SIDE, length, positions, rates, residue, rx, zbuf)
    ptx[...] = pack_rows(zbuf, shards // SIDE)

    def send_totals(group):
        pltpu.make_async_remote_copy(
            src_ref=ptx,
            dst_ref=prx.at[dp],
            send_sem=dp_sems.at[0],
            recv_sem=dp_sems.at[1],
            device_id=(group, owned),
            device_id_type=MESH,
        ).start()

    @pl.when(late == 1)
    def _():
        @pl.loop(0, half)
        def _(d):
            send_totals(other_half(d))

        send_totals(dp)

    @pl.loop(1, half)
    def _(d):
        send_totals(same_half(d))

    @pl.when(late == 0)
    def _():
        prx[dp] = ptx[...]
        pl.semaphore_wait(ready_sem, half)

        @pl.loop(0, half)
        def _(d):
            send_totals(other_half(d))

    for a in range(shards // SIDE):
        ztx[pl.ds(a * SIDE, SIDE)] = pack_rows(zbuf, a).reshape(SIDE, 1, LANES)
    zrx[owned] = ztx[ctx]

    @pl.loop(1, shards)
    def _(d):
        peer = lax.rem(ctx + d, shards)
        pltpu.make_async_remote_copy(
            src_ref=ztx.at[peer],
            dst_ref=zrx.at[owned],
            send_sem=back_sems.at[0],
            recv_sem=back_sems.at[1],
            device_id=(dp, peer),
            device_id_type=MESH,
        ).start()

    pltpu.make_async_copy(tx.at[most], tx.at[most], ctx_sems.at[0]).wait()
    pltpu.make_async_copy(zrx.at[most], zrx.at[most], back_sems.at[1]).wait()
    for g in range(blocks):
        rows = zrx[pl.ds(g * SIDE, SIDE)].reshape(SIDE, LANES)
        lanes = pl.ds(g * LANES, LANES)
        carry[pl.ds(0, MODES), lanes] = residue[:, lanes] * unpack_rows(rows)
    stores[1].start()
    pltpu.make_async_copy(ztx.at[most], ztx.at[most], back_sems.at[0]).wait()

    def wait_totals(sem):
        @pl.when(late == 1)
        def _():
            pltpu.make_async_copy(prx, prx, sem).wait()

        @pl.when(late == 0)
        def _():
            others = pl.ds(0, groups - 1)
            pltpu.make_async_copy(prx.at[others], prx.at[others], sem).wait()

    wait_totals(dp_sems.at[1])
    total = prx[0]
    for n in range(1, groups):
        total = total + prx[n]
    totals[...] = total
    stores[2].start()
    wait_totals(dp_sems.at[0])
    for store in stores:
        store.wait()


def finish_kernel(grads, carry, totals, out, out_residue, out_decay, out_skip):
    blocks, length, _ = grads.shape
    ahead = (SIDE - lax.broadcasted_iota(jnp.int32, (8, LANES), 0)).astype(jnp.float32)
    for g in range(blocks):
        lanes = pl.ds(g * LANES, LANES)
        rate = [jnp.broadcast_to(carry[pl.ds(MODES + m, 1), lanes], (8, LANES)) for m in range(MODES)]
        power = [jnp.exp(rate[m] * -8.0) for m in range(MODES)]
        term = [
            jnp.exp(-rate[m] * ahead) * jnp.broadcast_to(carry[pl.ds(m, 1), lanes], (8, LANES))
            for m in range(MODES)
        ]
        for b in range(length // 8 - 1, -1, -1):
            rows = pl.ds(b * 8, 8)
            total = grads[g, rows, :]
            for m in range(MODES):
                total = total + term[m]
                if b:
                    term[m] = power[m] * term[m]
            out[rows, lanes] = total
    sublane = lax.broadcasted_iota(jnp.int32, (8, LANES), 0)
    for row, ref in ((0, out_residue), (1, out_decay)):
        spread = jnp.broadcast_to(totals[pl.ds(row, 1), :], (8, LANES))
        value = spread
        for m in range(1, MODES):
            value = jnp.where(sublane == m, roll(spread, -m), value)
        ref[...] = value[:, :GROUP]
    out_skip[...] = totals[2, :GROUP]


def body(shards, groups, tokens, cotangent, decay, residue, skip):
    _, length, channels = tokens.shape
    positions = float(length * shards * groups)
    blocks = channels // LANES
    vmem = pl.BlockSpec(memory_space=pltpu.VMEM)
    hbm = pl.BlockSpec(memory_space=pltpu.HBM)
    f32 = jnp.float32
    grads, carry, totals = pl.pallas_call(
        functools.partial(exchange_kernel, shards, groups, positions),
        out_shape=[
            jax.ShapeDtypeStruct((blocks, length, LANES), f32),
            jax.ShapeDtypeStruct((2 * MODES, channels), f32),
            jax.ShapeDtypeStruct((8, LANES), f32),
        ],
        in_specs=[hbm] * 5,
        out_specs=[hbm] * 3,
        scratch_shapes=[
            pltpu.VMEM((length, channels), jnp.bfloat16),
            pltpu.VMEM((length, channels), jnp.bfloat16),
            pltpu.VMEM((MODES, channels), f32),
            pltpu.VMEM((MODES, channels), f32),
            pltpu.VMEM((1, channels), f32),
            pltpu.VMEM((blocks, length, LANES), f32),
            pltpu.VMEM((blocks, length, LANES), f32),
            pltpu.VMEM((MODES, channels), f32),
            pltpu.VMEM((4, MODES * RUNS, LANES), f32),
            pltpu.VMEM((RUN, LANES), f32),
            pltpu.VMEM((blocks, RUNS * MODES, LANES), f32),
            pltpu.VMEM((shards, 8, LANES), f32),
            pltpu.VMEM((shards, 8, LANES), f32),
            pltpu.VMEM(((shards + SIDE) * MODES, LANES), f32),
            pltpu.VMEM((shards, 1, LANES), f32),
            pltpu.VMEM((shards, 1, LANES), f32),
            pltpu.VMEM((8, LANES), f32),
            pltpu.VMEM((groups, 8, LANES), f32),
            pltpu.VMEM((blocks, length, LANES), f32),
            pltpu.VMEM((2 * MODES, channels), f32),
            pltpu.VMEM((8, LANES), f32),
            pltpu.SemaphoreType.DMA((5,)),
            pltpu.SemaphoreType.DMA((3,)),
            pltpu.SemaphoreType.DMA((2,)),
            pltpu.SemaphoreType.DMA((2,)),
            pltpu.SemaphoreType.DMA((2,)),
            pltpu.SemaphoreType.REGULAR,
        ],
        compiler_params=pltpu.CompilerParams(
            collective_id=1, has_side_effects=True, vmem_limit_bytes=60 * 1024 * 1024
        ),
        name="exchange",
    )(tokens[0], cotangent[0], decay, residue, skip.reshape(1, channels))
    out, grad_residue, grad_decay, grad_skip = pl.pallas_call(
        finish_kernel,
        out_shape=[
            jax.ShapeDtypeStruct((length, channels), f32),
            jax.ShapeDtypeStruct((MODES, GROUP), f32),
            jax.ShapeDtypeStruct((MODES, GROUP), f32),
            jax.ShapeDtypeStruct((GROUP,), f32),
        ],
        in_specs=[vmem] * 3,
        out_specs=[vmem] * 4,
        compiler_params=pltpu.CompilerParams(vmem_limit_bytes=60 * 1024 * 1024),
        name="finish",
    )(grads, carry, totals)
    return out[None], grad_residue, grad_decay, grad_skip


def solution(mesh):
    return jax.shard_map(
        functools.partial(body, mesh.shape["ctx"], mesh.shape["dp"]),
        mesh=mesh,
        in_specs=(P("dp", "ctx", None), P("dp", "ctx", None), P(), P(), P()),
        out_specs=(P("dp", "ctx", None), P(None, "ctx"), P(None, "ctx"), P("ctx")),
        check_vma=False,
    )
```

```python
import functools

import jax
import jax.numpy as jnp
from jax import lax
from jax.experimental import pallas as pl
from jax.experimental.pallas import tpu as pltpu
from jax.sharding import PartitionSpec as P

MESH = pl.DeviceIdType.MESH
MODES = 8
LANES = 128
GROUP = 16
RUNS = 8
RUN = 16
SIDE = 8
PLANE = 8


def roll(value, groups):
    return pltpu.roll(value, (groups * GROUP) % LANES, 1)


def lane_group():
    return lax.broadcasted_iota(jnp.int32, (8, LANES), 1) // GROUP


def swap_blocks(blocks):
    group = lane_group()
    blocks = list(blocks)
    for step in (4, 2, 1):
        low = (group // step) % 2 == 0
        for a in range(SIDE):
            if (a // step) % 2 == 0:
                first, second = blocks[a], blocks[a + step]
                blocks[a] = jnp.where(low, first, roll(second, step))
                blocks[a + step] = jnp.where(low, roll(first, -step), second)
    return blocks


def summarise(g, xs, cs, rates, factors, sums, lags, starts, tx):
    lanes = pl.ds(pl.multiple_of(g * LANES, LANES), LANES)
    x = [xs[g, pl.ds(i, RUNS, stride=RUN), :] for i in range(RUN)]
    c = [cs[g, pl.ds(i, RUNS, stride=RUN), :] for i in range(RUN)]
    for mode in range(MODES):
        factor = jnp.broadcast_to(factors[pl.ds(mode, 1), lanes], (RUNS, LANES))
        state, tail = x[0], jnp.zeros((RUNS, LANES), jnp.float32)
        for i in range(1, RUN):
            tail = factor * (tail + state)
            state = factor * state + x[i]
        adjoint, head = c[RUN - 1], jnp.zeros((RUNS, LANES), jnp.float32)
        for i in range(RUN - 2, -1, -1):
            head = factor * (head + adjoint)
            adjoint = factor * adjoint + c[i]
        rows = pl.ds(mode * RUNS, RUNS)
        sums[0, rows, :] = state
        sums[1, rows, :] = tail
        sums[2, rows, :] = adjoint
        sums[3, rows, :] = head + adjoint
    for lag in range(RUN):
        total = c[lag] * x[0]
        for i in range(1, RUN - lag):
            total = total + c[i + lag] * x[i]
        lags[pl.ds(lag, 1), :] = jnp.sum(total, axis=0, keepdims=True)
    rate = rates[:, lanes]
    factor = factors[:, lanes]
    power = jnp.exp(rate * -float(RUN))

    def spread(lag):
        return jnp.broadcast_to(lags[pl.ds(lag, 1), :], (MODES, LANES))

    zeros = jnp.zeros((MODES, LANES), jnp.float32)
    inner, cross = spread(RUN - 1), zeros
    for lag in range(RUN - 2, -1, -1):
        cross = factor * cross + inner
        inner = factor * inner + spread(lag)
    run = [[sums[q, pl.ds(a, MODES, stride=RUNS), :] for q in range(4)] for a in range(RUNS)]
    state, tail, outer = zeros, zeros, zeros
    befores = []
    for a in range(RUNS):
        run_state, run_tail, run_adjoint, run_head = run[a]
        befores.append(state)
        outer = outer + state * run_adjoint
        cross = cross + state * run_head
        tail = run_tail + power * (tail + float(RUN) * state)
        state = run_state + power * state
    adjoint, head = zeros, zeros
    for a in range(RUNS - 1, -1, -1):
        run_state, run_tail, run_adjoint, run_head = run[a]
        starts[g, pl.ds(a * MODES, MODES), :] = adjoint
        cross = cross + adjoint * (run_tail + (float(RUN) * power) * befores[a])
        head = run_head + power * (head + float(RUN) * adjoint)
        adjoint = run_adjoint + power * adjoint
    inner = inner + factor * outer
    tiles = swap_blocks([adjoint, state, head, state, inner, cross, spread(0), tail])
    for i in range(SIDE):
        tx[g * SIDE + i] = tiles[i]


def local_grads(g, cs, factors, residue, skip, starts, grads):
    lanes = pl.ds(pl.multiple_of(g * LANES, LANES), LANES)

    def row(ref, mode):
        return jnp.broadcast_to(ref[pl.ds(mode, 1), lanes], (RUNS, LANES))

    factor = [row(factors, mode) for mode in range(MODES)]
    weight = [row(residue, mode) for mode in range(MODES)]
    direct = row(skip, 0)
    adjoint = [starts[g, pl.ds(mode, RUNS, stride=MODES), :] for mode in range(MODES)]
    for i in range(RUN - 1, -1, -1):
        now = cs[g, pl.ds(i, RUNS, stride=RUN), :]
        total = direct * now
        for mode in range(MODES):
            adjoint[mode] = factor[mode] * adjoint[mode] + now
            total = total + weight[mode] * adjoint[mode]
        grads[g, pl.ds(i, RUNS, stride=RUN), :] = total


def own_lanes(value, place):
    value = jnp.where(lane_group() == place, value, 0.0)
    for step in (1, 2, 4):
        value = value + roll(value, step)
    return value


def owner_sums(place, block, length, positions, rates, residue, rx, zbuf):
    lanes = pl.ds(pl.multiple_of(block * LANES, LANES), LANES)
    rate = own_lanes(rates[:, lanes], place)
    weight = own_lanes(residue[:, lanes], place)
    factor = jnp.exp(-rate)
    power = jnp.exp(rate * -float(length))
    shards = rx.shape[0]
    zeros = jnp.zeros((MODES, LANES), jnp.float32)
    state, plain, by_state, by_adjoint, both = zeros, zeros, zeros, zeros, zeros
    befores = []
    for k in range(shards):
        tile = rx[k]
        befores.append(state)
        plain = plain + tile
        by_state = by_state + state * roll(tile, 1)
        state = power * state + tile
    adjoint = zeros
    for k in range(shards - 1, -1, -1):
        tile = rx[k]
        zbuf[pl.ds(k * MODES, MODES), :] = adjoint
        by_adjoint = by_adjoint + adjoint * roll(tile, 1)
        both = both + befores[k] * roll(adjoint, 1)
        adjoint = power * adjoint + tile
    scale = 1.0 / positions
    sum_residue = roll(plain, -4) + factor * roll(by_state, -1)
    sum_decay = roll(plain, -5) + roll(by_state, -3) + by_adjoint + (float(length) * power) * roll(both, -1)
    sum_skip = roll(plain, -6)
    last = [sum_residue * scale, (-scale) * factor * weight * sum_decay, sum_skip * scale]
    for k in range(SIDE):
        zbuf[pl.ds((shards + k) * MODES, MODES), :] = last[k] if k < len(last) else zeros


def pack_rows(zbuf, a):
    group = lane_group()
    packed = zbuf[pl.ds(a * SIDE * MODES, SIDE, stride=MODES), :]
    for mode in range(1, MODES):
        rows = zbuf[pl.ds(a * SIDE * MODES + mode, SIDE, stride=MODES), :]
        packed = jnp.where(group == mode, roll(rows, mode), packed)
    return packed


def unpack_rows(rows):
    apart = (lane_group() - lax.broadcasted_iota(jnp.int32, (8, LANES), 0) + SIDE) % SIDE
    out = rows
    for step in range(1, SIDE):
        moved = roll(pltpu.roll(rows, SIDE - step, 0), step)
        out = jnp.where(apart == step, moved, out)
    return out


def exchange_kernel(
    shards,
    groups,
    positions,
    tokens,
    cotangent,
    rates_in,
    residue_in,
    skip_in,
    grads_out,
    zrx,
    prx,
    x_raw,
    c_raw,
    rates,
    residue,
    skip,
    xs,
    cs,
    factors,
    sums,
    lags,
    starts,
    tx,
    rx,
    zbuf,
    ztx,
    ptx,
    grads,
    in_sems,
    out_sems,
    ctx_sems,
    back_sems,
    dp_sems,
    ready_sem,
):
    dp, ctx = lax.axis_index("dp"), lax.axis_index("ctx")
    length, channels = x_raw.shape
    blocks = channels // LANES
    loads = [
        pltpu.make_async_copy(source, target, in_sems.at[n])
        for n, (source, target) in enumerate(
            ((tokens, x_raw), (cotangent, c_raw), (rates_in, rates), (residue_in, residue), (skip_in, skip))
        )
    ]
    for load in loads:
        load.start()
    half = groups // 2
    late = dp // half
    place_x = lax.rem(dp, half)
    mirror = (shards // PLANE - 1 - ctx // PLANE) * PLANE + lax.rem(ctx, PLANE)
    owned = ctx + late * (mirror - ctx)

    def same_half(d):
        return late * half + lax.rem(place_x + d, half)

    def other_half(d):
        return (1 - late) * half + d

    barrier = pltpu.get_barrier_semaphore()

    def greet(group, peer):
        pl.semaphore_signal(barrier, inc=1, device_id=(group, peer), device_id_type=MESH)

    @pl.loop(1, shards)
    def _(d):
        greet(dp, lax.rem(ctx + d, shards))

    @pl.loop(1, half)
    def _(d):
        greet(same_half(d), owned)

    @pl.when(late == 0)
    def _():
        @pl.loop(0, half)
        def _(d):
            greet(other_half(d), mirror)
            greet(other_half(d), ctx)

    for load in loads[2:]:
        load.wait()
    factors[...] = jnp.exp(-rates[...])
    for load, raw, wide in ((loads[0], x_raw, xs), (loads[1], c_raw, cs)):
        load.wait()
        for g in range(blocks):
            wide[g] = raw[:, pl.ds(g * LANES, LANES)].astype(jnp.float32)

    @pl.loop(0, blocks)
    def _(g):
        summarise(g, xs, cs, rates, factors, sums, lags, starts, tx)

    rx[ctx] = tx[owned]
    pl.semaphore_wait(barrier, shards - 1 + half - 1 + late * 2 * half)

    @pl.when(late == 1)
    def _():
        @pl.loop(0, half)
        def _(d):
            pl.semaphore_signal(ready_sem, inc=1, device_id=(other_half(d), ctx), device_id_type=MESH)

    @pl.loop(1, shards)
    def _(d):
        peer = lax.rem(ctx + d, shards)
        across = (shards // PLANE - 1 - peer // PLANE) * PLANE + lax.rem(peer, PLANE)
        pltpu.make_async_remote_copy(
            src_ref=tx.at[peer + late * (across - peer)],
            dst_ref=rx.at[ctx],
            send_sem=ctx_sems.at[0],
            recv_sem=ctx_sems.at[1],
            device_id=(dp, peer),
            device_id_type=MESH,
        ).start()

    @pl.loop(0, blocks)
    def _(g):
        local_grads(g, cs, factors, residue, skip, starts, grads)

    store = pltpu.make_async_copy(grads, grads_out, out_sems.at[0])
    store.start()
    most = pl.ds(0, shards - 1)
    pltpu.make_async_copy(rx.at[most], rx.at[most], ctx_sems.at[1]).wait()
    owner_sums(lax.rem(owned, SIDE), owned // SIDE, length, positions, rates, residue, rx, zbuf)
    ptx[...] = pack_rows(zbuf, shards // SIDE)

    def send_totals(group):
        pltpu.make_async_remote_copy(
            src_ref=ptx,
            dst_ref=prx.at[dp],
            send_sem=dp_sems.at[0],
            recv_sem=dp_sems.at[1],
            device_id=(group, owned),
            device_id_type=MESH,
        ).start()

    @pl.when(late == 1)
    def _():
        @pl.loop(0, half)
        def _(d):
            send_totals(other_half(d))

        send_totals(dp)

    @pl.loop(1, half)
    def _(d):
        send_totals(same_half(d))

    for a in range(shards // SIDE):
        ztx[pl.ds(a * SIDE, SIDE)] = pack_rows(zbuf, a).reshape(SIDE, 1, LANES)

    @pl.loop(1, shards)
    def _(d):
        peer = lax.rem(ctx + d, shards)
        pltpu.make_async_remote_copy(
            src_ref=ztx.at[peer],
            dst_ref=zrx.at[owned],
            send_sem=back_sems.at[0],
            recv_sem=back_sems.at[1],
            device_id=(dp, peer),
            device_id_type=MESH,
        ).start()

    @pl.when(late == 0)
    def _():
        keep = pltpu.make_async_copy(ptx, prx.at[dp], out_sems.at[1])
        keep.start()
        keep.wait()
        pl.semaphore_wait(ready_sem, half)

        @pl.loop(0, half)
        def _(d):
            send_totals(other_half(d))

    keep_row = pltpu.make_async_copy(ztx.at[ctx], zrx.at[owned], out_sems.at[2])
    keep_row.start()
    pltpu.make_async_copy(tx.at[most], tx.at[most], ctx_sems.at[0]).wait()
    store.wait()
    keep_row.wait()
    pltpu.make_async_copy(zrx.at[most], zrx.at[most], back_sems.at[1]).wait()
    pltpu.make_async_copy(ztx.at[most], ztx.at[most], back_sems.at[0]).wait()

    def wait_totals(sem):
        @pl.when(late == 1)
        def _():
            pltpu.make_async_copy(prx, prx, sem).wait()

        @pl.when(late == 0)
        def _():
            others = pl.ds(0, groups - 1)
            pltpu.make_async_copy(prx.at[others], prx.at[others], sem).wait()

    wait_totals(dp_sems.at[1])
    wait_totals(dp_sems.at[0])


def finish_kernel(grads, zrx, prx, rates, residue, out, out_residue, out_decay, out_skip):
    blocks, length, _ = grads.shape
    ahead = (SIDE - lax.broadcasted_iota(jnp.int32, (8, LANES), 0)).astype(jnp.float32)
    for g in range(blocks):
        lanes = pl.ds(g * LANES, LANES)
        rate = [jnp.broadcast_to(rates[pl.ds(m, 1), lanes], (8, LANES)) for m in range(MODES)]
        power = [jnp.exp(rate[m] * -8.0) for m in range(MODES)]
        start = residue[:, lanes] * unpack_rows(zrx[pl.ds(g * SIDE, SIDE)].reshape(SIDE, LANES))
        term = [
            jnp.exp(-rate[m] * ahead) * jnp.broadcast_to(start[m : m + 1], (8, LANES))
            for m in range(MODES)
        ]
        for b in range(length // 8 - 1, -1, -1):
            rows = pl.ds(b * 8, 8)
            total = grads[g, rows, :]
            for m in range(MODES):
                total = total + term[m]
                if b:
                    term[m] = power[m] * term[m]
            out[rows, lanes] = total
    totals = prx[0]
    for n in range(1, prx.shape[0]):
        totals = totals + prx[n]
    sublane = lax.broadcasted_iota(jnp.int32, (8, LANES), 0)
    for row, ref in ((0, out_residue), (1, out_decay)):
        spread = jnp.broadcast_to(totals[row : row + 1], (8, LANES))
        value = spread
        for m in range(1, MODES):
            value = jnp.where(sublane == m, roll(spread, -m), value)
        ref[...] = value[:, :GROUP]
    out_skip[...] = totals[2, :GROUP]


def body(shards, groups, tokens, cotangent, decay, residue, skip):
    _, length, channels = tokens.shape
    positions = float(length * shards * groups)
    blocks = channels // LANES
    vmem = pl.BlockSpec(memory_space=pltpu.VMEM)
    hbm = pl.BlockSpec(memory_space=pltpu.HBM)
    f32 = jnp.float32
    grads, carry, totals = pl.pallas_call(
        functools.partial(exchange_kernel, shards, groups, positions),
        out_shape=[
            jax.ShapeDtypeStruct((blocks, length, LANES), f32),
            jax.ShapeDtypeStruct((shards, 1, LANES), f32),
            jax.ShapeDtypeStruct((groups, 8, LANES), f32),
        ],
        in_specs=[hbm] * 5,
        out_specs=[hbm] * 3,
        scratch_shapes=[
            pltpu.VMEM((length, channels), jnp.bfloat16),
            pltpu.VMEM((length, channels), jnp.bfloat16),
            pltpu.VMEM((MODES, channels), f32),
            pltpu.VMEM((MODES, channels), f32),
            pltpu.VMEM((1, channels), f32),
            pltpu.VMEM((blocks, length, LANES), f32),
            pltpu.VMEM((blocks, length, LANES), f32),
            pltpu.VMEM((MODES, channels), f32),
            pltpu.VMEM((4, MODES * RUNS, LANES), f32),
            pltpu.VMEM((RUN, LANES), f32),
            pltpu.VMEM((blocks, RUNS * MODES, LANES), f32),
            pltpu.VMEM((shards, 8, LANES), f32),
            pltpu.VMEM((shards, 8, LANES), f32),
            pltpu.VMEM(((shards + SIDE) * MODES, LANES), f32),
            pltpu.VMEM((shards, 1, LANES), f32),
            pltpu.VMEM((8, LANES), f32),
            pltpu.VMEM((blocks, length, LANES), f32),
            pltpu.SemaphoreType.DMA((5,)),
            pltpu.SemaphoreType.DMA((3,)),
            pltpu.SemaphoreType.DMA((2,)),
            pltpu.SemaphoreType.DMA((2,)),
            pltpu.SemaphoreType.DMA((2,)),
            pltpu.SemaphoreType.REGULAR,
        ],
        compiler_params=pltpu.CompilerParams(
            collective_id=1, has_side_effects=True, vmem_limit_bytes=60 * 1024 * 1024
        ),
        name="exchange",
    )(tokens[0], cotangent[0], decay, residue, skip.reshape(1, channels))
    out, grad_residue, grad_decay, grad_skip = pl.pallas_call(
        finish_kernel,
        out_shape=[
            jax.ShapeDtypeStruct((length, channels), f32),
            jax.ShapeDtypeStruct((MODES, GROUP), f32),
            jax.ShapeDtypeStruct((MODES, GROUP), f32),
            jax.ShapeDtypeStruct((GROUP,), f32),
        ],
        in_specs=[vmem] * 5,
        out_specs=[vmem] * 4,
        compiler_params=pltpu.CompilerParams(vmem_limit_bytes=60 * 1024 * 1024),
        name="finish",
    )(grads, carry, totals, decay, residue)
    return out[None], grad_residue, grad_decay, grad_skip


def solution(mesh):
    return jax.shard_map(
        functools.partial(body, mesh.shape["ctx"], mesh.shape["dp"]),
        mesh=mesh,
        in_specs=(P("dp", "ctx", None), P("dp", "ctx", None), P(), P(), P()),
        out_specs=(P("dp", "ctx", None), P(None, "ctx"), P(None, "ctx"), P("ctx")),
        check_vma=False,
    )
```

```python
import functools

import jax
import jax.numpy as jnp
from jax import lax
from jax.experimental import pallas as pl
from jax.experimental.pallas import tpu as pltpu
from jax.sharding import PartitionSpec as P

MESH = pl.DeviceIdType.MESH
MODES = 8
LANES = 128
GROUP = 16
RUNS = 8
RUN = 16
SIDE = 8
PLANE = 8


def roll(value, groups):
    return pltpu.roll(value, (groups * GROUP) % LANES, 1)


def lane_group():
    return lax.broadcasted_iota(jnp.int32, (8, LANES), 1) // GROUP


def swap_blocks(blocks):
    group = lane_group()
    blocks = list(blocks)
    for step in (4, 2, 1):
        low = (group // step) % 2 == 0
        for a in range(SIDE):
            if (a // step) % 2 == 0:
                first, second = blocks[a], blocks[a + step]
                blocks[a] = jnp.where(low, first, roll(second, step))
                blocks[a + step] = jnp.where(low, roll(first, -step), second)
    return blocks


def run_sums(g, xs, cs, factors, sums, lags):
    lanes = pl.ds(pl.multiple_of(g * LANES, LANES), LANES)
    x = [xs[g, pl.ds(i, RUNS, stride=RUN), :] for i in range(RUN)]
    c = [cs[g, pl.ds(i, RUNS, stride=RUN), :] for i in range(RUN)]
    for mode in range(MODES):
        factor = jnp.broadcast_to(factors[pl.ds(mode, 1), lanes], (RUNS, LANES))
        state, tail = x[0], jnp.zeros((RUNS, LANES), jnp.float32)
        for i in range(1, RUN):
            tail = factor * (tail + state)
            state = factor * state + x[i]
        adjoint, head = c[RUN - 1], jnp.zeros((RUNS, LANES), jnp.float32)
        for i in range(RUN - 2, -1, -1):
            head = factor * (head + adjoint)
            adjoint = factor * adjoint + c[i]
        rows = pl.ds(mode * RUNS, RUNS)
        sums[g, 0, rows, :] = state
        sums[g, 1, rows, :] = tail
        sums[g, 2, rows, :] = adjoint
        sums[g, 3, rows, :] = head + adjoint
    for lag in range(RUN):
        total = c[lag] * x[0]
        for i in range(1, RUN - lag):
            total = total + c[i + lag] * x[i]
        lags[pl.ds(lag, 1), lanes] = jnp.sum(total, axis=0, keepdims=True)


def join_runs(rates, factors, sums, lags, starts, tx):
    blocks = sums.shape[0]
    rate = rates[...]
    factor = factors[...]
    power = jnp.exp(rate * -float(RUN))

    def spread(lag):
        return jnp.broadcast_to(lags[pl.ds(lag, 1), :], rate.shape)

    def run(q, a):
        parts = [sums[g, q, pl.ds(a, MODES, stride=RUNS), :] for g in range(blocks)]
        return jnp.concatenate(parts, axis=1)

    zeros = jnp.zeros(rate.shape, jnp.float32)
    inner, cross = spread(RUN - 1), zeros
    for lag in range(RUN - 2, -1, -1):
        cross = factor * cross + inner
        inner = factor * inner + spread(lag)
    state, tail, outer = zeros, zeros, zeros
    befores = []
    for a in range(RUNS):
        befores.append(state)
        outer = outer + state * run(2, a)
        cross = cross + state * run(3, a)
        tail = run(1, a) + power * (tail + float(RUN) * state)
        state = run(0, a) + power * state
    adjoint, head, both = zeros, zeros, zeros
    for a in range(RUNS - 1, -1, -1):
        for g in range(blocks):
            starts[g, pl.ds(a * MODES, MODES), :] = adjoint[:, g * LANES : (g + 1) * LANES]
        cross = cross + adjoint * run(1, a)
        both = both + adjoint * befores[a]
        head = run(3, a) + power * (head + float(RUN) * adjoint)
        adjoint = run(2, a) + power * adjoint
    inner = inner + factor * outer
    cross = cross + (float(RUN) * power) * both
    wide = [adjoint, state, head, state, inner, cross, spread(0), tail]
    for g in range(blocks):
        tiles = swap_blocks([value[:, g * LANES : (g + 1) * LANES] for value in wide])
        for i in range(SIDE):
            tx[g * SIDE + i] = tiles[i]


def local_grads(g, cs, factors, residue, skip, starts, grads):
    lanes = pl.ds(pl.multiple_of(g * LANES, LANES), LANES)

    def row(ref, mode):
        return jnp.broadcast_to(ref[pl.ds(mode, 1), lanes], (RUNS, LANES))

    factor = [row(factors, mode) for mode in range(MODES)]
    weight = [row(residue, mode) for mode in range(MODES)]
    direct = row(skip, 0)
    adjoint = [starts[g, pl.ds(mode, RUNS, stride=MODES), :] for mode in range(MODES)]
    for i in range(RUN - 1, -1, -1):
        now = cs[g, pl.ds(i, RUNS, stride=RUN), :]
        total = direct * now
        for mode in range(MODES):
            adjoint[mode] = factor[mode] * adjoint[mode] + now
            total = total + weight[mode] * adjoint[mode]
        grads[g, pl.ds(i, RUNS, stride=RUN), :] = total


def own_lanes(value, place):
    value = jnp.where(lane_group() == place, value, 0.0)
    for step in (1, 2, 4):
        value = value + roll(value, step)
    return value


def owner_factors(place, block, length, rates, residue):
    lanes = pl.ds(pl.multiple_of(block * LANES, LANES), LANES)
    rate = own_lanes(rates[:, lanes], place)
    weight = own_lanes(residue[:, lanes], place)
    factor = jnp.exp(-rate)
    return factor, jnp.exp(rate * -float(length)), weight


def owner_sums(factor, power, weight, length, positions, rx, zbuf):
    shards = rx.shape[0]
    zeros = jnp.zeros((MODES, LANES), jnp.float32)
    state, plain, by_state, by_adjoint, both = zeros, zeros, zeros, zeros, zeros
    befores, moved = [], []
    for k in range(shards):
        tile = rx[k]
        befores.append(state)
        moved.append(roll(tile, 1))
        plain = plain + tile
        by_state = by_state + state * moved[k]
        state = power * state + tile
    adjoint = zeros
    for k in range(shards - 1, -1, -1):
        tile = rx[k]
        zbuf[pl.ds(k * MODES, MODES), :] = adjoint
        by_adjoint = by_adjoint + adjoint * moved[k]
        both = both + befores[k] * roll(adjoint, 1)
        adjoint = power * adjoint + tile
    scale = 1.0 / positions
    sum_residue = roll(plain, -4) + factor * roll(by_state, -1)
    sum_decay = roll(plain, -5) + roll(by_state, -3) + by_adjoint + (float(length) * power) * roll(both, -1)
    sum_skip = roll(plain, -6)
    last = [sum_residue * scale, (-scale) * factor * weight * sum_decay, sum_skip * scale]
    for k in range(SIDE):
        zbuf[pl.ds((shards + k) * MODES, MODES), :] = last[k] if k < len(last) else zeros


def pack_rows(zbuf, a):
    group = lane_group()
    packed = zbuf[pl.ds(a * SIDE * MODES, SIDE, stride=MODES), :]
    for mode in range(1, MODES):
        rows = zbuf[pl.ds(a * SIDE * MODES + mode, SIDE, stride=MODES), :]
        packed = jnp.where(group == mode, roll(rows, mode), packed)
    return packed


def unpack_rows(rows):
    apart = (lane_group() - lax.broadcasted_iota(jnp.int32, (8, LANES), 0) + SIDE) % SIDE
    out = rows
    for step in range(1, SIDE):
        moved = roll(pltpu.roll(rows, SIDE - step, 0), step)
        out = jnp.where(apart == step, moved, out)
    return out


def exchange_kernel(
    shards,
    groups,
    positions,
    tokens,
    cotangent,
    rates_in,
    residue_in,
    skip_in,
    grads_out,
    zrx,
    prx,
    x_raw,
    c_raw,
    rates,
    residue,
    skip,
    xs,
    cs,
    factors,
    sums,
    lags,
    starts,
    tx,
    rx,
    zbuf,
    ztx,
    ptx,
    grads,
    in_sems,
    out_sems,
    ctx_sems,
    back_sems,
    dp_sems,
    ready_sem,
):
    dp, ctx = lax.axis_index("dp"), lax.axis_index("ctx")
    length, channels = x_raw.shape
    blocks = channels // LANES
    loads = [
        pltpu.make_async_copy(source, target, in_sems.at[n])
        for n, (source, target) in enumerate(
            ((tokens, x_raw), (cotangent, c_raw), (rates_in, rates), (residue_in, residue), (skip_in, skip))
        )
    ]
    for load in loads:
        load.start()
    half = groups // 2
    late = dp // half
    place_x = lax.rem(dp, half)
    mirror = (shards // PLANE - 1 - ctx // PLANE) * PLANE + lax.rem(ctx, PLANE)
    owned = ctx + late * (mirror - ctx)

    def same_half(d):
        return late * half + lax.rem(place_x + d, half)

    def other_half(d):
        return (1 - late) * half + d

    barrier = pltpu.get_barrier_semaphore()

    def greet(group, peer):
        pl.semaphore_signal(barrier, inc=1, device_id=(group, peer), device_id_type=MESH)

    @pl.loop(1, shards)
    def _(d):
        greet(dp, lax.rem(ctx + d, shards))

    @pl.loop(1, half)
    def _(d):
        greet(same_half(d), owned)

    @pl.when(late == 0)
    def _():
        @pl.loop(0, half)
        def _(d):
            greet(other_half(d), mirror)
            greet(other_half(d), ctx)

    for load in loads[2:]:
        load.wait()
    factors[...] = jnp.exp(-rates[...])
    for load, raw, wide in ((loads[0], x_raw, xs), (loads[1], c_raw, cs)):
        load.wait()
        for g in range(blocks):
            wide[g] = raw[:, pl.ds(g * LANES, LANES)].astype(jnp.float32)

    @pl.loop(0, blocks)
    def _(g):
        run_sums(g, xs, cs, factors, sums, lags)

    join_runs(rates, factors, sums, lags, starts, tx)

    rx[ctx] = tx[owned]
    pl.semaphore_wait(barrier, shards - 1 + half - 1 + late * 2 * half)

    @pl.when(late == 1)
    def _():
        @pl.loop(0, half)
        def _(d):
            pl.semaphore_signal(ready_sem, inc=1, device_id=(other_half(d), ctx), device_id_type=MESH)

    @pl.loop(1, shards)
    def _(d):
        peer = lax.rem(ctx + d, shards)
        across = (shards // PLANE - 1 - peer // PLANE) * PLANE + lax.rem(peer, PLANE)
        pltpu.make_async_remote_copy(
            src_ref=tx.at[peer + late * (across - peer)],
            dst_ref=rx.at[ctx],
            send_sem=ctx_sems.at[0],
            recv_sem=ctx_sems.at[1],
            device_id=(dp, peer),
            device_id_type=MESH,
        ).start()

    @pl.loop(0, blocks)
    def _(g):
        local_grads(g, cs, factors, residue, skip, starts, grads)

    store = pltpu.make_async_copy(grads, grads_out, out_sems.at[0])
    store.start()
    most = pl.ds(0, shards - 1)
    factor, power, weight = owner_factors(lax.rem(owned, SIDE), owned // SIDE, length, rates, residue)
    pltpu.make_async_copy(rx.at[most], rx.at[most], ctx_sems.at[1]).wait()
    owner_sums(factor, power, weight, length, positions, rx, zbuf)
    ptx[...] = pack_rows(zbuf, shards // SIDE)

    def send_totals(group):
        pltpu.make_async_remote_copy(
            src_ref=ptx,
            dst_ref=prx.at[dp],
            send_sem=dp_sems.at[0],
            recv_sem=dp_sems.at[1],
            device_id=(group, owned),
            device_id_type=MESH,
        ).start()

    @pl.when(late == 1)
    def _():
        @pl.loop(0, half)
        def _(d):
            send_totals(other_half(d))

        send_totals(dp)

    @pl.loop(1, half)
    def _(d):
        send_totals(same_half(d))

    for a in range(shards // SIDE):
        ztx[pl.ds(a * SIDE, SIDE)] = pack_rows(zbuf, a).reshape(SIDE, 1, LANES)

    @pl.loop(1, shards)
    def _(d):
        peer = lax.rem(ctx + d, shards)
        pltpu.make_async_remote_copy(
            src_ref=ztx.at[peer],
            dst_ref=zrx.at[owned],
            send_sem=back_sems.at[0],
            recv_sem=back_sems.at[1],
            device_id=(dp, peer),
            device_id_type=MESH,
        ).start()

    @pl.when(late == 0)
    def _():
        keep = pltpu.make_async_copy(ptx, prx.at[dp], out_sems.at[1])
        keep.start()
        keep.wait()
        pl.semaphore_wait(ready_sem, half)

        @pl.loop(0, half)
        def _(d):
            send_totals(other_half(d))

    keep_row = pltpu.make_async_copy(ztx.at[ctx], zrx.at[owned], out_sems.at[2])
    keep_row.start()
    pltpu.make_async_copy(tx.at[most], tx.at[most], ctx_sems.at[0]).wait()
    store.wait()
    keep_row.wait()
    pltpu.make_async_copy(zrx.at[most], zrx.at[most], back_sems.at[1]).wait()
    pltpu.make_async_copy(ztx.at[most], ztx.at[most], back_sems.at[0]).wait()

    def wait_totals(sem):
        @pl.when(late == 1)
        def _():
            pltpu.make_async_copy(prx, prx, sem).wait()

        @pl.when(late == 0)
        def _():
            others = pl.ds(0, groups - 1)
            pltpu.make_async_copy(prx.at[others], prx.at[others], sem).wait()

    wait_totals(dp_sems.at[1])
    wait_totals(dp_sems.at[0])


def finish_kernel(grads, zrx, prx, rates, residue, out, out_residue, out_decay, out_skip):
    blocks, length, _ = grads.shape
    ahead = (SIDE - lax.broadcasted_iota(jnp.int32, (8, LANES), 0)).astype(jnp.float32)
    for g in range(blocks):
        lanes = pl.ds(g * LANES, LANES)
        rate = [jnp.broadcast_to(rates[pl.ds(m, 1), lanes], (8, LANES)) for m in range(MODES)]
        power = [jnp.exp(rate[m] * -8.0) for m in range(MODES)]
        start = residue[:, lanes] * unpack_rows(zrx[pl.ds(g * SIDE, SIDE)].reshape(SIDE, LANES))
        term = [
            jnp.exp(-rate[m] * ahead) * jnp.broadcast_to(start[m : m + 1], (8, LANES))
            for m in range(MODES)
        ]
        for b in range(length // 8 - 1, -1, -1):
            rows = pl.ds(b * 8, 8)
            total = grads[g, rows, :]
            for m in range(MODES):
                total = total + term[m]
                if b:
                    term[m] = power[m] * term[m]
            out[rows, lanes] = total
    totals = prx[0]
    for n in range(1, prx.shape[0]):
        totals = totals + prx[n]
    sublane = lax.broadcasted_iota(jnp.int32, (8, LANES), 0)
    for row, ref in ((0, out_residue), (1, out_decay)):
        spread = jnp.broadcast_to(totals[row : row + 1], (8, LANES))
        value = spread
        for m in range(1, MODES):
            value = jnp.where(sublane == m, roll(spread, -m), value)
        ref[...] = value[:, :GROUP]
    out_skip[...] = totals[2, :GROUP]


def body(shards, groups, tokens, cotangent, decay, residue, skip):
    _, length, channels = tokens.shape
    positions = float(length * shards * groups)
    blocks = channels // LANES
    vmem = pl.BlockSpec(memory_space=pltpu.VMEM)
    hbm = pl.BlockSpec(memory_space=pltpu.HBM)
    f32 = jnp.float32
    grads, carry, totals = pl.pallas_call(
        functools.partial(exchange_kernel, shards, groups, positions),
        out_shape=[
            jax.ShapeDtypeStruct((blocks, length, LANES), f32),
            jax.ShapeDtypeStruct((shards, 1, LANES), f32),
            jax.ShapeDtypeStruct((groups, 8, LANES), f32),
        ],
        in_specs=[hbm] * 5,
        out_specs=[hbm] * 3,
        scratch_shapes=[
            pltpu.VMEM((length, channels), jnp.bfloat16),
            pltpu.VMEM((length, channels), jnp.bfloat16),
            pltpu.VMEM((MODES, channels), f32),
            pltpu.VMEM((MODES, channels), f32),
            pltpu.VMEM((1, channels), f32),
            pltpu.VMEM((blocks, length, LANES), f32),
            pltpu.VMEM((blocks, length, LANES), f32),
            pltpu.VMEM((MODES, channels), f32),
            pltpu.VMEM((blocks, 4, MODES * RUNS, LANES), f32),
            pltpu.VMEM((RUN, channels), f32),
            pltpu.VMEM((blocks, RUNS * MODES, LANES), f32),
            pltpu.VMEM((shards, 8, LANES), f32),
            pltpu.VMEM((shards, 8, LANES), f32),
            pltpu.VMEM(((shards + SIDE) * MODES, LANES), f32),
            pltpu.VMEM((shards, 1, LANES), f32),
            pltpu.VMEM((8, LANES), f32),
            pltpu.VMEM((blocks, length, LANES), f32),
            pltpu.SemaphoreType.DMA((5,)),
            pltpu.SemaphoreType.DMA((3,)),
            pltpu.SemaphoreType.DMA((2,)),
            pltpu.SemaphoreType.DMA((2,)),
            pltpu.SemaphoreType.DMA((2,)),
            pltpu.SemaphoreType.REGULAR,
        ],
        compiler_params=pltpu.CompilerParams(
            collective_id=1, has_side_effects=True, vmem_limit_bytes=60 * 1024 * 1024
        ),
        name="exchange",
    )(tokens[0], cotangent[0], decay, residue, skip.reshape(1, channels))
    out, grad_residue, grad_decay, grad_skip = pl.pallas_call(
        finish_kernel,
        out_shape=[
            jax.ShapeDtypeStruct((length, channels), f32),
            jax.ShapeDtypeStruct((MODES, GROUP), f32),
            jax.ShapeDtypeStruct((MODES, GROUP), f32),
            jax.ShapeDtypeStruct((GROUP,), f32),
        ],
        in_specs=[vmem] * 5,
        out_specs=[vmem] * 4,
        compiler_params=pltpu.CompilerParams(vmem_limit_bytes=60 * 1024 * 1024),
        name="finish",
    )(grads, carry, totals, decay, residue)
    return out[None], grad_residue, grad_decay, grad_skip


def solution(mesh):
    return jax.shard_map(
        functools.partial(body, mesh.shape["ctx"], mesh.shape["dp"]),
        mesh=mesh,
        in_specs=(P("dp", "ctx", None), P("dp", "ctx", None), P(), P(), P()),
        out_specs=(P("dp", "ctx", None), P(None, "ctx"), P(None, "ctx"), P("ctx")),
        check_vma=False,
    )
```

```python
import functools

import jax
import jax.numpy as jnp
from jax import lax
from jax.experimental import pallas as pl
from jax.experimental.pallas import tpu as pltpu
from jax.sharding import PartitionSpec as P

MESH = pl.DeviceIdType.MESH
MODES = 8
LANES = 128
GROUP = 16
RUNS = 8
RUN = 16
SIDE = 8
PLANE = 8


def roll(value, groups):
    return pltpu.roll(value, (groups * GROUP) % LANES, 1)


def lane_group():
    return lax.broadcasted_iota(jnp.int32, (8, LANES), 1) // GROUP


def swap_blocks(blocks):
    group = lane_group()
    blocks = list(blocks)
    for step in (4, 2, 1):
        low = (group // step) % 2 == 0
        for a in range(SIDE):
            if (a // step) % 2 == 0:
                first, second = blocks[a], blocks[a + step]
                blocks[a] = jnp.where(low, first, roll(second, step))
                blocks[a + step] = jnp.where(low, roll(first, -step), second)
    return blocks


def run_sums(g, xs, cs, factors, sums, lags):
    lanes = pl.ds(pl.multiple_of(g * LANES, LANES), LANES)
    x = [xs[g, pl.ds(i, RUNS, stride=RUN), :] for i in range(RUN)]
    c = [cs[g, pl.ds(i, RUNS, stride=RUN), :] for i in range(RUN)]
    for mode in range(MODES):
        factor = jnp.broadcast_to(factors[pl.ds(mode, 1), lanes], (RUNS, LANES))
        state, tail = x[0], jnp.zeros((RUNS, LANES), jnp.float32)
        for i in range(1, RUN):
            tail = factor * (tail + state)
            state = factor * state + x[i]
        adjoint, head = c[RUN - 1], jnp.zeros((RUNS, LANES), jnp.float32)
        for i in range(RUN - 2, -1, -1):
            head = factor * (head + adjoint)
            adjoint = factor * adjoint + c[i]
        rows = pl.ds(mode * RUNS, RUNS)
        sums[g, 0, rows, :] = state
        sums[g, 1, rows, :] = tail
        sums[g, 2, rows, :] = adjoint
        sums[g, 3, rows, :] = head + adjoint
    for lag in range(RUN):
        total = c[lag] * x[0]
        for i in range(1, RUN - lag):
            total = total + c[i + lag] * x[i]
        lags[pl.ds(lag, 1), lanes] = jnp.sum(total, axis=0, keepdims=True)


def join_runs(rates, factors, sums, lags, starts, tx):
    blocks = sums.shape[0]
    rate = rates[...]
    factor = factors[...]
    power = jnp.exp(rate * -float(RUN))

    def spread(lag):
        return jnp.broadcast_to(lags[pl.ds(lag, 1), :], rate.shape)

    def run(q, a):
        parts = [sums[g, q, pl.ds(a, MODES, stride=RUNS), :] for g in range(blocks)]
        return jnp.concatenate(parts, axis=1)

    zeros = jnp.zeros(rate.shape, jnp.float32)
    inner, cross = spread(RUN - 1), zeros
    for lag in range(RUN - 2, -1, -1):
        cross = factor * cross + inner
        inner = factor * inner + spread(lag)
    state, tail, outer = zeros, zeros, zeros
    befores = []
    for a in range(RUNS):
        befores.append(state)
        outer = outer + state * run(2, a)
        cross = cross + state * run(3, a)
        tail = run(1, a) + power * (tail + float(RUN) * state)
        state = run(0, a) + power * state
    adjoint, head, both = zeros, zeros, zeros
    for a in range(RUNS - 1, -1, -1):
        for g in range(blocks):
            starts[g, pl.ds(a * MODES, MODES), :] = adjoint[:, g * LANES : (g + 1) * LANES]
        cross = cross + adjoint * run(1, a)
        both = both + adjoint * befores[a]
        head = run(3, a) + power * (head + float(RUN) * adjoint)
        adjoint = run(2, a) + power * adjoint
    inner = inner + factor * outer
    cross = cross + (float(RUN) * power) * both
    wide = [adjoint, state, head, state, inner, cross, spread(0), tail]
    for g in range(blocks):
        tiles = swap_blocks([value[:, g * LANES : (g + 1) * LANES] for value in wide])
        for i in range(SIDE):
            tx[g * SIDE + i] = tiles[i]


def local_grads(g, cs, factors, residue, skip, starts, grads):
    lanes = pl.ds(pl.multiple_of(g * LANES, LANES), LANES)

    def row(ref, mode):
        return jnp.broadcast_to(ref[pl.ds(mode, 1), lanes], (RUNS, LANES))

    factor = [row(factors, mode) for mode in range(MODES)]
    weight = [row(residue, mode) for mode in range(MODES)]
    direct = row(skip, 0)
    adjoint = [starts[g, pl.ds(mode, RUNS, stride=MODES), :] for mode in range(MODES)]
    for i in range(RUN - 1, -1, -1):
        now = cs[g, pl.ds(i, RUNS, stride=RUN), :]
        total = direct * now
        for mode in range(MODES):
            adjoint[mode] = factor[mode] * adjoint[mode] + now
            total = total + weight[mode] * adjoint[mode]
        grads[g, pl.ds(i, RUNS, stride=RUN), :] = total


def own_lanes(value, place):
    value = jnp.where(lane_group() == place, value, 0.0)
    for step in (1, 2, 4):
        value = value + roll(value, step)
    return value


def owner_factors(place, block, length, rates, residue):
    lanes = pl.ds(pl.multiple_of(block * LANES, LANES), LANES)
    rate = own_lanes(rates[:, lanes], place)
    weight = own_lanes(residue[:, lanes], place)
    factor = jnp.exp(-rate)
    return factor, jnp.exp(rate * -float(length)), weight


def owner_sums(factor, power, weight, length, positions, rx, zbuf):
    shards = rx.shape[0]
    zeros = jnp.zeros((MODES, LANES), jnp.float32)
    state, plain, by_state, by_adjoint, both = zeros, zeros, zeros, zeros, zeros
    befores, moved = [], []
    for k in range(shards):
        tile = rx[k]
        befores.append(state)
        moved.append(roll(tile, 1))
        plain = plain + tile
        by_state = by_state + state * moved[k]
        state = power * state + tile
    adjoint = zeros
    for k in range(shards - 1, -1, -1):
        tile = rx[k]
        zbuf[pl.ds(k * MODES, MODES), :] = adjoint
        by_adjoint = by_adjoint + adjoint * moved[k]
        both = both + befores[k] * roll(adjoint, 1)
        adjoint = power * adjoint + tile
    scale = 1.0 / positions
    sum_residue = roll(plain, -4) + factor * roll(by_state, -1)
    sum_decay = roll(plain, -5) + roll(by_state, -3) + by_adjoint + (float(length) * power) * roll(both, -1)
    sum_skip = roll(plain, -6)
    last = [sum_residue * scale, (-scale) * factor * weight * sum_decay, sum_skip * scale]
    for k in range(SIDE):
        zbuf[pl.ds((shards + k) * MODES, MODES), :] = last[k] if k < len(last) else zeros


def pack_rows(zbuf, a):
    group = lane_group()
    packed = zbuf[pl.ds(a * SIDE * MODES, SIDE, stride=MODES), :]
    for mode in range(1, MODES):
        rows = zbuf[pl.ds(a * SIDE * MODES + mode, SIDE, stride=MODES), :]
        packed = jnp.where(group == mode, roll(rows, mode), packed)
    return packed


def unpack_rows(rows):
    apart = (lane_group() - lax.broadcasted_iota(jnp.int32, (8, LANES), 0) + SIDE) % SIDE
    out = rows
    for step in range(1, SIDE):
        moved = roll(pltpu.roll(rows, SIDE - step, 0), step)
        out = jnp.where(apart == step, moved, out)
    return out


def exchange_kernel(
    shards,
    groups,
    positions,
    tokens,
    cotangent,
    rates_in,
    residue_in,
    skip_in,
    grads_out,
    zrx,
    prx,
    x_raw,
    c_raw,
    rates,
    residue,
    skip,
    xs,
    cs,
    factors,
    sums,
    lags,
    starts,
    tx,
    rx,
    zbuf,
    ztx,
    ptx,
    grads,
    in_sems,
    out_sems,
    ctx_sems,
    back_sems,
    dp_sems,
    ready_sem,
):
    dp, ctx = lax.axis_index("dp"), lax.axis_index("ctx")
    length, channels = x_raw.shape
    blocks = channels // LANES
    loads = [
        pltpu.make_async_copy(source, target, in_sems.at[n])
        for n, (source, target) in enumerate(
            ((tokens, x_raw), (cotangent, c_raw), (rates_in, rates), (residue_in, residue), (skip_in, skip))
        )
    ]
    for load in loads:
        load.start()
    half = groups // 2
    late = dp // half
    place_x = lax.rem(dp, half)
    mirror = (shards // PLANE - 1 - ctx // PLANE) * PLANE + lax.rem(ctx, PLANE)
    owned = ctx + late * (mirror - ctx)

    def same_half(d):
        return late * half + lax.rem(place_x + d, half)

    def other_half(d):
        return (1 - late) * half + d

    barrier = pltpu.get_barrier_semaphore()

    def greet(group, peer):
        pl.semaphore_signal(barrier, inc=1, device_id=(group, peer), device_id_type=MESH)

    @pl.loop(1, shards)
    def _(d):
        greet(dp, lax.rem(ctx + d, shards))

    @pl.loop(1, half)
    def _(d):
        greet(same_half(d), owned)

    @pl.when(late == 0)
    def _():
        @pl.loop(0, half)
        def _(d):
            greet(other_half(d), mirror)
            greet(other_half(d), ctx)

    for load in loads[2:]:
        load.wait()
    factors[...] = jnp.exp(-rates[...])
    for load, raw, wide in ((loads[0], x_raw, xs), (loads[1], c_raw, cs)):
        load.wait()
        for g in range(blocks):
            wide[g] = raw[:, pl.ds(g * LANES, LANES)].astype(jnp.float32)

    def send_plane(plane):
        @pl.loop(0, PLANE)
        def _(d):
            inside = lax.rem(ctx + d, PLANE)
            part = plane * PLANE + inside
            across = (shards // PLANE - 1 - plane) * PLANE + inside
            peer = part + late * (across - part)

            @pl.when(peer != ctx)
            def _():
                pltpu.make_async_remote_copy(
                    src_ref=tx.at[part],
                    dst_ref=rx.at[ctx],
                    send_sem=ctx_sems.at[0],
                    recv_sem=ctx_sems.at[1],
                    device_id=(dp, peer),
                    device_id_type=MESH,
                ).start()

    @pl.loop(0, blocks)
    def _(g):
        run_sums(g, xs, cs, factors, sums, lags)

    join_runs(rates, factors, sums, lags, starts, tx)
    pl.semaphore_wait(barrier, shards - 1 + half - 1 + late * 2 * half)
    for plane in range(shards // PLANE):
        send_plane(plane)

    rx[ctx] = tx[owned]

    @pl.when(late == 1)
    def _():
        @pl.loop(0, half)
        def _(d):
            pl.semaphore_signal(ready_sem, inc=1, device_id=(other_half(d), ctx), device_id_type=MESH)

    @pl.loop(0, blocks)
    def _(g):
        local_grads(g, cs, factors, residue, skip, starts, grads)

    store = pltpu.make_async_copy(grads, grads_out, out_sems.at[0])
    store.start()
    most = pl.ds(0, shards - 1)
    factor, power, weight = owner_factors(lax.rem(owned, SIDE), owned // SIDE, length, rates, residue)
    pltpu.make_async_copy(rx.at[most], rx.at[most], ctx_sems.at[1]).wait()
    owner_sums(factor, power, weight, length, positions, rx, zbuf)
    ptx[...] = pack_rows(zbuf, shards // SIDE)

    def send_totals(group):
        pltpu.make_async_remote_copy(
            src_ref=ptx,
            dst_ref=prx.at[dp],
            send_sem=dp_sems.at[0],
            recv_sem=dp_sems.at[1],
            device_id=(group, owned),
            device_id_type=MESH,
        ).start()

    @pl.when(late == 1)
    def _():
        @pl.loop(0, half)
        def _(d):
            send_totals(other_half(d))

        send_totals(dp)

    @pl.loop(1, half)
    def _(d):
        send_totals(same_half(d))

    for a in range(shards // SIDE):
        ztx[pl.ds(a * SIDE, SIDE)] = pack_rows(zbuf, a).reshape(SIDE, 1, LANES)

    @pl.loop(1, shards)
    def _(d):
        peer = lax.rem(ctx + d, shards)
        pltpu.make_async_remote_copy(
            src_ref=ztx.at[peer],
            dst_ref=zrx.at[owned],
            send_sem=back_sems.at[0],
            recv_sem=back_sems.at[1],
            device_id=(dp, peer),
            device_id_type=MESH,
        ).start()

    @pl.when(late == 0)
    def _():
        keep = pltpu.make_async_copy(ptx, prx.at[dp], out_sems.at[1])
        keep.start()
        keep.wait()
        pl.semaphore_wait(ready_sem, half)

        @pl.loop(0, half)
        def _(d):
            send_totals(other_half(d))

    keep_row = pltpu.make_async_copy(ztx.at[ctx], zrx.at[owned], out_sems.at[2])
    keep_row.start()
    pltpu.make_async_copy(tx.at[most], tx.at[most], ctx_sems.at[0]).wait()
    store.wait()
    keep_row.wait()
    pltpu.make_async_copy(zrx.at[most], zrx.at[most], back_sems.at[1]).wait()
    pltpu.make_async_copy(ztx.at[most], ztx.at[most], back_sems.at[0]).wait()

    def wait_totals(sem):
        @pl.when(late == 1)
        def _():
            pltpu.make_async_copy(prx, prx, sem).wait()

        @pl.when(late == 0)
        def _():
            others = pl.ds(0, groups - 1)
            pltpu.make_async_copy(prx.at[others], prx.at[others], sem).wait()

    wait_totals(dp_sems.at[1])
    wait_totals(dp_sems.at[0])


def finish_kernel(grads, zrx, prx, rates, residue, out, out_residue, out_decay, out_skip):
    blocks, length, _ = grads.shape
    ahead = (SIDE - lax.broadcasted_iota(jnp.int32, (8, LANES), 0)).astype(jnp.float32)
    for g in range(blocks):
        lanes = pl.ds(g * LANES, LANES)
        rate = [jnp.broadcast_to(rates[pl.ds(m, 1), lanes], (8, LANES)) for m in range(MODES)]
        power = [jnp.exp(rate[m] * -8.0) for m in range(MODES)]
        start = residue[:, lanes] * unpack_rows(zrx[pl.ds(g * SIDE, SIDE)].reshape(SIDE, LANES))
        term = [
            jnp.exp(-rate[m] * ahead) * jnp.broadcast_to(start[m : m + 1], (8, LANES))
            for m in range(MODES)
        ]
        for b in range(length // 8 - 1, -1, -1):
            rows = pl.ds(b * 8, 8)
            total = grads[g, rows, :]
            for m in range(MODES):
                total = total + term[m]
                if b:
                    term[m] = power[m] * term[m]
            out[rows, lanes] = total
    totals = prx[0]
    for n in range(1, prx.shape[0]):
        totals = totals + prx[n]
    sublane = lax.broadcasted_iota(jnp.int32, (8, LANES), 0)
    for row, ref in ((0, out_residue), (1, out_decay)):
        spread = jnp.broadcast_to(totals[row : row + 1], (8, LANES))
        value = spread
        for m in range(1, MODES):
            value = jnp.where(sublane == m, roll(spread, -m), value)
        ref[...] = value[:, :GROUP]
    out_skip[...] = totals[2, :GROUP]


def body(shards, groups, tokens, cotangent, decay, residue, skip):
    _, length, channels = tokens.shape
    positions = float(length * shards * groups)
    blocks = channels // LANES
    vmem = pl.BlockSpec(memory_space=pltpu.VMEM)
    hbm = pl.BlockSpec(memory_space=pltpu.HBM)
    f32 = jnp.float32
    grads, carry, totals = pl.pallas_call(
        functools.partial(exchange_kernel, shards, groups, positions),
        out_shape=[
            jax.ShapeDtypeStruct((blocks, length, LANES), f32),
            jax.ShapeDtypeStruct((shards, 1, LANES), f32),
            jax.ShapeDtypeStruct((groups, 8, LANES), f32),
        ],
        in_specs=[hbm] * 5,
        out_specs=[hbm] * 3,
        scratch_shapes=[
            pltpu.VMEM((length, channels), jnp.bfloat16),
            pltpu.VMEM((length, channels), jnp.bfloat16),
            pltpu.VMEM((MODES, channels), f32),
            pltpu.VMEM((MODES, channels), f32),
            pltpu.VMEM((1, channels), f32),
            pltpu.VMEM((blocks, length, LANES), f32),
            pltpu.VMEM((blocks, length, LANES), f32),
            pltpu.VMEM((MODES, channels), f32),
            pltpu.VMEM((blocks, 4, MODES * RUNS, LANES), f32),
            pltpu.VMEM((RUN, channels), f32),
            pltpu.VMEM((blocks, RUNS * MODES, LANES), f32),
            pltpu.VMEM((shards, 8, LANES), f32),
            pltpu.VMEM((shards, 8, LANES), f32),
            pltpu.VMEM(((shards + SIDE) * MODES, LANES), f32),
            pltpu.VMEM((shards, 1, LANES), f32),
            pltpu.VMEM((8, LANES), f32),
            pltpu.VMEM((blocks, length, LANES), f32),
            pltpu.SemaphoreType.DMA((5,)),
            pltpu.SemaphoreType.DMA((3,)),
            pltpu.SemaphoreType.DMA((2,)),
            pltpu.SemaphoreType.DMA((2,)),
            pltpu.SemaphoreType.DMA((2,)),
            pltpu.SemaphoreType.REGULAR,
        ],
        compiler_params=pltpu.CompilerParams(
            collective_id=1, has_side_effects=True, vmem_limit_bytes=60 * 1024 * 1024
        ),
        name="exchange",
    )(tokens[0], cotangent[0], decay, residue, skip.reshape(1, channels))
    out, grad_residue, grad_decay, grad_skip = pl.pallas_call(
        finish_kernel,
        out_shape=[
            jax.ShapeDtypeStruct((length, channels), f32),
            jax.ShapeDtypeStruct((MODES, GROUP), f32),
            jax.ShapeDtypeStruct((MODES, GROUP), f32),
            jax.ShapeDtypeStruct((GROUP,), f32),
        ],
        in_specs=[vmem] * 5,
        out_specs=[vmem] * 4,
        compiler_params=pltpu.CompilerParams(vmem_limit_bytes=60 * 1024 * 1024),
        name="finish",
    )(grads, carry, totals, decay, residue)
    return out[None], grad_residue, grad_decay, grad_skip


def solution(mesh):
    return jax.shard_map(
        functools.partial(body, mesh.shape["ctx"], mesh.shape["dp"]),
        mesh=mesh,
        in_specs=(P("dp", "ctx", None), P("dp", "ctx", None), P(), P(), P()),
        out_specs=(P("dp", "ctx", None), P(None, "ctx"), P(None, "ctx"), P("ctx")),
        check_vma=False,
    )
```

```python
import functools

import jax
import jax.numpy as jnp
from jax import lax
from jax.experimental import pallas as pl
from jax.experimental.pallas import tpu as pltpu
from jax.sharding import PartitionSpec as P

MESH = pl.DeviceIdType.MESH
MODES = 8
LANES = 128
GROUP = 16
RUNS = 8
RUN = 16
SIDE = 8
SENT = 7
PLANE = 8


def roll(value, groups):
    return pltpu.roll(value, (groups * GROUP) % LANES, 1)


def lane_group():
    return lax.broadcasted_iota(jnp.int32, (8, LANES), 1) // GROUP


def swap_blocks(blocks):
    group = lane_group()
    blocks = list(blocks)
    for step in (4, 2, 1):
        low = (group // step) % 2 == 0
        for a in range(SIDE):
            if (a // step) % 2 == 0:
                first, second = blocks[a], blocks[a + step]
                blocks[a] = jnp.where(low, first, roll(second, step))
                blocks[a + step] = jnp.where(low, roll(first, -step), second)
    return blocks


def run_sums(g, xs, cs, factors, sums, lags):
    lanes = pl.ds(pl.multiple_of(g * LANES, LANES), LANES)
    x = [xs[g, pl.ds(i, RUNS, stride=RUN), :] for i in range(RUN)]
    c = [cs[g, pl.ds(i, RUNS, stride=RUN), :] for i in range(RUN)]
    for mode in range(MODES):
        factor = jnp.broadcast_to(factors[pl.ds(mode, 1), lanes], (RUNS, LANES))
        state, tail = x[0], jnp.zeros((RUNS, LANES), jnp.float32)
        for i in range(1, RUN):
            tail = factor * (tail + state)
            state = factor * state + x[i]
        adjoint, head = c[RUN - 1], jnp.zeros((RUNS, LANES), jnp.float32)
        for i in range(RUN - 2, -1, -1):
            head = factor * (head + adjoint)
            adjoint = factor * adjoint + c[i]
        rows = pl.ds(mode * RUNS, RUNS)
        sums[g, 0, rows, :] = state
        sums[g, 1, rows, :] = tail
        sums[g, 2, rows, :] = adjoint
        sums[g, 3, rows, :] = head + adjoint
    for lag in range(RUN):
        total = c[lag] * x[0]
        for i in range(1, RUN - lag):
            total = total + c[i + lag] * x[i]
        lags[pl.ds(lag, 1), lanes] = jnp.sum(total, axis=0, keepdims=True)


def join_runs(rates, factors, sums, lags, starts, stage, tx):
    blocks = sums.shape[0]
    rate = rates[...]
    factor = factors[...]
    power = jnp.exp(rate * -float(RUN))

    def spread(lag):
        return jnp.broadcast_to(lags[pl.ds(lag, 1), :], rate.shape)

    def run(q, a):
        parts = [sums[g, q, pl.ds(a, MODES, stride=RUNS), :] for g in range(blocks)]
        return jnp.concatenate(parts, axis=1)

    zeros = jnp.zeros(rate.shape, jnp.float32)
    inner, cross = spread(RUN - 1), zeros
    for lag in range(RUN - 2, -1, -1):
        cross = factor * cross + inner
        inner = factor * inner + spread(lag)
    state, tail, outer = zeros, zeros, zeros
    befores = []
    for a in range(RUNS):
        befores.append(state)
        outer = outer + state * run(2, a)
        cross = cross + state * run(3, a)
        tail = run(1, a) + power * (tail + float(RUN) * state)
        state = run(0, a) + power * state
    adjoint, head, both = zeros, zeros, zeros
    for a in range(RUNS - 1, -1, -1):
        for g in range(blocks):
            starts[g, pl.ds(a * MODES, MODES), :] = adjoint[:, g * LANES : (g + 1) * LANES]
        cross = cross + adjoint * run(1, a)
        both = both + adjoint * befores[a]
        head = run(3, a) + power * (head + float(RUN) * adjoint)
        adjoint = run(2, a) + power * adjoint
    inner = inner + factor * outer
    cross = cross + (float(RUN) * power) * both
    wide = [tail, adjoint, state, head, inner, cross, spread(0), zeros]
    for g in range(blocks):
        for q in range(SIDE):
            stage[g, pl.ds(q * MODES, MODES), :] = wide[q][:, g * LANES : (g + 1) * LANES]
    for g in range(blocks):
        tiles = swap_blocks([stage[g, pl.ds(m, SIDE, stride=MODES), :] for m in range(MODES)])
        for i in range(SIDE):
            tx[g * SIDE + i] = tiles[i]


def local_grads(g, cs, factors, residue, skip, starts, grads):
    lanes = pl.ds(pl.multiple_of(g * LANES, LANES), LANES)

    def row(ref, mode):
        return jnp.broadcast_to(ref[pl.ds(mode, 1), lanes], (RUNS, LANES))

    factor = [row(factors, mode) for mode in range(MODES)]
    weight = [row(residue, mode) for mode in range(MODES)]
    direct = row(skip, 0)
    adjoint = [starts[g, pl.ds(mode, RUNS, stride=MODES), :] for mode in range(MODES)]
    for i in range(RUN - 1, -1, -1):
        now = cs[g, pl.ds(i, RUNS, stride=RUN), :]
        total = direct * now
        for mode in range(MODES):
            adjoint[mode] = factor[mode] * adjoint[mode] + now
            total = total + weight[mode] * adjoint[mode]
        grads[g, pl.ds(i, RUNS, stride=RUN), :] = total


def own_lanes(value, place):
    value = jnp.where(lane_group() == place, value, 0.0)
    for step in (1, 2, 4):
        value = value + roll(value, step)
    return value


def own_row(value, place):
    return jnp.sum(jnp.where(own_rows() == lane_group(), own_lanes(value, place), 0.0), axis=0, keepdims=True)


def own_rows():
    return lax.broadcasted_iota(jnp.int32, (8, LANES), 0)


def owner_factors(place, block, length, rates, residue):
    lanes = pl.ds(pl.multiple_of(block * LANES, LANES), LANES)
    rate = own_row(rates[:, lanes], place)
    weight = own_row(residue[:, lanes], place)
    return jnp.exp(-rate), jnp.exp(rate * -float(length)), weight


def owner_sums(factor, power, weight, length, positions, rx, ztx, ptx):
    shards = rx.shape[0]
    zeros = jnp.zeros((SIDE, LANES), jnp.float32)
    step = jnp.broadcast_to(power, (SIDE, LANES))
    state, plain, by_start, by_head, by_tail, both = zeros, zeros, zeros, zeros, zeros, zeros
    befores, moved = [], []
    for k in range(shards):
        tile = rx[k]
        befores.append(state)
        moved.append(pltpu.roll(tile, 1, 0))
        plain = plain + tile
        by_start = by_start + state * moved[k]
        by_head = by_head + state * pltpu.roll(tile, SIDE - 1, 0)
        state = step * state + tile
    adjoint = zeros
    for k in range(shards - 1, -1, -1):
        ztx[k] = adjoint[1:2]
        by_tail = by_tail + adjoint * moved[k]
        both = both + befores[k] * pltpu.roll(adjoint, 1, 0)
        adjoint = step * adjoint + rx[k]
    scale = 1.0 / positions
    sum_residue = plain[4:5] + factor * by_start[2:3]
    sum_decay = plain[5:6] + by_head[2:3] + by_tail[1:2] + (float(length) * power) * both[2:3]
    ptx[0:1] = sum_residue * scale
    ptx[1:2] = (-scale) * factor * weight * sum_decay
    ptx[2:3] = plain[6:7] * scale
    ptx[3:8] = jnp.zeros((SIDE - 3, LANES), jnp.float32)


def unpack_rows(rows):
    apart = (lane_group() - lax.broadcasted_iota(jnp.int32, (8, LANES), 0) + SIDE) % SIDE
    out = rows
    for step in range(1, SIDE):
        moved = roll(pltpu.roll(rows, SIDE - step, 0), step)
        out = jnp.where(apart == step, moved, out)
    return out


def exchange_kernel(
    shards,
    groups,
    positions,
    tokens,
    cotangent,
    rates_in,
    residue_in,
    skip_in,
    grads_out,
    zrx,
    prx,
    x_raw,
    c_raw,
    rates,
    residue,
    skip,
    xs,
    cs,
    factors,
    sums,
    lags,
    starts,
    stage,
    tx,
    rx,
    ztx,
    ptx,
    grads,
    in_sems,
    out_sems,
    ctx_sems,
    back_sems,
    dp_sems,
    ready_sem,
):
    dp, ctx = lax.axis_index("dp"), lax.axis_index("ctx")
    length, channels = x_raw.shape
    blocks = channels // LANES
    loads = [
        pltpu.make_async_copy(source, target, in_sems.at[n])
        for n, (source, target) in enumerate(
            ((tokens, x_raw), (cotangent, c_raw), (rates_in, rates), (residue_in, residue), (skip_in, skip))
        )
    ]
    for load in loads:
        load.start()
    half = groups // 2
    late = dp // half
    place_x = lax.rem(dp, half)
    mirror = (shards // PLANE - 1 - ctx // PLANE) * PLANE + lax.rem(ctx, PLANE)
    owned = ctx + late * (mirror - ctx)

    def same_half(d):
        return late * half + lax.rem(place_x + d, half)

    def other_half(d):
        return (1 - late) * half + d

    sent = pl.ds(0, SENT)
    rx[...] = jnp.zeros(rx.shape, jnp.float32)
    barrier = pltpu.get_barrier_semaphore()

    def greet(group, peer):
        pl.semaphore_signal(barrier, inc=1, device_id=(group, peer), device_id_type=MESH)

    @pl.loop(1, shards)
    def _(d):
        greet(dp, lax.rem(ctx + d, shards))

    @pl.loop(1, half)
    def _(d):
        greet(same_half(d), owned)

    @pl.when(late == 0)
    def _():
        @pl.loop(0, half)
        def _(d):
            greet(other_half(d), mirror)
            greet(other_half(d), ctx)

    for load in loads[2:]:
        load.wait()
    factors[...] = jnp.exp(-rates[...])
    for load, raw, wide in ((loads[0], x_raw, xs), (loads[1], c_raw, cs)):
        load.wait()
        for g in range(blocks):
            wide[g] = raw[:, pl.ds(g * LANES, LANES)].astype(jnp.float32)

    def send_plane(plane):
        @pl.loop(0, PLANE)
        def _(d):
            inside = lax.rem(ctx + d, PLANE)
            part = plane * PLANE + inside
            across = (shards // PLANE - 1 - plane) * PLANE + inside
            peer = part + late * (across - part)

            @pl.when(peer != ctx)
            def _():
                pltpu.make_async_remote_copy(
                    src_ref=tx.at[part, sent],
                    dst_ref=rx.at[ctx, sent],
                    send_sem=ctx_sems.at[0],
                    recv_sem=ctx_sems.at[1],
                    device_id=(dp, peer),
                    device_id_type=MESH,
                ).start()

    @pl.loop(0, blocks)
    def _(g):
        run_sums(g, xs, cs, factors, sums, lags)

    join_runs(rates, factors, sums, lags, starts, stage, tx)
    pl.semaphore_wait(barrier, shards - 1 + half - 1 + late * 2 * half)
    for plane in range(shards // PLANE):
        send_plane(plane)

    rx[ctx] = tx[owned]

    @pl.when(late == 1)
    def _():
        @pl.loop(0, half)
        def _(d):
            pl.semaphore_signal(ready_sem, inc=1, device_id=(other_half(d), ctx), device_id_type=MESH)

    @pl.loop(0, blocks)
    def _(g):
        local_grads(g, cs, factors, residue, skip, starts, grads)

    store = pltpu.make_async_copy(grads, grads_out, out_sems.at[0])
    store.start()
    most = pl.ds(0, shards - 1)
    factor, power, weight = owner_factors(lax.rem(owned, SIDE), owned // SIDE, length, rates, residue)
    pltpu.make_async_copy(rx.at[most, sent], rx.at[most, sent], ctx_sems.at[1]).wait()
    owner_sums(factor, power, weight, length, positions, rx, ztx, ptx)

    def send_totals(group):
        pltpu.make_async_remote_copy(
            src_ref=ptx,
            dst_ref=prx.at[dp],
            send_sem=dp_sems.at[0],
            recv_sem=dp_sems.at[1],
            device_id=(group, owned),
            device_id_type=MESH,
        ).start()

    @pl.when(late == 1)
    def _():
        @pl.loop(0, half)
        def _(d):
            send_totals(other_half(d))

        send_totals(dp)

    @pl.loop(1, half)
    def _(d):
        send_totals(same_half(d))


    @pl.loop(1, shards)
    def _(d):
        peer = lax.rem(ctx + d, shards)
        pltpu.make_async_remote_copy(
            src_ref=ztx.at[peer],
            dst_ref=zrx.at[owned],
            send_sem=back_sems.at[0],
            recv_sem=back_sems.at[1],
            device_id=(dp, peer),
            device_id_type=MESH,
        ).start()

    @pl.when(late == 0)
    def _():
        keep = pltpu.make_async_copy(ptx, prx.at[dp], out_sems.at[1])
        keep.start()
        keep.wait()
        pl.semaphore_wait(ready_sem, half)

        @pl.loop(0, half)
        def _(d):
            send_totals(other_half(d))

    keep_row = pltpu.make_async_copy(ztx.at[ctx], zrx.at[owned], out_sems.at[2])
    keep_row.start()
    pltpu.make_async_copy(tx.at[most, sent], tx.at[most, sent], ctx_sems.at[0]).wait()
    store.wait()
    keep_row.wait()
    pltpu.make_async_copy(zrx.at[most], zrx.at[most], back_sems.at[1]).wait()
    pltpu.make_async_copy(ztx.at[most], ztx.at[most], back_sems.at[0]).wait()

    def wait_totals(sem):
        @pl.when(late == 1)
        def _():
            pltpu.make_async_copy(prx, prx, sem).wait()

        @pl.when(late == 0)
        def _():
            others = pl.ds(0, groups - 1)
            pltpu.make_async_copy(prx.at[others], prx.at[others], sem).wait()

    wait_totals(dp_sems.at[1])
    wait_totals(dp_sems.at[0])


def finish_kernel(grads, zrx, prx, rates, residue, out, out_residue, out_decay, out_skip):
    blocks, length, _ = grads.shape
    ahead = (SIDE - lax.broadcasted_iota(jnp.int32, (8, LANES), 0)).astype(jnp.float32)
    for g in range(blocks):
        lanes = pl.ds(g * LANES, LANES)
        rate = [jnp.broadcast_to(rates[pl.ds(m, 1), lanes], (8, LANES)) for m in range(MODES)]
        power = [jnp.exp(rate[m] * -8.0) for m in range(MODES)]
        start = residue[:, lanes] * unpack_rows(zrx[pl.ds(g * SIDE, SIDE)].reshape(SIDE, LANES))
        term = [
            jnp.exp(-rate[m] * ahead) * jnp.broadcast_to(start[m : m + 1], (8, LANES))
            for m in range(MODES)
        ]
        for b in range(length // 8 - 1, -1, -1):
            rows = pl.ds(b * 8, 8)
            total = grads[g, rows, :]
            for m in range(MODES):
                total = total + term[m]
                if b:
                    term[m] = power[m] * term[m]
            out[rows, lanes] = total
    totals = prx[0]
    for n in range(1, prx.shape[0]):
        totals = totals + prx[n]
    sublane = lax.broadcasted_iota(jnp.int32, (8, LANES), 0)
    for row, ref in ((0, out_residue), (1, out_decay)):
        spread = jnp.broadcast_to(totals[row : row + 1], (8, LANES))
        value = spread
        for m in range(1, MODES):
            value = jnp.where(sublane == m, roll(spread, -m), value)
        ref[...] = value[:, :GROUP]
    out_skip[...] = totals[2, :GROUP]


def body(shards, groups, tokens, cotangent, decay, residue, skip):
    _, length, channels = tokens.shape
    positions = float(length * shards * groups)
    blocks = channels // LANES
    vmem = pl.BlockSpec(memory_space=pltpu.VMEM)
    hbm = pl.BlockSpec(memory_space=pltpu.HBM)
    f32 = jnp.float32
    grads, carry, totals = pl.pallas_call(
        functools.partial(exchange_kernel, shards, groups, positions),
        out_shape=[
            jax.ShapeDtypeStruct((blocks, length, LANES), f32),
            jax.ShapeDtypeStruct((shards, 1, LANES), f32),
            jax.ShapeDtypeStruct((groups, 8, LANES), f32),
        ],
        in_specs=[hbm] * 5,
        out_specs=[hbm] * 3,
        scratch_shapes=[
            pltpu.VMEM((length, channels), jnp.bfloat16),
            pltpu.VMEM((length, channels), jnp.bfloat16),
            pltpu.VMEM((MODES, channels), f32),
            pltpu.VMEM((MODES, channels), f32),
            pltpu.VMEM((1, channels), f32),
            pltpu.VMEM((blocks, length, LANES), f32),
            pltpu.VMEM((blocks, length, LANES), f32),
            pltpu.VMEM((MODES, channels), f32),
            pltpu.VMEM((blocks, 4, MODES * RUNS, LANES), f32),
            pltpu.VMEM((RUN, channels), f32),
            pltpu.VMEM((blocks, RUNS * MODES, LANES), f32),
            pltpu.VMEM((blocks, SIDE * MODES, LANES), f32),
            pltpu.VMEM((shards, 8, LANES), f32),
            pltpu.VMEM((shards, 8, LANES), f32),
            pltpu.VMEM((shards, 1, LANES), f32),
            pltpu.VMEM((8, LANES), f32),
            pltpu.VMEM((blocks, length, LANES), f32),
            pltpu.SemaphoreType.DMA((5,)),
            pltpu.SemaphoreType.DMA((3,)),
            pltpu.SemaphoreType.DMA((2,)),
            pltpu.SemaphoreType.DMA((2,)),
            pltpu.SemaphoreType.DMA((2,)),
            pltpu.SemaphoreType.REGULAR,
        ],
        compiler_params=pltpu.CompilerParams(
            collective_id=1, has_side_effects=True, vmem_limit_bytes=60 * 1024 * 1024
        ),
        name="exchange",
    )(tokens[0], cotangent[0], decay, residue, skip.reshape(1, channels))
    out, grad_residue, grad_decay, grad_skip = pl.pallas_call(
        finish_kernel,
        out_shape=[
            jax.ShapeDtypeStruct((length, channels), f32),
            jax.ShapeDtypeStruct((MODES, GROUP), f32),
            jax.ShapeDtypeStruct((MODES, GROUP), f32),
            jax.ShapeDtypeStruct((GROUP,), f32),
        ],
        in_specs=[vmem] * 5,
        out_specs=[vmem] * 4,
        compiler_params=pltpu.CompilerParams(vmem_limit_bytes=60 * 1024 * 1024),
        name="finish",
    )(grads, carry, totals, decay, residue)
    return out[None], grad_residue, grad_decay, grad_skip


def solution(mesh):
    return jax.shard_map(
        functools.partial(body, mesh.shape["ctx"], mesh.shape["dp"]),
        mesh=mesh,
        in_specs=(P("dp", "ctx", None), P("dp", "ctx", None), P(), P(), P()),
        out_specs=(P("dp", "ctx", None), P(None, "ctx"), P(None, "ctx"), P("ctx")),
        check_vma=False,
    )
```

```python
import functools

import jax
import jax.numpy as jnp
from jax import lax
from jax.experimental import pallas as pl
from jax.experimental.pallas import tpu as pltpu
from jax.sharding import PartitionSpec as P

MESH = pl.DeviceIdType.MESH
MODES = 8
LANES = 128
GROUP = 16
RUNS = 8
RUN = 16
SIDE = 8
KEPT = 3
SENT = 7
PLANE = 8


def roll(value, groups):
    return pltpu.roll(value, (groups * GROUP) % LANES, 1)


def lane_group():
    return lax.broadcasted_iota(jnp.int32, (8, LANES), 1) // GROUP


def swap_blocks(blocks):
    group = lane_group()
    blocks = list(blocks)
    for step in (4, 2, 1):
        low = (group // step) % 2 == 0
        for a in range(SIDE):
            if (a // step) % 2 == 0:
                first, second = blocks[a], blocks[a + step]
                blocks[a] = jnp.where(low, first, roll(second, step))
                blocks[a + step] = jnp.where(low, roll(first, -step), second)
    return blocks


def run_sums(g, xs, cs, factors, sums, lags):
    lanes = pl.ds(pl.multiple_of(g * LANES, LANES), LANES)
    x = [xs[g, pl.ds(i, RUNS, stride=RUN), :] for i in range(RUN)]
    c = [cs[g, pl.ds(i, RUNS, stride=RUN), :] for i in range(RUN)]
    for mode in range(MODES):
        factor = jnp.broadcast_to(factors[pl.ds(mode, 1), lanes], (RUNS, LANES))
        state, tail = x[0], jnp.zeros((RUNS, LANES), jnp.float32)
        for i in range(1, RUN):
            tail = factor * (tail + state)
            state = factor * state + x[i]
        adjoint, head = c[RUN - 1], jnp.zeros((RUNS, LANES), jnp.float32)
        for i in range(RUN - 2, -1, -1):
            head = factor * (head + adjoint)
            adjoint = factor * adjoint + c[i]
        rows = pl.ds(mode * RUNS, RUNS)
        sums[g, 0, rows, :] = state
        sums[g, 1, rows, :] = tail
        sums[g, 2, rows, :] = adjoint
        sums[g, 3, rows, :] = head + adjoint
    for lag in range(RUN):
        total = c[lag] * x[0]
        for i in range(1, RUN - lag):
            total = total + c[i + lag] * x[i]
        lags[pl.ds(lag, 1), lanes] = jnp.sum(total, axis=0, keepdims=True)


def join_runs(rates, factors, sums, lags, starts, stage, tx):
    blocks = sums.shape[0]
    rate = rates[...]
    factor = factors[...]
    power = jnp.exp(rate * -float(RUN))

    def spread(lag):
        return jnp.broadcast_to(lags[pl.ds(lag, 1), :], rate.shape)

    def run(q, a):
        parts = [sums[g, q, pl.ds(a, MODES, stride=RUNS), :] for g in range(blocks)]
        return jnp.concatenate(parts, axis=1)

    zeros = jnp.zeros(rate.shape, jnp.float32)
    inner, cross = spread(RUN - 1), zeros
    for lag in range(RUN - 2, -1, -1):
        cross = factor * cross + inner
        inner = factor * inner + spread(lag)
    state, tail, outer = zeros, zeros, zeros
    befores = []
    for a in range(RUNS):
        befores.append(state)
        outer = outer + state * run(2, a)
        cross = cross + state * run(3, a)
        tail = run(1, a) + power * (tail + float(RUN) * state)
        state = run(0, a) + power * state
    adjoint, head, both = zeros, zeros, zeros
    for a in range(RUNS - 1, -1, -1):
        for g in range(blocks):
            starts[g, pl.ds(a * MODES, MODES), :] = adjoint[:, g * LANES : (g + 1) * LANES]
        cross = cross + adjoint * run(1, a)
        both = both + adjoint * befores[a]
        head = run(3, a) + power * (head + float(RUN) * adjoint)
        adjoint = run(2, a) + power * adjoint
    inner = inner + factor * outer
    cross = cross + (float(RUN) * power) * both
    wide = [tail, adjoint, state, head, inner, cross, spread(0), zeros]
    for g in range(blocks):
        for q in range(SIDE):
            stage[g, pl.ds(q * MODES, MODES), :] = wide[q][:, g * LANES : (g + 1) * LANES]
    for g in range(blocks):
        tiles = swap_blocks([stage[g, pl.ds(m, SIDE, stride=MODES), :] for m in range(MODES)])
        for i in range(SIDE):
            tx[g * SIDE + i] = tiles[i]


def local_grads(g, cs, factors, residue, skip, starts, grads):
    lanes = pl.ds(pl.multiple_of(g * LANES, LANES), LANES)

    def row(ref, mode):
        return jnp.broadcast_to(ref[pl.ds(mode, 1), lanes], (RUNS, LANES))

    factor = [row(factors, mode) for mode in range(MODES)]
    weight = [row(residue, mode) for mode in range(MODES)]
    direct = row(skip, 0)
    adjoint = [starts[g, pl.ds(mode, RUNS, stride=MODES), :] for mode in range(MODES)]
    for i in range(RUN - 1, -1, -1):
        now = cs[g, pl.ds(i, RUNS, stride=RUN), :]
        total = direct * now
        for mode in range(MODES):
            adjoint[mode] = factor[mode] * adjoint[mode] + now
            total = total + weight[mode] * adjoint[mode]
        grads[g, pl.ds(i, RUNS, stride=RUN), :] = total


def own_lanes(value, place):
    value = jnp.where(lane_group() == place, value, 0.0)
    for step in (1, 2, 4):
        value = value + roll(value, step)
    return value


def own_row(value, place):
    return jnp.sum(jnp.where(own_rows() == lane_group(), own_lanes(value, place), 0.0), axis=0, keepdims=True)


def own_rows():
    return lax.broadcasted_iota(jnp.int32, (8, LANES), 0)


def owner_factors(place, block, length, rates, residue):
    lanes = pl.ds(pl.multiple_of(block * LANES, LANES), LANES)
    rate = own_row(rates[:, lanes], place)
    weight = own_row(residue[:, lanes], place)
    return jnp.exp(-rate), jnp.exp(rate * -float(length)), weight


def owner_sums(factor, power, weight, length, positions, rx, ztx, ptx):
    shards = rx.shape[0]
    zeros = jnp.zeros((SIDE, LANES), jnp.float32)
    step = jnp.broadcast_to(power, (SIDE, LANES))
    state, plain, by_start, by_head, by_tail, both = zeros, zeros, zeros, zeros, zeros, zeros
    befores, moved = [], []
    for k in range(shards):
        tile = rx[k]
        befores.append(state)
        moved.append(pltpu.roll(tile, 1, 0))
        plain = plain + tile
        by_start = by_start + state * moved[k]
        by_head = by_head + state * pltpu.roll(tile, SIDE - 1, 0)
        state = step * state + tile
    adjoint = zeros
    for k in range(shards - 1, -1, -1):
        ztx[k] = adjoint[1:2]
        by_tail = by_tail + adjoint * moved[k]
        both = both + befores[k] * pltpu.roll(adjoint, 1, 0)
        adjoint = step * adjoint + rx[k]
    scale = 1.0 / positions
    sum_residue = plain[4:5] + factor * by_start[2:3]
    sum_decay = plain[5:6] + by_head[2:3] + by_tail[1:2] + (float(length) * power) * both[2:3]
    ptx[0:1] = sum_residue * scale
    ptx[1:2] = (-scale) * factor * weight * sum_decay
    ptx[2:3] = plain[6:7] * scale
    ptx[3:8] = jnp.zeros((SIDE - 3, LANES), jnp.float32)


def unpack_rows(rows):
    apart = (lane_group() - lax.broadcasted_iota(jnp.int32, (8, LANES), 0) + SIDE) % SIDE
    out = rows
    for step in range(1, SIDE):
        moved = roll(pltpu.roll(rows, SIDE - step, 0), step)
        out = jnp.where(apart == step, moved, out)
    return out


def exchange_kernel(
    shards,
    groups,
    positions,
    tokens,
    cotangent,
    rates_in,
    residue_in,
    skip_in,
    grads_out,
    zrx,
    prx,
    x_raw,
    c_raw,
    rates,
    residue,
    skip,
    xs,
    cs,
    factors,
    sums,
    lags,
    starts,
    stage,
    tx,
    rx,
    ztx,
    ptx,
    grads,
    in_sems,
    out_sems,
    ctx_sems,
    back_sems,
    dp_sems,
    ready_sem,
):
    dp, ctx = lax.axis_index("dp"), lax.axis_index("ctx")
    length, channels = x_raw.shape
    blocks = channels // LANES
    loads = [
        pltpu.make_async_copy(source, target, in_sems.at[n])
        for n, (source, target) in enumerate(
            ((tokens, x_raw), (cotangent, c_raw), (rates_in, rates), (residue_in, residue), (skip_in, skip))
        )
    ]
    for load in loads:
        load.start()
    half = groups // 2
    late = dp // half
    place_x = lax.rem(dp, half)
    mirror = (shards // PLANE - 1 - ctx // PLANE) * PLANE + lax.rem(ctx, PLANE)
    owned = ctx + late * (mirror - ctx)

    def same_half(d):
        return late * half + lax.rem(place_x + d, half)

    def other_half(d):
        return (1 - late) * half + d

    sent = pl.ds(0, SENT)
    kept = pl.ds(0, KEPT)
    rx[...] = jnp.zeros(rx.shape, jnp.float32)
    barrier = pltpu.get_barrier_semaphore()

    def greet(group, peer):
        pl.semaphore_signal(barrier, inc=1, device_id=(group, peer), device_id_type=MESH)

    @pl.loop(1, shards)
    def _(d):
        greet(dp, lax.rem(ctx + d, shards))

    @pl.loop(1, half)
    def _(d):
        greet(same_half(d), owned)

    @pl.when(late == 0)
    def _():
        @pl.loop(0, half)
        def _(d):
            greet(other_half(d), mirror)
            greet(other_half(d), ctx)

    for load in loads[2:]:
        load.wait()
    factors[...] = jnp.exp(-rates[...])
    for load, raw, wide in ((loads[0], x_raw, xs), (loads[1], c_raw, cs)):
        load.wait()
        for g in range(blocks):
            wide[g] = raw[:, pl.ds(g * LANES, LANES)].astype(jnp.float32)

    def send_plane(plane):
        @pl.loop(0, PLANE)
        def _(d):
            inside = d
            part = plane * PLANE + inside
            across = (shards // PLANE - 1 - plane) * PLANE + inside
            peer = part + late * (across - part)

            @pl.when(peer != ctx)
            def _():
                pltpu.make_async_remote_copy(
                    src_ref=tx.at[part, sent],
                    dst_ref=rx.at[ctx, sent],
                    send_sem=ctx_sems.at[0],
                    recv_sem=ctx_sems.at[1],
                    device_id=(dp, peer),
                    device_id_type=MESH,
                ).start()

    @pl.loop(0, blocks)
    def _(g):
        run_sums(g, xs, cs, factors, sums, lags)

    join_runs(rates, factors, sums, lags, starts, stage, tx)
    pl.semaphore_wait(barrier, shards - 1 + half - 1 + late * 2 * half)
    for plane in range(shards // PLANE):
        send_plane(plane)

    rx[ctx] = tx[owned]

    @pl.when(late == 1)
    def _():
        @pl.loop(0, half)
        def _(d):
            pl.semaphore_signal(ready_sem, inc=1, device_id=(other_half(d), ctx), device_id_type=MESH)

    @pl.loop(0, blocks)
    def _(g):
        local_grads(g, cs, factors, residue, skip, starts, grads)

    store = pltpu.make_async_copy(grads, grads_out, out_sems.at[0])
    store.start()
    most = pl.ds(0, shards - 1)
    factor, power, weight = owner_factors(lax.rem(owned, SIDE), owned // SIDE, length, rates, residue)
    pltpu.make_async_copy(rx.at[most, sent], rx.at[most, sent], ctx_sems.at[1]).wait()
    owner_sums(factor, power, weight, length, positions, rx, ztx, ptx)

    def send_totals(group):
        pltpu.make_async_remote_copy(
            src_ref=ptx.at[kept],
            dst_ref=prx.at[dp, kept],
            send_sem=dp_sems.at[0],
            recv_sem=dp_sems.at[1],
            device_id=(group, owned),
            device_id_type=MESH,
        ).start()

    @pl.when(late == 1)
    def _():
        @pl.loop(0, half)
        def _(d):
            send_totals(other_half(d))

        send_totals(dp)

    @pl.loop(1, half)
    def _(d):
        send_totals(same_half(d))


    @pl.loop(1, shards)
    def _(d):
        peer = lax.rem(ctx + d, shards)
        pltpu.make_async_remote_copy(
            src_ref=ztx.at[peer],
            dst_ref=zrx.at[owned],
            send_sem=back_sems.at[0],
            recv_sem=back_sems.at[1],
            device_id=(dp, peer),
            device_id_type=MESH,
        ).start()

    @pl.when(late == 0)
    def _():
        keep = pltpu.make_async_copy(ptx.at[kept], prx.at[dp, kept], out_sems.at[1])
        keep.start()
        keep.wait()
        pl.semaphore_wait(ready_sem, half)

        @pl.loop(0, half)
        def _(d):
            send_totals(other_half(d))

    keep_row = pltpu.make_async_copy(ztx.at[ctx], zrx.at[owned], out_sems.at[2])
    keep_row.start()
    pltpu.make_async_copy(tx.at[most, sent], tx.at[most, sent], ctx_sems.at[0]).wait()
    store.wait()
    keep_row.wait()
    pltpu.make_async_copy(zrx.at[most], zrx.at[most], back_sems.at[1]).wait()
    pltpu.make_async_copy(ztx.at[most], ztx.at[most], back_sems.at[0]).wait()

    def wait_totals(sem):
        @pl.when(late == 1)
        def _():
            pltpu.make_async_copy(prx.at[:, kept], prx.at[:, kept], sem).wait()

        @pl.when(late == 0)
        def _():
            others = pl.ds(0, groups - 1)
            pltpu.make_async_copy(prx.at[others, kept], prx.at[others, kept], sem).wait()

    wait_totals(dp_sems.at[1])
    wait_totals(dp_sems.at[0])


def finish_kernel(grads, zrx, prx, rates, residue, out, out_residue, out_decay, out_skip):
    blocks, length, _ = grads.shape
    ahead = (SIDE - lax.broadcasted_iota(jnp.int32, (8, LANES), 0)).astype(jnp.float32)
    for g in range(blocks):
        lanes = pl.ds(g * LANES, LANES)
        rate = [jnp.broadcast_to(rates[pl.ds(m, 1), lanes], (8, LANES)) for m in range(MODES)]
        power = [jnp.exp(rate[m] * -8.0) for m in range(MODES)]
        start = residue[:, lanes] * unpack_rows(zrx[pl.ds(g * SIDE, SIDE)].reshape(SIDE, LANES))
        term = [
            jnp.exp(-rate[m] * ahead) * jnp.broadcast_to(start[m : m + 1], (8, LANES))
            for m in range(MODES)
        ]
        for b in range(length // 8 - 1, -1, -1):
            rows = pl.ds(b * 8, 8)
            total = grads[g, rows, :]
            for m in range(MODES):
                total = total + term[m]
                if b:
                    term[m] = power[m] * term[m]
            out[rows, lanes] = total
    totals = prx[0]
    for n in range(1, prx.shape[0]):
        totals = totals + prx[n]
    sublane = lax.broadcasted_iota(jnp.int32, (8, LANES), 0)
    for row, ref in ((0, out_residue), (1, out_decay)):
        spread = jnp.broadcast_to(totals[row : row + 1], (8, LANES))
        value = spread
        for m in range(1, MODES):
            value = jnp.where(sublane == m, roll(spread, -m), value)
        ref[...] = value[:, :GROUP]
    out_skip[...] = totals[2, :GROUP]


def body(shards, groups, tokens, cotangent, decay, residue, skip):
    _, length, channels = tokens.shape
    positions = float(length * shards * groups)
    blocks = channels // LANES
    vmem = pl.BlockSpec(memory_space=pltpu.VMEM)
    hbm = pl.BlockSpec(memory_space=pltpu.HBM)
    f32 = jnp.float32
    grads, carry, totals = pl.pallas_call(
        functools.partial(exchange_kernel, shards, groups, positions),
        out_shape=[
            jax.ShapeDtypeStruct((blocks, length, LANES), f32),
            jax.ShapeDtypeStruct((shards, 1, LANES), f32),
            jax.ShapeDtypeStruct((groups, 8, LANES), f32),
        ],
        in_specs=[hbm] * 5,
        out_specs=[hbm] * 3,
        scratch_shapes=[
            pltpu.VMEM((length, channels), jnp.bfloat16),
            pltpu.VMEM((length, channels), jnp.bfloat16),
            pltpu.VMEM((MODES, channels), f32),
            pltpu.VMEM((MODES, channels), f32),
            pltpu.VMEM((1, channels), f32),
            pltpu.VMEM((blocks, length, LANES), f32),
            pltpu.VMEM((blocks, length, LANES), f32),
            pltpu.VMEM((MODES, channels), f32),
            pltpu.VMEM((blocks, 4, MODES * RUNS, LANES), f32),
            pltpu.VMEM((RUN, channels), f32),
            pltpu.VMEM((blocks, RUNS * MODES, LANES), f32),
            pltpu.VMEM((blocks, SIDE * MODES, LANES), f32),
            pltpu.VMEM((shards, 8, LANES), f32),
            pltpu.VMEM((shards, 8, LANES), f32),
            pltpu.VMEM((shards, 1, LANES), f32),
            pltpu.VMEM((8, LANES), f32),
            pltpu.VMEM((blocks, length, LANES), f32),
            pltpu.SemaphoreType.DMA((5,)),
            pltpu.SemaphoreType.DMA((3,)),
            pltpu.SemaphoreType.DMA((2,)),
            pltpu.SemaphoreType.DMA((2,)),
            pltpu.SemaphoreType.DMA((2,)),
            pltpu.SemaphoreType.REGULAR,
        ],
        compiler_params=pltpu.CompilerParams(
            collective_id=1, has_side_effects=True, vmem_limit_bytes=60 * 1024 * 1024
        ),
        name="exchange",
    )(tokens[0], cotangent[0], decay, residue, skip.reshape(1, channels))
    out, grad_residue, grad_decay, grad_skip = pl.pallas_call(
        finish_kernel,
        out_shape=[
            jax.ShapeDtypeStruct((length, channels), f32),
            jax.ShapeDtypeStruct((MODES, GROUP), f32),
            jax.ShapeDtypeStruct((MODES, GROUP), f32),
            jax.ShapeDtypeStruct((GROUP,), f32),
        ],
        in_specs=[vmem] * 5,
        out_specs=[vmem] * 4,
        compiler_params=pltpu.CompilerParams(vmem_limit_bytes=60 * 1024 * 1024),
        name="finish",
    )(grads, carry, totals, decay, residue)
    return out[None], grad_residue, grad_decay, grad_skip


def solution(mesh):
    return jax.shard_map(
        functools.partial(body, mesh.shape["ctx"], mesh.shape["dp"]),
        mesh=mesh,
        in_specs=(P("dp", "ctx", None), P("dp", "ctx", None), P(), P(), P()),
        out_specs=(P("dp", "ctx", None), P(None, "ctx"), P(None, "ctx"), P("ctx")),
        check_vma=False,
    )
```

```python
import functools

import jax
import jax.numpy as jnp
from jax import lax
from jax.experimental import pallas as pl
from jax.experimental.pallas import tpu as pltpu
from jax.sharding import PartitionSpec as P

MESH = pl.DeviceIdType.MESH
MODES = 8
LANES = 128
GROUP = 16
RUNS = 8
RUN = 16
SIDE = 8
KEPT = 3
SENT = 7
PLANE = 8


def roll(value, groups):
    return pltpu.roll(value, (groups * GROUP) % LANES, 1)


def lane_group():
    return lax.broadcasted_iota(jnp.int32, (8, LANES), 1) // GROUP


def swap_blocks(blocks):
    group = lane_group()
    blocks = list(blocks)
    for step in (4, 2, 1):
        low = (group // step) % 2 == 0
        for a in range(SIDE):
            if (a // step) % 2 == 0:
                first, second = blocks[a], blocks[a + step]
                blocks[a] = jnp.where(low, first, roll(second, step))
                blocks[a + step] = jnp.where(low, roll(first, -step), second)
    return blocks


def run_sums(g, xs, cs, factors, sums, lags):
    lanes = pl.ds(pl.multiple_of(g * LANES, LANES), LANES)
    x = [xs[g, pl.ds(i, RUNS, stride=RUN), :] for i in range(RUN)]
    c = [cs[g, pl.ds(i, RUNS, stride=RUN), :] for i in range(RUN)]
    for mode in range(MODES):
        factor = jnp.broadcast_to(factors[pl.ds(mode, 1), lanes], (RUNS, LANES))
        state, tail = x[0], jnp.zeros((RUNS, LANES), jnp.float32)
        for i in range(1, RUN):
            tail = factor * (tail + state)
            state = factor * state + x[i]
        adjoint, head = c[RUN - 1], jnp.zeros((RUNS, LANES), jnp.float32)
        for i in range(RUN - 2, -1, -1):
            head = factor * (head + adjoint)
            adjoint = factor * adjoint + c[i]
        rows = pl.ds(mode * RUNS, RUNS)
        sums[g, 0, rows, :] = state
        sums[g, 1, rows, :] = tail
        sums[g, 2, rows, :] = adjoint
        sums[g, 3, rows, :] = head + adjoint
    for lag in range(RUN):
        total = c[lag] * x[0]
        for i in range(1, RUN - lag):
            total = total + c[i + lag] * x[i]
        lags[pl.ds(lag, 1), lanes] = jnp.sum(total, axis=0, keepdims=True)


def join_runs(rates, factors, sums, lags, starts, stage, tx):
    blocks = sums.shape[0]
    rate = rates[...]
    factor = factors[...]
    power = jnp.exp(rate * -float(RUN))

    def spread(lag):
        return jnp.broadcast_to(lags[pl.ds(lag, 1), :], rate.shape)

    def run(q, a):
        parts = [sums[g, q, pl.ds(a, MODES, stride=RUNS), :] for g in range(blocks)]
        return jnp.concatenate(parts, axis=1)

    zeros = jnp.zeros(rate.shape, jnp.float32)
    inner, cross = spread(RUN - 1), zeros
    for lag in range(RUN - 2, -1, -1):
        cross = factor * cross + inner
        inner = factor * inner + spread(lag)
    state, tail, outer = zeros, zeros, zeros
    befores = []
    for a in range(RUNS):
        befores.append(state)
        outer = outer + state * run(2, a)
        cross = cross + state * run(3, a)
        tail = run(1, a) + power * (tail + float(RUN) * state)
        state = run(0, a) + power * state
    adjoint, head, both = zeros, zeros, zeros
    for a in range(RUNS - 1, -1, -1):
        for g in range(blocks):
            starts[g, pl.ds(a * MODES, MODES), :] = adjoint[:, g * LANES : (g + 1) * LANES]
        cross = cross + adjoint * run(1, a)
        both = both + adjoint * befores[a]
        head = run(3, a) + power * (head + float(RUN) * adjoint)
        adjoint = run(2, a) + power * adjoint
    inner = inner + factor * outer
    cross = cross + (float(RUN) * power) * both
    wide = [tail, adjoint, state, head, inner, cross, spread(0), zeros]
    for g in range(blocks):
        for q in range(SIDE):
            stage[g, pl.ds(q * MODES, MODES), :] = wide[q][:, g * LANES : (g + 1) * LANES]
    for g in range(blocks):
        tiles = swap_blocks([stage[g, pl.ds(m, SIDE, stride=MODES), :] for m in range(MODES)])
        for i in range(SIDE):
            tx[g * SIDE + i] = tiles[i]


def local_grads(g, cs, factors, residue, skip, starts, grads):
    lanes = pl.ds(pl.multiple_of(g * LANES, LANES), LANES)

    def row(ref, mode):
        return jnp.broadcast_to(ref[pl.ds(mode, 1), lanes], (RUNS, LANES))

    factor = [row(factors, mode) for mode in range(MODES)]
    weight = [row(residue, mode) for mode in range(MODES)]
    direct = row(skip, 0)
    adjoint = [starts[g, pl.ds(mode, RUNS, stride=MODES), :] for mode in range(MODES)]
    for i in range(RUN - 1, -1, -1):
        now = cs[g, pl.ds(i, RUNS, stride=RUN), :]
        total = direct * now
        for mode in range(MODES):
            adjoint[mode] = factor[mode] * adjoint[mode] + now
            total = total + weight[mode] * adjoint[mode]
        grads[g, pl.ds(i, RUNS, stride=RUN), :] = total


def own_lanes(value, place):
    value = jnp.where(lane_group() == place, value, 0.0)
    for step in (1, 2, 4):
        value = value + roll(value, step)
    return value


def own_row(value, place):
    return jnp.sum(jnp.where(own_rows() == lane_group(), own_lanes(value, place), 0.0), axis=0, keepdims=True)


def own_rows():
    return lax.broadcasted_iota(jnp.int32, (8, LANES), 0)


def owner_factors(place, block, length, rates, residue):
    lanes = pl.ds(pl.multiple_of(block * LANES, LANES), LANES)
    rate = own_row(rates[:, lanes], place)
    weight = own_row(residue[:, lanes], place)
    return jnp.exp(-rate), jnp.exp(rate * -float(length)), weight


def owner_sums(factor, power, weight, length, positions, rx, ztx, ptx):
    shards = rx.shape[0]
    zeros = jnp.zeros((SIDE, LANES), jnp.float32)
    step = jnp.broadcast_to(power, (SIDE, LANES))
    state, plain, by_start, by_head, by_tail, both = zeros, zeros, zeros, zeros, zeros, zeros
    befores, moved = [], []
    for k in range(shards):
        tile = rx[k]
        befores.append(state)
        moved.append(pltpu.roll(tile, 1, 0))
        plain = plain + tile
        by_start = by_start + state * moved[k]
        by_head = by_head + state * pltpu.roll(tile, SIDE - 1, 0)
        state = step * state + tile
    adjoint = zeros
    for k in range(shards - 1, -1, -1):
        ztx[k] = adjoint[1:2]
        by_tail = by_tail + adjoint * moved[k]
        both = both + befores[k] * pltpu.roll(adjoint, 1, 0)
        adjoint = step * adjoint + rx[k]
    scale = 1.0 / positions
    sum_residue = plain[4:5] + factor * by_start[2:3]
    sum_decay = plain[5:6] + by_head[2:3] + by_tail[1:2] + (float(length) * power) * both[2:3]
    ptx[0:1] = sum_residue * scale
    ptx[1:2] = (-scale) * factor * weight * sum_decay
    ptx[2:3] = plain[6:7] * scale
    ptx[3:8] = jnp.zeros((SIDE - 3, LANES), jnp.float32)


def unpack_rows(rows):
    apart = (lane_group() - lax.broadcasted_iota(jnp.int32, (8, LANES), 0) + SIDE) % SIDE
    out = rows
    for step in range(1, SIDE):
        moved = roll(pltpu.roll(rows, SIDE - step, 0), step)
        out = jnp.where(apart == step, moved, out)
    return out


def exchange_kernel(
    shards,
    groups,
    positions,
    tokens,
    cotangent,
    rates_in,
    residue_in,
    skip_in,
    grads_out,
    zrx,
    prx,
    x_raw,
    c_raw,
    rates,
    residue,
    skip,
    xs,
    cs,
    factors,
    sums,
    lags,
    starts,
    stage,
    tx,
    rx,
    ztx,
    ptx,
    grads,
    in_sems,
    out_sems,
    ctx_sems,
    back_sems,
    dp_sems,
    ready_sem,
):
    dp, ctx = lax.axis_index("dp"), lax.axis_index("ctx")
    length, channels = x_raw.shape
    blocks = channels // LANES
    loads = [
        pltpu.make_async_copy(source, target, in_sems.at[n])
        for n, (source, target) in enumerate(
            ((tokens, x_raw), (cotangent, c_raw), (rates_in, rates), (residue_in, residue), (skip_in, skip))
        )
    ]
    for load in loads:
        load.start()
    half = groups // 2
    late = dp // half
    place_x = lax.rem(dp, half)
    mirror = (shards // PLANE - 1 - ctx // PLANE) * PLANE + lax.rem(ctx, PLANE)
    owned = ctx + late * (mirror - ctx)

    def same_half(d):
        return late * half + lax.rem(place_x + d, half)

    def other_half(d):
        return (1 - late) * half + d

    sent = pl.ds(0, SENT)
    kept = pl.ds(0, KEPT)
    rx[...] = jnp.zeros(rx.shape, jnp.float32)
    barrier = pltpu.get_barrier_semaphore()

    def greet(group, peer):
        pl.semaphore_signal(barrier, inc=1, device_id=(group, peer), device_id_type=MESH)

    @pl.loop(1, shards, unroll=True)
    def _(d):
        greet(dp, lax.rem(ctx + d, shards))

    @pl.loop(1, half, unroll=True)
    def _(d):
        greet(same_half(d), owned)

    @pl.when(late == 0)
    def _():
        @pl.loop(0, half, unroll=True)
        def _(d):
            greet(other_half(d), mirror)
            greet(other_half(d), ctx)

    for load in loads[2:]:
        load.wait()
    factors[...] = jnp.exp(-rates[...])
    for load, raw, wide in ((loads[0], x_raw, xs), (loads[1], c_raw, cs)):
        load.wait()
        for g in range(blocks):
            wide[g] = raw[:, pl.ds(g * LANES, LANES)].astype(jnp.float32)

    def send_plane(plane):
        @pl.loop(0, PLANE, unroll=True)
        def _(d):
            inside = d
            part = plane * PLANE + inside
            across = (shards // PLANE - 1 - plane) * PLANE + inside
            peer = part + late * (across - part)

            @pl.when(peer != ctx)
            def _():
                pltpu.make_async_remote_copy(
                    src_ref=tx.at[part, sent],
                    dst_ref=rx.at[ctx, sent],
                    send_sem=ctx_sems.at[0],
                    recv_sem=ctx_sems.at[1],
                    device_id=(dp, peer),
                    device_id_type=MESH,
                ).start()

    @pl.loop(0, blocks)
    def _(g):
        run_sums(g, xs, cs, factors, sums, lags)

    join_runs(rates, factors, sums, lags, starts, stage, tx)
    pl.semaphore_wait(barrier, shards - 1 + half - 1 + late * 2 * half)
    for plane in range(shards // PLANE):
        send_plane(plane)

    rx[ctx] = tx[owned]

    @pl.when(late == 1)
    def _():
        @pl.loop(0, half, unroll=True)
        def _(d):
            pl.semaphore_signal(ready_sem, inc=1, device_id=(other_half(d), ctx), device_id_type=MESH)

    @pl.loop(0, blocks)
    def _(g):
        local_grads(g, cs, factors, residue, skip, starts, grads)

    store = pltpu.make_async_copy(grads, grads_out, out_sems.at[0])
    store.start()
    most = pl.ds(0, shards - 1)
    factor, power, weight = owner_factors(lax.rem(owned, SIDE), owned // SIDE, length, rates, residue)
    pltpu.make_async_copy(rx.at[most, sent], rx.at[most, sent], ctx_sems.at[1]).wait()
    owner_sums(factor, power, weight, length, positions, rx, ztx, ptx)

    def send_totals(group):
        pltpu.make_async_remote_copy(
            src_ref=ptx.at[kept],
            dst_ref=prx.at[dp, kept],
            send_sem=dp_sems.at[0],
            recv_sem=dp_sems.at[1],
            device_id=(group, owned),
            device_id_type=MESH,
        ).start()

    @pl.when(late == 1)
    def _():
        @pl.loop(0, half, unroll=True)
        def _(d):
            send_totals(other_half(d))

        send_totals(dp)

    @pl.loop(1, half, unroll=True)
    def _(d):
        send_totals(same_half(d))


    @pl.loop(1, shards, unroll=True)
    def _(d):
        peer = lax.rem(ctx + d, shards)
        pltpu.make_async_remote_copy(
            src_ref=ztx.at[peer],
            dst_ref=zrx.at[owned],
            send_sem=back_sems.at[0],
            recv_sem=back_sems.at[1],
            device_id=(dp, peer),
            device_id_type=MESH,
        ).start()

    @pl.when(late == 0)
    def _():
        keep = pltpu.make_async_copy(ptx.at[kept], prx.at[dp, kept], out_sems.at[1])
        keep.start()
        keep.wait()
        pl.semaphore_wait(ready_sem, half)

        @pl.loop(0, half, unroll=True)
        def _(d):
            send_totals(other_half(d))

    keep_row = pltpu.make_async_copy(ztx.at[ctx], zrx.at[owned], out_sems.at[2])
    keep_row.start()
    pltpu.make_async_copy(tx.at[most, sent], tx.at[most, sent], ctx_sems.at[0]).wait()
    store.wait()
    keep_row.wait()
    pltpu.make_async_copy(zrx.at[most], zrx.at[most], back_sems.at[1]).wait()
    pltpu.make_async_copy(ztx.at[most], ztx.at[most], back_sems.at[0]).wait()

    def wait_totals(sem):
        @pl.when(late == 1)
        def _():
            pltpu.make_async_copy(prx.at[:, kept], prx.at[:, kept], sem).wait()

        @pl.when(late == 0)
        def _():
            others = pl.ds(0, groups - 1)
            pltpu.make_async_copy(prx.at[others, kept], prx.at[others, kept], sem).wait()

    wait_totals(dp_sems.at[1])
    wait_totals(dp_sems.at[0])


def finish_kernel(grads, zrx, prx, rates, residue, out, out_residue, out_decay, out_skip):
    blocks, length, _ = grads.shape
    ahead = (SIDE - lax.broadcasted_iota(jnp.int32, (8, LANES), 0)).astype(jnp.float32)
    for g in range(blocks):
        lanes = pl.ds(g * LANES, LANES)
        rate = [jnp.broadcast_to(rates[pl.ds(m, 1), lanes], (8, LANES)) for m in range(MODES)]
        power = [jnp.exp(rate[m] * -8.0) for m in range(MODES)]
        start = residue[:, lanes] * unpack_rows(zrx[pl.ds(g * SIDE, SIDE)].reshape(SIDE, LANES))
        term = [
            jnp.exp(-rate[m] * ahead) * jnp.broadcast_to(start[m : m + 1], (8, LANES))
            for m in range(MODES)
        ]
        for b in range(length // 8 - 1, -1, -1):
            rows = pl.ds(b * 8, 8)
            total = grads[g, rows, :]
            for m in range(MODES):
                total = total + term[m]
                if b:
                    term[m] = power[m] * term[m]
            out[rows, lanes] = total
    totals = prx[0]
    for n in range(1, prx.shape[0]):
        totals = totals + prx[n]
    sublane = lax.broadcasted_iota(jnp.int32, (8, LANES), 0)
    for row, ref in ((0, out_residue), (1, out_decay)):
        spread = jnp.broadcast_to(totals[row : row + 1], (8, LANES))
        value = spread
        for m in range(1, MODES):
            value = jnp.where(sublane == m, roll(spread, -m), value)
        ref[...] = value[:, :GROUP]
    out_skip[...] = totals[2, :GROUP]


def body(shards, groups, tokens, cotangent, decay, residue, skip):
    _, length, channels = tokens.shape
    positions = float(length * shards * groups)
    blocks = channels // LANES
    vmem = pl.BlockSpec(memory_space=pltpu.VMEM)
    hbm = pl.BlockSpec(memory_space=pltpu.HBM)
    f32 = jnp.float32
    grads, carry, totals = pl.pallas_call(
        functools.partial(exchange_kernel, shards, groups, positions),
        out_shape=[
            jax.ShapeDtypeStruct((blocks, length, LANES), f32),
            jax.ShapeDtypeStruct((shards, 1, LANES), f32),
            jax.ShapeDtypeStruct((groups, 8, LANES), f32),
        ],
        in_specs=[hbm] * 5,
        out_specs=[hbm] * 3,
        scratch_shapes=[
            pltpu.VMEM((length, channels), jnp.bfloat16),
            pltpu.VMEM((length, channels), jnp.bfloat16),
            pltpu.VMEM((MODES, channels), f32),
            pltpu.VMEM((MODES, channels), f32),
            pltpu.VMEM((1, channels), f32),
            pltpu.VMEM((blocks, length, LANES), f32),
            pltpu.VMEM((blocks, length, LANES), f32),
            pltpu.VMEM((MODES, channels), f32),
            pltpu.VMEM((blocks, 4, MODES * RUNS, LANES), f32),
            pltpu.VMEM((RUN, channels), f32),
            pltpu.VMEM((blocks, RUNS * MODES, LANES), f32),
            pltpu.VMEM((blocks, SIDE * MODES, LANES), f32),
            pltpu.VMEM((shards, 8, LANES), f32),
            pltpu.VMEM((shards, 8, LANES), f32),
            pltpu.VMEM((shards, 1, LANES), f32),
            pltpu.VMEM((8, LANES), f32),
            pltpu.VMEM((blocks, length, LANES), f32),
            pltpu.SemaphoreType.DMA((5,)),
            pltpu.SemaphoreType.DMA((3,)),
            pltpu.SemaphoreType.DMA((2,)),
            pltpu.SemaphoreType.DMA((2,)),
            pltpu.SemaphoreType.DMA((2,)),
            pltpu.SemaphoreType.REGULAR,
        ],
        compiler_params=pltpu.CompilerParams(
            collective_id=1, has_side_effects=True, vmem_limit_bytes=60 * 1024 * 1024
        ),
        name="exchange",
    )(tokens[0], cotangent[0], decay, residue, skip.reshape(1, channels))
    out, grad_residue, grad_decay, grad_skip = pl.pallas_call(
        finish_kernel,
        out_shape=[
            jax.ShapeDtypeStruct((length, channels), f32),
            jax.ShapeDtypeStruct((MODES, GROUP), f32),
            jax.ShapeDtypeStruct((MODES, GROUP), f32),
            jax.ShapeDtypeStruct((GROUP,), f32),
        ],
        in_specs=[vmem] * 5,
        out_specs=[vmem] * 4,
        compiler_params=pltpu.CompilerParams(vmem_limit_bytes=60 * 1024 * 1024),
        name="finish",
    )(grads, carry, totals, decay, residue)
    return out[None], grad_residue, grad_decay, grad_skip


def solution(mesh):
    return jax.shard_map(
        functools.partial(body, mesh.shape["ctx"], mesh.shape["dp"]),
        mesh=mesh,
        in_specs=(P("dp", "ctx", None), P("dp", "ctx", None), P(), P(), P()),
        out_specs=(P("dp", "ctx", None), P(None, "ctx"), P(None, "ctx"), P("ctx")),
        check_vma=False,
    )
```

```python
import functools

import jax
import jax.numpy as jnp
from jax import lax
from jax.experimental import pallas as pl
from jax.experimental.pallas import tpu as pltpu
from jax.sharding import PartitionSpec as P

MESH = pl.DeviceIdType.MESH
MODES = 8
LANES = 128
GROUP = 16
RUNS = 8
RUN = 16
SIDE = 8
KEPT = 3
SENT = 7
PLANE = 8


def roll(value, groups):
    return pltpu.roll(value, (groups * GROUP) % LANES, 1)


def lane_group():
    return lax.broadcasted_iota(jnp.int32, (8, LANES), 1) // GROUP


def swap_blocks(blocks):
    group = lane_group()
    blocks = list(blocks)
    for step in (4, 2, 1):
        low = (group // step) % 2 == 0
        for a in range(SIDE):
            if (a // step) % 2 == 0:
                first, second = blocks[a], blocks[a + step]
                blocks[a] = jnp.where(low, first, roll(second, step))
                blocks[a + step] = jnp.where(low, roll(first, -step), second)
    return blocks


def run_sums(g, xs, cs, factors, sums, lags):
    lanes = pl.ds(pl.multiple_of(g * LANES, LANES), LANES)
    x = [xs[g, pl.ds(i, RUNS, stride=RUN), :] for i in range(RUN)]
    c = [cs[g, pl.ds(i, RUNS, stride=RUN), :] for i in range(RUN)]
    for mode in range(MODES):
        factor = jnp.broadcast_to(factors[pl.ds(mode, 1), lanes], (RUNS, LANES))
        state, tail = x[0], jnp.zeros((RUNS, LANES), jnp.float32)
        for i in range(1, RUN):
            tail = factor * (tail + state)
            state = factor * state + x[i]
        adjoint, head = c[RUN - 1], jnp.zeros((RUNS, LANES), jnp.float32)
        for i in range(RUN - 2, -1, -1):
            head = factor * (head + adjoint)
            adjoint = factor * adjoint + c[i]
        rows = pl.ds(mode * RUNS, RUNS)
        sums[g, 0, rows, :] = state
        sums[g, 1, rows, :] = tail
        sums[g, 2, rows, :] = adjoint
        sums[g, 3, rows, :] = head + adjoint
    for lag in range(RUN):
        total = c[lag] * x[0]
        for i in range(1, RUN - lag):
            total = total + c[i + lag] * x[i]
        lags[pl.ds(lag, 1), lanes] = jnp.sum(total, axis=0, keepdims=True)


def join_runs(rates, factors, sums, lags, starts, stage, tx):
    blocks = sums.shape[0]
    rate = rates[...]
    factor = factors[...]
    power = jnp.exp(rate * -float(RUN))

    def spread(lag):
        return jnp.broadcast_to(lags[pl.ds(lag, 1), :], rate.shape)

    def run(q, a):
        parts = [sums[g, q, pl.ds(a, MODES, stride=RUNS), :] for g in range(blocks)]
        return jnp.concatenate(parts, axis=1)

    zeros = jnp.zeros(rate.shape, jnp.float32)
    inner, cross = spread(RUN - 1), zeros
    for lag in range(RUN - 2, -1, -1):
        cross = factor * cross + inner
        inner = factor * inner + spread(lag)
    state, tail, outer = zeros, zeros, zeros
    befores = []
    for a in range(RUNS):
        befores.append(state)
        outer = outer + state * run(2, a)
        cross = cross + state * run(3, a)
        tail = run(1, a) + power * (tail + float(RUN) * state)
        state = run(0, a) + power * state
    adjoint, head, both = zeros, zeros, zeros
    for a in range(RUNS - 1, -1, -1):
        for g in range(blocks):
            starts[g, pl.ds(a * MODES, MODES), :] = adjoint[:, g * LANES : (g + 1) * LANES]
        cross = cross + adjoint * run(1, a)
        both = both + adjoint * befores[a]
        head = run(3, a) + power * (head + float(RUN) * adjoint)
        adjoint = run(2, a) + power * adjoint
    inner = inner + factor * outer
    cross = cross + (float(RUN) * power) * both
    wide = [tail, adjoint, state, head, inner, cross, spread(0), zeros]
    for g in range(blocks):
        for q in range(SIDE):
            stage[g, pl.ds(q * MODES, MODES), :] = wide[q][:, g * LANES : (g + 1) * LANES]
    for g in range(blocks):
        tiles = swap_blocks([stage[g, pl.ds(m, SIDE, stride=MODES), :] for m in range(MODES)])
        for i in range(SIDE):
            tx[g * SIDE + i] = tiles[i]


def local_grads(g, cs, factors, residue, skip, starts, grads):
    lanes = pl.ds(pl.multiple_of(g * LANES, LANES), LANES)

    def row(ref, mode):
        return jnp.broadcast_to(ref[pl.ds(mode, 1), lanes], (RUNS, LANES))

    factor = [row(factors, mode) for mode in range(MODES)]
    weight = [row(residue, mode) for mode in range(MODES)]
    direct = row(skip, 0)
    adjoint = [starts[g, pl.ds(mode, RUNS, stride=MODES), :] for mode in range(MODES)]
    for i in range(RUN - 1, -1, -1):
        now = cs[g, pl.ds(i, RUNS, stride=RUN), :]
        total = direct * now
        for mode in range(MODES):
            adjoint[mode] = factor[mode] * adjoint[mode] + now
            total = total + weight[mode] * adjoint[mode]
        grads[g, pl.ds(i, RUNS, stride=RUN), :] = total


def own_lanes(value, place):
    value = jnp.where(lane_group() == place, value, 0.0)
    for step in (1, 2, 4):
        value = value + roll(value, step)
    return value


def own_row(value, place):
    return jnp.sum(jnp.where(own_rows() == lane_group(), own_lanes(value, place), 0.0), axis=0, keepdims=True)


def own_rows():
    return lax.broadcasted_iota(jnp.int32, (8, LANES), 0)


def owner_factors(place, block, length, rates, residue):
    lanes = pl.ds(pl.multiple_of(block * LANES, LANES), LANES)
    rate = own_row(rates[:, lanes], place)
    weight = own_row(residue[:, lanes], place)
    return jnp.exp(-rate), jnp.exp(rate * -float(length)), weight


def owner_sums(factor, power, weight, length, positions, rx, ztx, ptx):
    shards = rx.shape[0]
    zeros = jnp.zeros((SIDE, LANES), jnp.float32)
    step = jnp.broadcast_to(power, (SIDE, LANES))
    state, plain, by_start, by_head, by_tail, both = zeros, zeros, zeros, zeros, zeros, zeros
    befores, moved = [], []
    for k in range(shards):
        tile = rx[k]
        befores.append(state)
        moved.append(pltpu.roll(tile, 1, 0))
        plain = plain + tile
        by_start = by_start + state * moved[k]
        by_head = by_head + state * pltpu.roll(tile, SIDE - 1, 0)
        state = step * state + tile
    adjoint = zeros
    for k in range(shards - 1, -1, -1):
        ztx[k] = adjoint[1:2]
        by_tail = by_tail + adjoint * moved[k]
        both = both + befores[k] * pltpu.roll(adjoint, 1, 0)
        adjoint = step * adjoint + rx[k]
    scale = 1.0 / positions
    sum_residue = plain[4:5] + factor * by_start[2:3]
    sum_decay = plain[5:6] + by_head[2:3] + by_tail[1:2] + (float(length) * power) * both[2:3]
    ptx[0:1] = sum_residue * scale
    ptx[1:2] = (-scale) * factor * weight * sum_decay
    ptx[2:3] = plain[6:7] * scale
    ptx[3:8] = jnp.zeros((SIDE - 3, LANES), jnp.float32)


def unpack_rows(rows):
    apart = (lane_group() - lax.broadcasted_iota(jnp.int32, (8, LANES), 0) + SIDE) % SIDE
    out = rows
    for step in range(1, SIDE):
        moved = roll(pltpu.roll(rows, SIDE - step, 0), step)
        out = jnp.where(apart == step, moved, out)
    return out


def exchange_kernel(
    shards,
    groups,
    positions,
    tokens,
    cotangent,
    rates_in,
    residue_in,
    skip_in,
    grads_out,
    zrx,
    prx,
    x_raw,
    c_raw,
    rates,
    residue,
    skip,
    xs,
    cs,
    factors,
    sums,
    lags,
    starts,
    stage,
    tx,
    rx,
    ztx,
    ptx,
    grads,
    in_sems,
    out_sems,
    ctx_sems,
    back_sems,
    dp_sems,
    ready_sem,
):
    dp, ctx = lax.axis_index("dp"), lax.axis_index("ctx")
    length, channels = x_raw.shape
    blocks = channels // LANES
    loads = [
        pltpu.make_async_copy(source, target, in_sems.at[n])
        for n, (source, target) in enumerate(
            ((tokens, x_raw), (cotangent, c_raw), (rates_in, rates), (residue_in, residue), (skip_in, skip))
        )
    ]
    for load in loads:
        load.start()
    half = groups // 2
    late = dp // half
    place_x = lax.rem(dp, half)
    mirror = (shards // PLANE - 1 - ctx // PLANE) * PLANE + lax.rem(ctx, PLANE)
    owned = ctx + late * (mirror - ctx)

    def same_half(d):
        return late * half + lax.rem(place_x + d, half)

    def other_half(d):
        return (1 - late) * half + d

    sent = pl.ds(0, SENT)
    kept = pl.ds(0, KEPT)
    rx[...] = jnp.zeros(rx.shape, jnp.float32)
    barrier = pltpu.get_barrier_semaphore()

    def greet(group, peer):
        pl.semaphore_signal(barrier, inc=1, device_id=(group, peer), device_id_type=MESH)

    @pl.loop(1, shards, unroll=True)
    def _(d):
        greet(dp, lax.rem(ctx + d, shards))

    @pl.loop(1, half, unroll=True)
    def _(d):
        greet(same_half(d), owned)

    @pl.when(late == 0)
    def _():
        @pl.loop(0, half, unroll=True)
        def _(d):
            greet(other_half(d), mirror)
            greet(other_half(d), ctx)

    for load in loads[2:]:
        load.wait()
    factors[...] = jnp.exp(-rates[...])
    for load, raw, wide in ((loads[0], x_raw, xs), (loads[1], c_raw, cs)):
        load.wait()
        for g in range(blocks):
            wide[g] = raw[:, pl.ds(g * LANES, LANES)].astype(jnp.float32)

    def send_plane(plane):
        @pl.loop(0, PLANE, unroll=True)
        def _(d):
            inside = d
            part = plane * PLANE + inside
            across = (shards // PLANE - 1 - plane) * PLANE + inside
            peer = part + late * (across - part)

            @pl.when(peer != ctx)
            def _():
                pltpu.make_async_remote_copy(
                    src_ref=tx.at[part, sent],
                    dst_ref=rx.at[ctx, sent],
                    send_sem=ctx_sems.at[0],
                    recv_sem=ctx_sems.at[1],
                    device_id=(dp, peer),
                    device_id_type=MESH,
                ).start()

    @pl.loop(0, blocks)
    def _(g):
        run_sums(g, xs, cs, factors, sums, lags)

    join_runs(rates, factors, sums, lags, starts, stage, tx)
    pl.semaphore_wait(barrier, shards - 1 + half - 1 + late * 2 * half)
    for plane in range(shards // PLANE):
        send_plane(plane)

    rx[ctx] = tx[owned]

    @pl.when(late == 1)
    def _():
        @pl.loop(0, half, unroll=True)
        def _(d):
            pl.semaphore_signal(ready_sem, inc=1, device_id=(other_half(d), ctx), device_id_type=MESH)

    @pl.loop(0, blocks)
    def _(g):
        local_grads(g, cs, factors, residue, skip, starts, grads)

    store = pltpu.make_async_copy(grads, grads_out, out_sems.at[0])
    store.start()
    most = pl.ds(0, shards - 1)
    factor, power, weight = owner_factors(lax.rem(owned, SIDE), owned // SIDE, length, rates, residue)
    pltpu.make_async_copy(rx.at[most, sent], rx.at[most, sent], ctx_sems.at[1]).wait()
    owner_sums(factor, power, weight, length, positions, rx, ztx, ptx)

    def send_totals(group):
        pltpu.make_async_remote_copy(
            src_ref=ptx.at[kept],
            dst_ref=prx.at[dp, kept],
            send_sem=dp_sems.at[0],
            recv_sem=dp_sems.at[1],
            device_id=(group, owned),
            device_id_type=MESH,
        ).start()

    @pl.when(late == 1)
    def _():
        @pl.loop(0, half, unroll=True)
        def _(d):
            send_totals(other_half(d))

        send_totals(dp)

    @pl.loop(1, half, unroll=True)
    def _(d):
        send_totals(same_half(d))


    @pl.loop(1, shards, unroll=True)
    def _(d):
        peer = lax.rem(ctx + d, shards)
        pltpu.make_async_remote_copy(
            src_ref=ztx.at[peer],
            dst_ref=zrx.at[owned],
            send_sem=back_sems.at[0],
            recv_sem=back_sems.at[1],
            device_id=(dp, peer),
            device_id_type=MESH,
        ).start()

    @pl.when(late == 0)
    def _():
        keep = pltpu.make_async_copy(ptx.at[kept], prx.at[dp, kept], out_sems.at[1])
        keep.start()
        keep.wait()
        pl.semaphore_wait(ready_sem, half)

        @pl.loop(0, half, unroll=True)
        def _(d):
            send_totals(other_half(d))

    keep_row = pltpu.make_async_copy(ztx.at[ctx], zrx.at[owned], out_sems.at[2])
    keep_row.start()
    pltpu.make_async_copy(tx.at[most, sent], tx.at[most, sent], ctx_sems.at[0]).wait()
    store.wait()
    keep_row.wait()
    pltpu.make_async_copy(zrx.at[most], zrx.at[most], back_sems.at[1]).wait()
    pltpu.make_async_copy(ztx.at[most], ztx.at[most], back_sems.at[0]).wait()

    def wait_totals(sem):
        @pl.when(late == 1)
        def _():
            pltpu.make_async_copy(prx.at[:, kept], prx.at[:, kept], sem).wait()

        @pl.when(late == 0)
        def _():
            others = pl.ds(0, groups - 1)
            pltpu.make_async_copy(prx.at[others, kept], prx.at[others, kept], sem).wait()

    wait_totals(dp_sems.at[1])
    wait_totals(dp_sems.at[0])


def finish_kernel(grads, zrx, prx, rates, residue, out, out_residue, out_decay, out_skip):
    blocks, length, _ = grads.shape
    ahead = (SIDE - lax.broadcasted_iota(jnp.int32, (8, LANES), 0)).astype(jnp.float32)
    powers = jnp.exp(rates[...] * -8.0)
    for g in range(blocks):
        lanes = pl.ds(g * LANES, LANES)
        rate = [jnp.broadcast_to(rates[pl.ds(m, 1), lanes], (8, LANES)) for m in range(MODES)]
        power = [
            jnp.broadcast_to(powers[m : m + 1, g * LANES : (g + 1) * LANES], (8, LANES)) for m in range(MODES)
        ]
        start = residue[:, lanes] * unpack_rows(zrx[pl.ds(g * SIDE, SIDE)].reshape(SIDE, LANES))
        term = [
            jnp.exp(-rate[m] * ahead) * jnp.broadcast_to(start[m : m + 1], (8, LANES))
            for m in range(MODES)
        ]
        for b in range(length // 8 - 1, -1, -1):
            rows = pl.ds(b * 8, 8)
            total = grads[g, rows, :]
            for m in range(MODES):
                total = total + term[m]
                if b:
                    term[m] = power[m] * term[m]
            out[rows, lanes] = total
    totals = prx[0]
    for n in range(1, prx.shape[0]):
        totals = totals + prx[n]
    sublane = lax.broadcasted_iota(jnp.int32, (8, LANES), 0)
    for row, ref in ((0, out_residue), (1, out_decay)):
        spread = jnp.broadcast_to(totals[row : row + 1], (8, LANES))
        value = spread
        for m in range(1, MODES):
            value = jnp.where(sublane == m, roll(spread, -m), value)
        ref[...] = value[:, :GROUP]
    out_skip[...] = totals[2, :GROUP]


def body(shards, groups, tokens, cotangent, decay, residue, skip):
    _, length, channels = tokens.shape
    positions = float(length * shards * groups)
    blocks = channels // LANES
    vmem = pl.BlockSpec(memory_space=pltpu.VMEM)
    hbm = pl.BlockSpec(memory_space=pltpu.HBM)
    f32 = jnp.float32
    grads, carry, totals = pl.pallas_call(
        functools.partial(exchange_kernel, shards, groups, positions),
        out_shape=[
            jax.ShapeDtypeStruct((blocks, length, LANES), f32),
            jax.ShapeDtypeStruct((shards, 1, LANES), f32),
            jax.ShapeDtypeStruct((groups, 8, LANES), f32),
        ],
        in_specs=[hbm] * 5,
        out_specs=[hbm] * 3,
        scratch_shapes=[
            pltpu.VMEM((length, channels), jnp.bfloat16),
            pltpu.VMEM((length, channels), jnp.bfloat16),
            pltpu.VMEM((MODES, channels), f32),
            pltpu.VMEM((MODES, channels), f32),
            pltpu.VMEM((1, channels), f32),
            pltpu.VMEM((blocks, length, LANES), f32),
            pltpu.VMEM((blocks, length, LANES), f32),
            pltpu.VMEM((MODES, channels), f32),
            pltpu.VMEM((blocks, 4, MODES * RUNS, LANES), f32),
            pltpu.VMEM((RUN, channels), f32),
            pltpu.VMEM((blocks, RUNS * MODES, LANES), f32),
            pltpu.VMEM((blocks, SIDE * MODES, LANES), f32),
            pltpu.VMEM((shards, 8, LANES), f32),
            pltpu.VMEM((shards, 8, LANES), f32),
            pltpu.VMEM((shards, 1, LANES), f32),
            pltpu.VMEM((8, LANES), f32),
            pltpu.VMEM((blocks, length, LANES), f32),
            pltpu.SemaphoreType.DMA((5,)),
            pltpu.SemaphoreType.DMA((3,)),
            pltpu.SemaphoreType.DMA((2,)),
            pltpu.SemaphoreType.DMA((2,)),
            pltpu.SemaphoreType.DMA((2,)),
            pltpu.SemaphoreType.REGULAR,
        ],
        compiler_params=pltpu.CompilerParams(
            collective_id=1, has_side_effects=True, vmem_limit_bytes=60 * 1024 * 1024
        ),
        name="exchange",
    )(tokens[0], cotangent[0], decay, residue, skip.reshape(1, channels))
    out, grad_residue, grad_decay, grad_skip = pl.pallas_call(
        finish_kernel,
        out_shape=[
            jax.ShapeDtypeStruct((length, channels), f32),
            jax.ShapeDtypeStruct((MODES, GROUP), f32),
            jax.ShapeDtypeStruct((MODES, GROUP), f32),
            jax.ShapeDtypeStruct((GROUP,), f32),
        ],
        in_specs=[vmem] * 5,
        out_specs=[vmem] * 4,
        compiler_params=pltpu.CompilerParams(vmem_limit_bytes=60 * 1024 * 1024),
        name="finish",
    )(grads, carry, totals, decay, residue)
    return out[None], grad_residue, grad_decay, grad_skip


def solution(mesh):
    return jax.shard_map(
        functools.partial(body, mesh.shape["ctx"], mesh.shape["dp"]),
        mesh=mesh,
        in_specs=(P("dp", "ctx", None), P("dp", "ctx", None), P(), P(), P()),
        out_specs=(P("dp", "ctx", None), P(None, "ctx"), P(None, "ctx"), P("ctx")),
        check_vma=False,
    )
```

```python
import functools

import jax
import jax.numpy as jnp
from jax import lax
from jax.experimental import pallas as pl
from jax.experimental.pallas import tpu as pltpu
from jax.sharding import PartitionSpec as P

MESH = pl.DeviceIdType.MESH
MODES = 8
LANES = 128
GROUP = 16
RUNS = 8
RUN = 16
SIDE = 8
KEPT = 3
SENT = 7
PLANE = 8


def roll(value, groups):
    return pltpu.roll(value, (groups * GROUP) % LANES, 1)


def lane_group():
    return lax.broadcasted_iota(jnp.int32, (8, LANES), 1) // GROUP


def swap_blocks(blocks):
    group = lane_group()
    blocks = list(blocks)
    for step in (4, 2, 1):
        low = (group // step) % 2 == 0
        for a in range(SIDE):
            if (a // step) % 2 == 0:
                first, second = blocks[a], blocks[a + step]
                blocks[a] = jnp.where(low, first, roll(second, step))
                blocks[a + step] = jnp.where(low, roll(first, -step), second)
    return blocks


def run_sums(g, xs, cs, factors, sums, lags):
    lanes = pl.ds(pl.multiple_of(g * LANES, LANES), LANES)
    x = [xs[g, pl.ds(i, RUNS, stride=RUN), :] for i in range(RUN)]
    c = [cs[g, pl.ds(i, RUNS, stride=RUN), :] for i in range(RUN)]
    for mode in range(MODES):
        factor = jnp.broadcast_to(factors[pl.ds(mode, 1), lanes], (RUNS, LANES))
        state, tail = x[0], jnp.zeros((RUNS, LANES), jnp.float32)
        for i in range(1, RUN):
            tail = factor * (tail + state)
            state = factor * state + x[i]
        adjoint, head = c[RUN - 1], jnp.zeros((RUNS, LANES), jnp.float32)
        for i in range(RUN - 2, -1, -1):
            head = factor * (head + adjoint)
            adjoint = factor * adjoint + c[i]
        rows = pl.ds(mode * RUNS, RUNS)
        sums[g, 0, rows, :] = state
        sums[g, 1, rows, :] = tail
        sums[g, 2, rows, :] = adjoint
        sums[g, 3, rows, :] = head + adjoint
    for lag in range(RUN):
        total = c[lag] * x[0]
        for i in range(1, RUN - lag):
            total = total + c[i + lag] * x[i]
        lags[pl.ds(lag, 1), lanes] = jnp.sum(total, axis=0, keepdims=True)


def join_runs(rates, factors, sums, lags, starts, stage, tx):
    blocks = sums.shape[0]
    rate = rates[...]
    factor = factors[...]
    power = jnp.exp(rate * -float(RUN))

    def spread(lag):
        return jnp.broadcast_to(lags[pl.ds(lag, 1), :], rate.shape)

    def run(q, a):
        parts = [sums[g, q, pl.ds(a, MODES, stride=RUNS), :] for g in range(blocks)]
        return jnp.concatenate(parts, axis=1)

    zeros = jnp.zeros(rate.shape, jnp.float32)
    inner, cross = spread(RUN - 1), zeros
    for lag in range(RUN - 2, -1, -1):
        cross = factor * cross + inner
        inner = factor * inner + spread(lag)
    state, tail, outer = zeros, zeros, zeros
    befores = []
    for a in range(RUNS):
        befores.append(state)
        outer = outer + state * run(2, a)
        cross = cross + state * run(3, a)
        tail = run(1, a) + power * (tail + float(RUN) * state)
        state = run(0, a) + power * state
    adjoint, head, both = zeros, zeros, zeros
    for a in range(RUNS - 1, -1, -1):
        for g in range(blocks):
            starts[g, pl.ds(a * MODES, MODES), :] = adjoint[:, g * LANES : (g + 1) * LANES]
        cross = cross + adjoint * run(1, a)
        both = both + adjoint * befores[a]
        head = run(3, a) + power * (head + float(RUN) * adjoint)
        adjoint = run(2, a) + power * adjoint
    inner = inner + factor * outer
    cross = cross + (float(RUN) * power) * both
    wide = [tail, adjoint, state, head, inner, cross, spread(0), zeros]
    for g in range(blocks):
        for q in range(SIDE):
            stage[g, pl.ds(q * MODES, MODES), :] = wide[q][:, g * LANES : (g + 1) * LANES]
    for g in range(blocks):
        tiles = swap_blocks([stage[g, pl.ds(m, SIDE, stride=MODES), :] for m in range(MODES)])
        for i in range(SIDE):
            tx[g * SIDE + i] = tiles[i]


def local_grads(g, cs, factors, residue, skip, starts, grads):
    lanes = pl.ds(pl.multiple_of(g * LANES, LANES), LANES)

    def row(ref, mode):
        return jnp.broadcast_to(ref[pl.ds(mode, 1), lanes], (RUNS, LANES))

    factor = [row(factors, mode) for mode in range(MODES)]
    weight = [row(residue, mode) for mode in range(MODES)]
    direct = row(skip, 0)
    adjoint = [starts[g, pl.ds(mode, RUNS, stride=MODES), :] for mode in range(MODES)]
    for i in range(RUN - 1, -1, -1):
        now = cs[g, pl.ds(i, RUNS, stride=RUN), :]
        total = direct * now
        for mode in range(MODES):
            adjoint[mode] = factor[mode] * adjoint[mode] + now
            total = total + weight[mode] * adjoint[mode]
        grads[g, pl.ds(i, RUNS, stride=RUN), :] = total


def own_lanes(value, place):
    value = jnp.where(lane_group() == place, value, 0.0)
    for step in (1, 2, 4):
        value = value + roll(value, step)
    return value


def own_row(value, place):
    return jnp.sum(jnp.where(own_rows() == lane_group(), own_lanes(value, place), 0.0), axis=0, keepdims=True)


def own_rows():
    return lax.broadcasted_iota(jnp.int32, (8, LANES), 0)


def owner_factors(place, block, length, rates, residue):
    lanes = pl.ds(pl.multiple_of(block * LANES, LANES), LANES)
    rate = own_row(rates[:, lanes], place)
    weight = own_row(residue[:, lanes], place)
    return jnp.exp(-rate), jnp.exp(rate * -float(length)), weight


def owner_sums(factor, power, weight, length, positions, rx, ztx, ptx):
    shards = rx.shape[0]
    zeros = jnp.zeros((SIDE, LANES), jnp.float32)
    step = jnp.broadcast_to(power, (SIDE, LANES))
    state, plain, by_start, by_head, by_tail, both = zeros, zeros, zeros, zeros, zeros, zeros
    befores, moved = [], []
    for k in range(shards):
        tile = rx[k]
        befores.append(state)
        moved.append(pltpu.roll(tile, 1, 0))
        plain = plain + tile
        by_start = by_start + state * moved[k]
        by_head = by_head + state * pltpu.roll(tile, SIDE - 1, 0)
        state = step * state + tile
    adjoint = zeros
    for k in range(shards - 1, -1, -1):
        ztx[k] = adjoint[1:2]
        by_tail = by_tail + adjoint * moved[k]
        both = both + befores[k] * pltpu.roll(adjoint, 1, 0)
        adjoint = step * adjoint + rx[k]
    scale = 1.0 / positions
    sum_residue = plain[4:5] + factor * by_start[2:3]
    sum_decay = plain[5:6] + by_head[2:3] + by_tail[1:2] + (float(length) * power) * both[2:3]
    ptx[0:1] = sum_residue * scale
    ptx[1:2] = (-scale) * factor * weight * sum_decay
    ptx[2:3] = plain[6:7] * scale
    ptx[3:8] = jnp.zeros((SIDE - 3, LANES), jnp.float32)


def unpack_rows(rows):
    apart = (lane_group() - lax.broadcasted_iota(jnp.int32, (8, LANES), 0) + SIDE) % SIDE
    out = rows
    for step in range(1, SIDE):
        moved = roll(pltpu.roll(rows, SIDE - step, 0), step)
        out = jnp.where(apart == step, moved, out)
    return out


def exchange_kernel(
    shards,
    groups,
    positions,
    tokens,
    cotangent,
    rates_in,
    residue_in,
    skip_in,
    grads_out,
    zrx,
    prx,
    x_raw,
    c_raw,
    rates,
    residue,
    skip,
    xs,
    cs,
    factors,
    sums,
    lags,
    starts,
    stage,
    tx,
    rx,
    ztx,
    ptx,
    grads,
    in_sems,
    out_sems,
    ctx_sems,
    back_sems,
    dp_sems,
    ready_sem,
):
    dp, ctx = lax.axis_index("dp"), lax.axis_index("ctx")
    length, channels = x_raw.shape
    blocks = channels // LANES
    loads = [
        pltpu.make_async_copy(source, target, in_sems.at[n])
        for n, (source, target) in enumerate(
            ((tokens, x_raw), (cotangent, c_raw), (rates_in, rates), (residue_in, residue), (skip_in, skip))
        )
    ]
    half = groups // 2
    late = dp // half
    place_x = lax.rem(dp, half)
    mirror = (shards // PLANE - 1 - ctx // PLANE) * PLANE + lax.rem(ctx, PLANE)
    owned = ctx + late * (mirror - ctx)

    def same_half(d):
        return late * half + lax.rem(place_x + d, half)

    def other_half(d):
        return (1 - late) * half + d

    sent = pl.ds(0, SENT)
    kept = pl.ds(0, KEPT)
    rx[...] = jnp.zeros(rx.shape, jnp.float32)
    barrier = pltpu.get_barrier_semaphore()

    def greet(group, peer):
        pl.semaphore_signal(barrier, inc=1, device_id=(group, peer), device_id_type=MESH)

    @pl.loop(1, shards, unroll=True)
    def _(d):
        greet(dp, lax.rem(ctx + d, shards))

    for load in loads:
        load.start()

    @pl.loop(1, half, unroll=True)
    def _(d):
        greet(same_half(d), owned)

    @pl.when(late == 0)
    def _():
        @pl.loop(0, half, unroll=True)
        def _(d):
            greet(other_half(d), mirror)
            greet(other_half(d), ctx)

    for load in loads[2:]:
        load.wait()
    factors[...] = jnp.exp(-rates[...])
    for load, raw, wide in ((loads[0], x_raw, xs), (loads[1], c_raw, cs)):
        load.wait()
        for g in range(blocks):
            wide[g] = raw[:, pl.ds(g * LANES, LANES)].astype(jnp.float32)

    def send_plane(plane):
        @pl.loop(0, PLANE, unroll=True)
        def _(d):
            inside = d
            part = plane * PLANE + inside
            across = (shards // PLANE - 1 - plane) * PLANE + inside
            peer = part + late * (across - part)

            @pl.when(peer != ctx)
            def _():
                pltpu.make_async_remote_copy(
                    src_ref=tx.at[part, sent],
                    dst_ref=rx.at[ctx, sent],
                    send_sem=ctx_sems.at[0],
                    recv_sem=ctx_sems.at[1],
                    device_id=(dp, peer),
                    device_id_type=MESH,
                ).start()

    @pl.loop(0, blocks)
    def _(g):
        run_sums(g, xs, cs, factors, sums, lags)

    join_runs(rates, factors, sums, lags, starts, stage, tx)
    pl.semaphore_wait(barrier, shards - 1 + half - 1 + late * 2 * half)
    for plane in range(shards // PLANE):
        send_plane(plane)

    rx[ctx] = tx[owned]

    @pl.when(late == 1)
    def _():
        @pl.loop(0, half, unroll=True)
        def _(d):
            pl.semaphore_signal(ready_sem, inc=1, device_id=(other_half(d), ctx), device_id_type=MESH)

    @pl.loop(0, blocks)
    def _(g):
        local_grads(g, cs, factors, residue, skip, starts, grads)

    store = pltpu.make_async_copy(grads, grads_out, out_sems.at[0])
    store.start()
    most = pl.ds(0, shards - 1)
    factor, power, weight = owner_factors(lax.rem(owned, SIDE), owned // SIDE, length, rates, residue)
    pltpu.make_async_copy(rx.at[most, sent], rx.at[most, sent], ctx_sems.at[1]).wait()
    owner_sums(factor, power, weight, length, positions, rx, ztx, ptx)

    def send_totals(group):
        pltpu.make_async_remote_copy(
            src_ref=ptx.at[kept],
            dst_ref=prx.at[dp, kept],
            send_sem=dp_sems.at[0],
            recv_sem=dp_sems.at[1],
            device_id=(group, owned),
            device_id_type=MESH,
        ).start()

    @pl.when(late == 1)
    def _():
        @pl.loop(0, half, unroll=True)
        def _(d):
            send_totals(other_half(d))

        send_totals(dp)

    @pl.loop(1, half, unroll=True)
    def _(d):
        send_totals(same_half(d))


    @pl.loop(1, shards, unroll=True)
    def _(d):
        peer = lax.rem(ctx + d, shards)
        pltpu.make_async_remote_copy(
            src_ref=ztx.at[peer],
            dst_ref=zrx.at[owned],
            send_sem=back_sems.at[0],
            recv_sem=back_sems.at[1],
            device_id=(dp, peer),
            device_id_type=MESH,
        ).start()

    @pl.when(late == 0)
    def _():
        keep = pltpu.make_async_copy(ptx.at[kept], prx.at[dp, kept], out_sems.at[1])
        keep.start()
        keep.wait()
        pl.semaphore_wait(ready_sem, half)

        @pl.loop(0, half, unroll=True)
        def _(d):
            send_totals(other_half(d))

    keep_row = pltpu.make_async_copy(ztx.at[ctx], zrx.at[owned], out_sems.at[2])
    keep_row.start()
    pltpu.make_async_copy(tx.at[most, sent], tx.at[most, sent], ctx_sems.at[0]).wait()
    store.wait()
    keep_row.wait()
    pltpu.make_async_copy(zrx.at[most], zrx.at[most], back_sems.at[1]).wait()
    pltpu.make_async_copy(ztx.at[most], ztx.at[most], back_sems.at[0]).wait()

    def wait_totals(sem):
        @pl.when(late == 1)
        def _():
            pltpu.make_async_copy(prx.at[:, kept], prx.at[:, kept], sem).wait()

        @pl.when(late == 0)
        def _():
            others = pl.ds(0, groups - 1)
            pltpu.make_async_copy(prx.at[others, kept], prx.at[others, kept], sem).wait()

    wait_totals(dp_sems.at[1])
    wait_totals(dp_sems.at[0])


def finish_kernel(grads, zrx, prx, rates, residue, out, out_residue, out_decay, out_skip):
    blocks, length, _ = grads.shape
    ahead = (SIDE - lax.broadcasted_iota(jnp.int32, (8, LANES), 0)).astype(jnp.float32)
    powers = jnp.exp(rates[...] * -8.0)
    for g in range(blocks):
        lanes = pl.ds(g * LANES, LANES)
        rate = [jnp.broadcast_to(rates[pl.ds(m, 1), lanes], (8, LANES)) for m in range(MODES)]
        power = [
            jnp.broadcast_to(powers[m : m + 1, g * LANES : (g + 1) * LANES], (8, LANES)) for m in range(MODES)
        ]
        start = residue[:, lanes] * unpack_rows(zrx[pl.ds(g * SIDE, SIDE)].reshape(SIDE, LANES))
        term = [
            jnp.exp(-rate[m] * ahead) * jnp.broadcast_to(start[m : m + 1], (8, LANES))
            for m in range(MODES)
        ]
        for b in range(length // 8 - 1, -1, -1):
            rows = pl.ds(b * 8, 8)
            total = grads[g, rows, :]
            for m in range(MODES):
                total = total + term[m]
                if b:
                    term[m] = power[m] * term[m]
            out[rows, lanes] = total
    totals = prx[0]
    for n in range(1, prx.shape[0]):
        totals = totals + prx[n]
    sublane = lax.broadcasted_iota(jnp.int32, (8, LANES), 0)
    for row, ref in ((0, out_residue), (1, out_decay)):
        spread = jnp.broadcast_to(totals[row : row + 1], (8, LANES))
        value = spread
        for m in range(1, MODES):
            value = jnp.where(sublane == m, roll(spread, -m), value)
        ref[...] = value[:, :GROUP]
    out_skip[...] = totals[2, :GROUP]


def body(shards, groups, tokens, cotangent, decay, residue, skip):
    _, length, channels = tokens.shape
    positions = float(length * shards * groups)
    blocks = channels // LANES
    vmem = pl.BlockSpec(memory_space=pltpu.VMEM)
    hbm = pl.BlockSpec(memory_space=pltpu.HBM)
    f32 = jnp.float32
    grads, carry, totals = pl.pallas_call(
        functools.partial(exchange_kernel, shards, groups, positions),
        out_shape=[
            jax.ShapeDtypeStruct((blocks, length, LANES), f32),
            jax.ShapeDtypeStruct((shards, 1, LANES), f32),
            jax.ShapeDtypeStruct((groups, 8, LANES), f32),
        ],
        in_specs=[hbm] * 5,
        out_specs=[hbm] * 3,
        scratch_shapes=[
            pltpu.VMEM((length, channels), jnp.bfloat16),
            pltpu.VMEM((length, channels), jnp.bfloat16),
            pltpu.VMEM((MODES, channels), f32),
            pltpu.VMEM((MODES, channels), f32),
            pltpu.VMEM((1, channels), f32),
            pltpu.VMEM((blocks, length, LANES), f32),
            pltpu.VMEM((blocks, length, LANES), f32),
            pltpu.VMEM((MODES, channels), f32),
            pltpu.VMEM((blocks, 4, MODES * RUNS, LANES), f32),
            pltpu.VMEM((RUN, channels), f32),
            pltpu.VMEM((blocks, RUNS * MODES, LANES), f32),
            pltpu.VMEM((blocks, SIDE * MODES, LANES), f32),
            pltpu.VMEM((shards, 8, LANES), f32),
            pltpu.VMEM((shards, 8, LANES), f32),
            pltpu.VMEM((shards, 1, LANES), f32),
            pltpu.VMEM((8, LANES), f32),
            pltpu.VMEM((blocks, length, LANES), f32),
            pltpu.SemaphoreType.DMA((5,)),
            pltpu.SemaphoreType.DMA((3,)),
            pltpu.SemaphoreType.DMA((2,)),
            pltpu.SemaphoreType.DMA((2,)),
            pltpu.SemaphoreType.DMA((2,)),
            pltpu.SemaphoreType.REGULAR,
        ],
        compiler_params=pltpu.CompilerParams(
            collective_id=1, has_side_effects=True, vmem_limit_bytes=60 * 1024 * 1024
        ),
        name="exchange",
    )(tokens[0], cotangent[0], decay, residue, skip.reshape(1, channels))
    out, grad_residue, grad_decay, grad_skip = pl.pallas_call(
        finish_kernel,
        out_shape=[
            jax.ShapeDtypeStruct((length, channels), f32),
            jax.ShapeDtypeStruct((MODES, GROUP), f32),
            jax.ShapeDtypeStruct((MODES, GROUP), f32),
            jax.ShapeDtypeStruct((GROUP,), f32),
        ],
        in_specs=[vmem] * 5,
        out_specs=[vmem] * 4,
        compiler_params=pltpu.CompilerParams(vmem_limit_bytes=60 * 1024 * 1024),
        name="finish",
    )(grads, carry, totals, decay, residue)
    return out[None], grad_residue, grad_decay, grad_skip


def solution(mesh):
    return jax.shard_map(
        functools.partial(body, mesh.shape["ctx"], mesh.shape["dp"]),
        mesh=mesh,
        in_specs=(P("dp", "ctx", None), P("dp", "ctx", None), P(), P(), P()),
        out_specs=(P("dp", "ctx", None), P(None, "ctx"), P(None, "ctx"), P("ctx")),
        check_vma=False,
    )
```
